128 devices in a mesh: ctx: 16 (over y, z_lo, core), fsdp: 8 (over x, z_hi).
Axes of the slice: x: 4, y: 4, z: 4 (z_hi: 2, z_lo: 2; z = z_hi * 2 + z_lo), core: 2. Of those that a mesh axis runs over, the one named last changes fastest.
Arguments:
- layer_input: bfloat16 [8, 2048, 1024], P('fsdp', 'ctx'), may hold values from -6 to 6
- segment_ids: int32 [8, 2048], P('fsdp', 'ctx'), may hold values from 0 to 2, as said below
- norm_gain: bfloat16 [1024], P('fsdp'), may hold values from 0.5 to 1.5
- w_query: bfloat16 [1024, 512], P('fsdp'), may hold values from -0.1875 to 0.1875
- w_key: bfloat16 [1024, 128], P('fsdp'), may hold values from -0.1875 to 0.1875
- w_value: bfloat16 [1024, 128], P('fsdp'), may hold values from -0.1875 to 0.1875
- w_attn_out: bfloat16 [512, 1024], P('fsdp'), may hold values from -0.75 to 0.75
- w_gate_z: bfloat16 [1024, 1536], P('fsdp'), may hold values from -0.1875 to 0.1875
- w_inner: bfloat16 [1024, 1792], P('fsdp'), may hold values from -0.1875 to 0.1875
- w_step: bfloat16 [1024, 24], P('fsdp'), may hold values from -0.1875 to 0.1875
- conv_weight: bfloat16 [4, 1792], P(None, 'fsdp'), may hold values from -3 to 3
- conv_bias: bfloat16 [1792], P('fsdp'), may hold values from -3 to 3
- step_bias: bfloat16 [24], P('fsdp'), may hold values from -6 to -2
- decay_log: bfloat16 [24], P('fsdp'), may hold values from -4 to 1
- skip_gain: bfloat16 [24], P('fsdp'), may hold values from 0.5 to 1.5
- mixer_gain: bfloat16 [1536], P('fsdp'), may hold values from 0.5 to 1.5
- w_mixer_out: bfloat16 [1536, 1024], P('fsdp'), may hold values from -0.3125 to 0.3125
- ffn_gain: bfloat16 [1024], P('fsdp'), may hold values from 0.5 to 1.5
- w_gate: bfloat16 [1024, 2048], P('fsdp'), may hold values from -0.1875 to 0.1875
- w_up: bfloat16 [1024, 2048], P('fsdp'), may hold values from -0.1875 to 0.1875
- w_down: bfloat16 [2048, 1024], P('fsdp'), may hold values from -0.125 to 0.125
- out_grad: bfloat16 [8, 2048, 1024], P('fsdp', 'ctx'), may hold values from -6 to 6
Outputs:
- layer_output: bfloat16 [8, 2048, 1024], P('fsdp', 'ctx')
- input_grad: float32 [8, 2048, 1024], P('fsdp', 'ctx')
- grad_norm_gain: float32 [1024], P('fsdp')
- grad_w_query: float32 [1024, 512], P('fsdp')
- grad_w_key: float32 [1024, 128], P('fsdp')
- grad_w_value: float32 [1024, 128], P('fsdp')
- grad_w_attn_out: float32 [512, 1024], P('fsdp')
- grad_w_gate_z: float32 [1024, 1536], P('fsdp')
- grad_w_inner: float32 [1024, 1792], P('fsdp')
- grad_w_step: float32 [1024, 24], P('fsdp')
- grad_conv_weight: float32 [4, 1792], P(None, 'fsdp')
- grad_conv_bias: float32 [1792], P('fsdp')
- grad_step_bias: float32 [24], P('fsdp')
- grad_decay_log: float32 [24], P('fsdp')
- grad_skip_gain: float32 [24], P('fsdp')
- grad_mixer_gain: float32 [1536], P('fsdp')
- grad_w_mixer_out: float32 [1536, 1024], P('fsdp')
- grad_ffn_gain: float32 [1024], P('fsdp')
- grad_w_gate: float32 [1024, 2048], P('fsdp')
- grad_w_up: float32 [1024, 2048], P('fsdp')
- grad_w_down: float32 [2048, 1024], P('fsdp')
The draws below stay inside these ranges and needn't reach their ends.
Inputs may be any that keep to these rules, and one draw needn't show every extreme that they name: `segment_ids`: each row holds three documents numbered 0, 1, 2 in order: document 0 ends within the first 128 positions and document 2 begins within the last 128.
All inputs are finite; a program needn't handle non-finite values.
Results may differ from the reference program's by a relative error of at most 0.025.
Values may be sent and summed in bfloat16 or wider, within the bound.
A program may use at most 192 MiB of HBM per device.

```python
import math
import jax
import jax.numpy as jnp
from jax import lax

D = 1024
HEADS = 8
KV_HEADS = 2
HEAD_DIM = 64
SSM_HEADS = 24
SSM_DIM = 64
STATE = 128
CONV = 4
FF = 2048
TOK_DEV = 128
SEQLEN = 2048
SEQS = 8


def draw_segment_ids(key, part):
    key = jax.random.fold_in(key, 11)
    first_key, second_key = jax.random.split(key)
    first_end = jax.random.randint(first_key, (SEQS, 1), 1, TOK_DEV)
    second_start = jax.random.randint(second_key, (SEQS, 1), SEQLEN - TOK_DEV + 1, SEQLEN)
    order_idx = jnp.arange(SEQLEN, dtype=jnp.int32)[None, :]
    return (order_idx >= first_end).astype(jnp.int32) + (order_idx >= second_start).astype(jnp.int32)


def levels(stream_key, dims, cuts, least, largest):
    level, own = 1.0, jax.random.fold_in(stream_key, 6)
    for axis_at, shards_of in cuts:
        heights = jnp.exp(jax.random.uniform(jax.random.fold_in(own, axis_at), (shards_of,), jnp.float32, least / len(cuts), largest / len(cuts)))
        level = level * jnp.repeat(heights, dims[axis_at] // shards_of).reshape([-1 if axis == axis_at else 1 for axis in range(len(dims))])
    return level


def normal_values(own_key, extent, scale, most, cuts=(), held_as=jnp.bfloat16):
    array = scale * jax.random.normal(own_key, extent, jnp.float32)
    if cuts:
        array = array * levels(own_key, extent, cuts, -0.22, 0.18)
    return jnp.clip(array, -most, most).astype(held_as)


def setup_inputs(seed: int = 0) -> dict:
    key_list = jax.random.split(jax.random.key(seed), 23)
    layer_input = normal_values(key_list[0], (SEQS, SEQLEN, D), 1.0, 6.0, ((0, 8), (1, 16)))
    segment_ids = draw_segment_ids(jax.random.fold_in(key_list[22], 71), 0)
    norm_gain = jnp.clip(1.0 + 0.1 * jax.random.normal(key_list[2], (D,), jnp.float32), 0.5, 1.5).astype(jnp.bfloat16)
    w_query = normal_values(key_list[3], (D, HEADS * HEAD_DIM), D ** -0.5, 0.1875, ((0, 8),))
    w_key = normal_values(key_list[4], (D, KV_HEADS * HEAD_DIM), D ** -0.5, 0.1875, ((0, 8),))
    w_value = normal_values(key_list[5], (D, KV_HEADS * HEAD_DIM), D ** -0.5, 0.1875, ((0, 8),))
    w_attn_out = normal_values(key_list[6], (HEADS * HEAD_DIM, D), (HEADS * HEAD_DIM // 8) ** -0.5, 0.75, ((0, 8),))
    w_gate_z = normal_values(key_list[7], (D, SSM_HEADS * SSM_DIM), D ** -0.5, 0.1875, ((0, 8),))
    w_inner = normal_values(key_list[8], (D, SSM_HEADS * SSM_DIM + 2 * STATE), D ** -0.5, 0.1875, ((0, 8),))
    w_step = normal_values(key_list[9], (D, SSM_HEADS), D ** -0.5, 0.1875, ((0, 8),))
    conv_weight = normal_values(key_list[10], (CONV, SSM_HEADS * SSM_DIM + 2 * STATE), CONV ** -0.5, 3.0, ((1, 8),))
    conv_bias = normal_values(key_list[11], (SSM_HEADS * SSM_DIM + 2 * STATE,), 0.5, 3.0, ((0, 8),))
    step_bias = jnp.clip(-6.0 + 4.0 * jax.random.uniform(key_list[12], (SSM_HEADS,), jnp.float32) ** levels(key_list[12], (SSM_HEADS,), ((0, 8),), -0.2, 0.2), -6.0, -2.0).astype(jnp.bfloat16)
    decay_log = jnp.clip(-4.0 + 5.0 * jax.random.uniform(key_list[13], (SSM_HEADS,), jnp.float32) ** levels(key_list[13], (SSM_HEADS,), ((0, 8),), -0.2, 0.2), -4.0, 1.0).astype(jnp.bfloat16)
    skip_gain = jnp.clip(0.5 + 1.0 * jax.random.uniform(key_list[14], (SSM_HEADS,), jnp.float32) ** levels(key_list[14], (SSM_HEADS,), ((0, 8),), -0.2, 0.2), 0.5, 1.5).astype(jnp.bfloat16)
    mixer_gain = jnp.clip(1.0 + 0.1 * jax.random.normal(key_list[15], (SSM_HEADS * SSM_DIM,), jnp.float32), 0.5, 1.5).astype(jnp.bfloat16)
    w_mixer_out = normal_values(key_list[16], (SSM_HEADS * SSM_DIM, D), (SSM_HEADS * SSM_DIM // 4) ** -0.5, 0.3125, ((0, 8),))
    ffn_gain = jnp.clip(1.0 + 0.1 * jax.random.normal(key_list[17], (D,), jnp.float32), 0.5, 1.5).astype(jnp.bfloat16)
    w_gate = normal_values(key_list[18], (D, FF), D ** -0.5, 0.1875, ((0, 8),))
    w_up = normal_values(key_list[19], (D, FF), D ** -0.5, 0.1875, ((0, 8),))
    w_down = normal_values(key_list[20], (FF, D), FF ** -0.5, 0.125, ((0, 8),))
    out_grad = normal_values(key_list[21], (SEQS, SEQLEN, D), 1.0, 6.0, ((0, 8), (1, 16)))
    return {"layer_input": layer_input, "segment_ids": segment_ids, "norm_gain": norm_gain, "w_query": w_query, "w_key": w_key, "w_value": w_value, "w_attn_out": w_attn_out, "w_gate_z": w_gate_z, "w_inner": w_inner, "w_step": w_step, "conv_weight": conv_weight, "conv_bias": conv_bias, "step_bias": step_bias, "decay_log": decay_log, "skip_gain": skip_gain, "mixer_gain": mixer_gain, "w_mixer_out": w_mixer_out, "ffn_gain": ffn_gain, "w_gate": w_gate, "w_up": w_up, "w_down": w_down, "out_grad": out_grad}


@jax.custom_vjp
def low(v):
    return lax.optimization_barrier(v.astype(jnp.bfloat16)).astype(jnp.float32)

@jax.custom_vjp
def low_back(v):
    return v

def low_keep(v):
    return (low(v), None)

def low_pass(kept, grad):
    return (grad,)

def back_keep(v):
    return (v, None)

def back_low(kept, grad):
    return (low(grad),)
low.defvjp(low_keep, low_pass)
low_back.defvjp(back_keep, back_low)
epsilon = 1e-05
rope_base = 10000.0
key_scale = 0.5
attn_out_scale = 0.8
mixer_out_scale = 0.5
gate_scale = 0.75
down_scale = 0.8
masked_score = -1e+30
highest = lax.Precision.HIGHEST

def project(left_side, right_side):
    return jnp.dot(left_side, right_side, precision=highest, preferred_element_type=jnp.float32)

def rms_scale(values, gain_vec):
    return values * lax.rsqrt(lax.optimization_barrier(jnp.mean(values * values, axis=-1, keepdims=True)) + epsilon) * gain_vec

def rope_tables(positions):
    half_dim = HEAD_DIM // 2
    inverse = rope_base ** (-jnp.arange(half_dim, dtype=jnp.float32) / half_dim)
    angles = positions.astype(jnp.float32)[:, None] * inverse[None, :]
    return (jnp.cos(angles)[:, None, :], jnp.sin(angles)[:, None, :])

def rotate(values, angle_cos, angle_sin):
    half_dim = values.shape[-1] // 2
    first_half = values[..., :half_dim]
    second_half = values[..., half_dim:]
    return jnp.concatenate([first_half * angle_cos - second_half * angle_sin, second_half * angle_cos + first_half * angle_sin], axis=-1)

def conv_mix(extended, seg_ext, seg_here, conv_weight, conv_bias):
    row_count = seg_here.shape[0]
    summed = jnp.broadcast_to(conv_bias[None, :], (row_count, conv_bias.shape[0]))
    for offset in range(conv_weight.shape[0]):
        same_doc = (seg_ext[offset:offset + row_count] == seg_here)[:, None]
        summed = summed + conv_weight[offset][None, :] * jnp.where(same_doc, extended[offset:offset + row_count], 0.0)
    return jax.nn.silu(summed)

def mixer_features(extended, seg_ext, seg_here, step_raw, conv_weight, conv_bias, step_bias, decay_log):
    mixed_rows = conv_mix(extended, seg_ext, seg_here, conv_weight, conv_bias)
    row_count = seg_here.shape[0]
    width_inner = SSM_HEADS * SSM_DIM
    values_ssm = mixed_rows[:, :width_inner].reshape(row_count, SSM_HEADS, SSM_DIM)
    input_map = mixed_rows[:, width_inner:width_inner + STATE]
    output_map = mixed_rows[:, width_inner + STATE:]
    step_size = jax.nn.softplus(step_raw + step_bias[None, :])
    log_decay = -step_size * jnp.exp(decay_log)[None, :]
    return (values_ssm, input_map, output_map, step_size, log_decay)

def ssd_states(values_ssm, input_map, step_size, log_decay, seg_here, seg_before):
    cumulative = jnp.cumsum(log_decay, axis=0)
    last_seg = seg_here[-1]
    tail_weight = jnp.where((seg_here == last_seg)[:, None], jnp.exp(cumulative[-1][None, :] - cumulative), 0.0) * step_size
    weighted = tail_weight[:, :, None] * values_ssm
    block_state = jnp.einsum('shp,sn->hpn', weighted, input_map, precision=highest)
    block_decay = jnp.exp(cumulative[-1]) * (last_seg == seg_before).astype(jnp.float32)
    return (block_decay, block_state)

def ssd_output(values_ssm, input_map, output_map, step_size, log_decay, seg_here, seg_before, skip_gain, carried):
    row_count = seg_here.shape[0]
    cumulative = jnp.cumsum(log_decay, axis=0)
    order_idx = jnp.arange(row_count, dtype=jnp.int32)
    causal_same = (seg_here[:, None] == seg_here[None, :]) & (order_idx[:, None] >= order_idx[None, :])
    keep_mask = causal_same[:, :, None]
    spread = cumulative[:, None, :] - cumulative[None, :, :]
    decay_mat = jnp.where(keep_mask, jnp.exp(jnp.where(keep_mask, spread, 0.0)), 0.0)
    pairing = jnp.dot(output_map, input_map.T, precision=highest)
    mixing = decay_mat * pairing[:, :, None] * step_size[None, :, :]
    result = jnp.einsum('tsh,shp->thp', mixing, values_ssm, precision=highest)
    entering = jnp.exp(cumulative) * (seg_here == seg_before).astype(jnp.float32)[:, None]
    result = result + entering[:, :, None] * jnp.einsum('tn,hpn->thp', output_map, carried, precision=highest)
    return (result + skip_gain[None, :, None] * values_ssm, entering)

def gate_norm(result, gate_z, mixer_gain):
    flat_rows = result.reshape(gate_z.shape) * jax.nn.silu(gate_z)
    return rms_scale(flat_rows, mixer_gain)

def attend_block(block_parts, key_all, value_all, pos_all, seg_all):
    query_blk, pos_blk, seg_blk = block_parts
    row_count = query_blk.shape[0]
    grouped = query_blk.reshape(row_count, KV_HEADS, HEADS // KV_HEADS, HEAD_DIM)
    scores = low_back(jnp.einsum('tkgd,jkd->kgtj', grouped, key_all, precision=highest))
    visible = (pos_all[None, :] <= pos_blk[:, None]) & (seg_all[None, :] == seg_blk[:, None])
    prob_low = low(jax.nn.softmax(jnp.where(visible[None, None], scores, masked_score), axis=-1))
    attended = jnp.einsum('kgtj,jkd->tkgd', prob_low, value_all, precision=highest)
    return attended.reshape(row_count, HEADS * HEAD_DIM)

def block_step(carried, pieces):
    values_ssm, input_map, output_map, step_size, log_decay, seg_here, seg_before, skip_gain = pieces
    result, entering = ssd_output(values_ssm, input_map, output_map, step_size, log_decay, seg_here, seg_before, skip_gain, carried)
    block_decay, block_state = ssd_states(values_ssm, input_map, step_size, log_decay, seg_here, seg_before)
    return (block_decay[:, None, None] * carried + block_state, result)

def layer_row(row_in, seg_row, weights):
    norm_gain, w_query, w_key, w_value, w_attn_out, w_gate_z, w_inner, w_step, conv_weight, conv_bias, step_bias, decay_log, skip_gain, mixer_gain, w_mixer_out, ffn_gain, w_gate, w_up, w_down = weights
    seq_len = row_in.shape[0]
    positions = jnp.arange(seq_len, dtype=jnp.int32)
    normed_low = low(rms_scale(row_in, norm_gain))
    angle_cos, angle_sin = rope_tables(positions)
    query_rot = low(rotate(low_back(project(normed_low, w_query)).reshape(seq_len, HEADS, HEAD_DIM), angle_cos, angle_sin) * HEAD_DIM ** (-0.5))
    key_rot = low(rotate(low_back(project(normed_low, w_key)).reshape(seq_len, KV_HEADS, HEAD_DIM), angle_cos, angle_sin) * key_scale)
    value_low = low(low_back(project(normed_low, w_value))).reshape(seq_len, KV_HEADS, HEAD_DIM)
    block_rows = math.gcd(seq_len, 512)
    blocks = seq_len // block_rows
    attend_saved = jax.checkpoint(attend_block)
    attended = lax.map(lambda block_parts: attend_saved(block_parts, key_rot, value_low, positions, seg_row), (query_rot.reshape(blocks, block_rows, HEADS, HEAD_DIM), positions.reshape(blocks, block_rows), seg_row.reshape(blocks, block_rows)))
    attn_low = low(low_back(attended.reshape(seq_len, HEADS * HEAD_DIM)))
    attn_branch = low_back(project(attn_low, w_attn_out)) * attn_out_scale
    gate_z = low_back(project(normed_low, w_gate_z))
    inner_pre = low_back(project(normed_low, w_inner))
    step_raw = low_back(project(normed_low, w_step))
    rim_rows = CONV - 1
    extended = jnp.concatenate([jnp.zeros((rim_rows, inner_pre.shape[1]), jnp.float32), inner_pre], axis=0)
    seg_ext = jnp.concatenate([jnp.full((rim_rows,), -1, jnp.int32), seg_row])
    values_ssm, input_map, output_map, step_size, log_decay = mixer_features(extended, seg_ext, seg_row, step_raw, conv_weight, conv_bias, step_bias, decay_log)
    block_len = TOK_DEV
    block_count = seq_len // block_len
    seg_prev = jnp.concatenate([jnp.full((1,), -1, jnp.int32), seg_row[block_len - 1:seq_len - 1:block_len]])
    skip_rows = jnp.broadcast_to(skip_gain[None, :], (block_count, SSM_HEADS))
    start_state = jnp.zeros((SSM_HEADS, SSM_DIM, STATE), jnp.float32)
    _, mixer_result = lax.scan(jax.checkpoint(block_step), start_state, (values_ssm.reshape(block_count, block_len, SSM_HEADS, SSM_DIM), input_map.reshape(block_count, block_len, STATE), output_map.reshape(block_count, block_len, STATE), step_size.reshape(block_count, block_len, SSM_HEADS), log_decay.reshape(block_count, block_len, SSM_HEADS), seg_row.reshape(block_count, block_len), seg_prev, skip_rows))
    mixer_result = mixer_result.reshape(seq_len, SSM_HEADS, SSM_DIM)
    mixer_low = low(gate_norm(mixer_result, gate_z, mixer_gain))
    mixer_branch = low_back(project(mixer_low, w_mixer_out)) * mixer_out_scale
    middle = row_in + attn_branch + mixer_branch
    normed_two_low = low(rms_scale(middle, ffn_gain))
    gate_pre = low_back(project(normed_two_low, w_gate)) * gate_scale
    up_pre = low_back(project(normed_two_low, w_up))
    hidden_low = low(jax.nn.silu(gate_pre) * up_pre)
    return middle + low_back(project(hidden_low, w_down)) * down_scale

def reference(layer_input, segment_ids, norm_gain, w_query, w_key, w_value, w_attn_out, w_gate_z, w_inner, w_step, conv_weight, conv_bias, step_bias, decay_log, skip_gain, mixer_gain, w_mixer_out, ffn_gain, w_gate, w_up, w_down, out_grad):
    weights = (norm_gain.astype(jnp.float32), w_query.astype(jnp.float32), w_key.astype(jnp.float32), w_value.astype(jnp.float32), w_attn_out.astype(jnp.float32), w_gate_z.astype(jnp.float32), w_inner.astype(jnp.float32), w_step.astype(jnp.float32), conv_weight.astype(jnp.float32), conv_bias.astype(jnp.float32), step_bias.astype(jnp.float32), decay_log.astype(jnp.float32), skip_gain.astype(jnp.float32), mixer_gain.astype(jnp.float32), w_mixer_out.astype(jnp.float32), ffn_gain.astype(jnp.float32), w_gate.astype(jnp.float32), w_up.astype(jnp.float32), w_down.astype(jnp.float32))

    def one_row(totals, row_parts):
        row_in, seg_row, grad_row = row_parts
        row_out, pull_back = jax.vjp(lambda hidden, params: layer_row(hidden, seg_row, params), row_in.astype(jnp.float32), weights)
        grad_hidden, grad_params = pull_back(grad_row.astype(jnp.float32))
        totals = jax.tree.map(lambda acc_total, new_part: acc_total + new_part, totals, grad_params)
        return (totals, (row_out.astype(jnp.bfloat16), grad_hidden))
    zero_grads = jax.tree.map(jnp.zeros_like, weights)
    totals, (outputs, input_grads) = lax.scan(one_row, zero_grads, (layer_input, segment_ids, out_grad))
    return (outputs, input_grads, totals[0], totals[1], totals[2], totals[3], totals[4], totals[5], totals[6], totals[7], totals[8], totals[9], totals[10], totals[11], totals[12], totals[13], totals[14], totals[15], totals[16], totals[17], totals[18])
```

```python
import jax
import jax.numpy as jnp
from jax import lax
from jax.experimental import pallas as pl
from jax.experimental.pallas import tpu as pltpu
from jax.sharding import PartitionSpec as P

HEADS = 8
KV_HEADS = 2
HEAD_DIM = 64
SSM_HEADS = 24
SSM_DIM = 64
STATE = 128
CONV = 4


epsilon = 1e-05
rope_base = 10000.0
key_scale = 0.5
attn_out_scale = 0.8
mixer_out_scale = 0.5
gate_scale = 0.75
down_scale = 0.8
masked_score = -1e30
highest = lax.Precision.HIGHEST


def matmul_f32(left_side, right_side):
    return jnp.dot(left_side, right_side, preferred_element_type=jnp.float32)


def right_trans(left_side, right_side):
    return lax.dot_general(
        left_side, right_side, (((1,), (1,)), ((), ())), preferred_element_type=jnp.float32
    )


def rms_scale(values, gain_vec):
    return (
        values * lax.rsqrt(jnp.mean(values * values, axis=-1, keepdims=True) + epsilon) * gain_vec
    )


def rope_tables(positions):
    half_dim = HEAD_DIM // 2
    inverse = rope_base ** (-jnp.arange(half_dim, dtype=jnp.float32) / half_dim)
    angles = positions.astype(jnp.float32)[:, None] * inverse[None, :]
    return (jnp.cos(angles)[:, None, :], jnp.sin(angles)[:, None, :])


def rotate(values, angle_cos, angle_sin):
    half_dim = values.shape[-1] // 2
    first_half = values[..., :half_dim]
    second_half = values[..., half_dim:]
    return jnp.concatenate(
        [
            first_half * angle_cos - second_half * angle_sin,
            second_half * angle_cos + first_half * angle_sin,
        ],
        axis=-1,
    )


def rotate_back(values, angle_cos, angle_sin):
    half_dim = values.shape[-1] // 2
    first_half = values[..., :half_dim]
    second_half = values[..., half_dim:]
    return jnp.concatenate(
        [
            first_half * angle_cos + second_half * angle_sin,
            second_half * angle_cos - first_half * angle_sin,
        ],
        axis=-1,
    )


def conv_mix(extended, seg_ext, seg_here, conv_weight, conv_bias):
    row_count = seg_here.shape[0]
    summed = jnp.broadcast_to(conv_bias[None, :], (row_count, conv_bias.shape[0]))
    for offset in range(conv_weight.shape[0]):
        same_doc = (seg_ext[offset : offset + row_count] == seg_here)[:, None]
        summed = summed + conv_weight[offset][None, :] * jnp.where(
            same_doc, extended[offset : offset + row_count], 0.0
        )
    return jax.nn.silu(summed)


def mixer_features(
    extended, seg_ext, seg_here, step_raw, conv_weight, conv_bias, step_bias, decay_log
):
    mixed_rows = conv_mix(extended, seg_ext, seg_here, conv_weight, conv_bias)
    row_count = seg_here.shape[0]
    width_inner = SSM_HEADS * SSM_DIM
    values_ssm = mixed_rows[:, :width_inner].reshape(row_count, SSM_HEADS, SSM_DIM)
    input_map = mixed_rows[:, width_inner : width_inner + STATE]
    output_map = mixed_rows[:, width_inner + STATE :]
    step_size = jax.nn.softplus(step_raw + step_bias[None, :])
    log_decay = -step_size * jnp.exp(decay_log)[None, :]
    return (values_ssm, input_map, output_map, step_size, log_decay)


def ssd_states(values_ssm, input_map, step_size, log_decay, seg_here, seg_before):
    cumulative = jnp.cumsum(log_decay, axis=0)
    last_seg = seg_here[-1]
    tail_weight = (
        jnp.where(
            (seg_here == last_seg)[:, None], jnp.exp(cumulative[-1][None, :] - cumulative), 0.0
        )
        * step_size
    )
    weighted = tail_weight[:, :, None] * values_ssm
    block_state = jnp.einsum("shp,sn->phn", weighted, input_map, precision=highest)
    block_decay = jnp.exp(cumulative[-1]) * (last_seg == seg_before).astype(jnp.float32)
    return (block_decay, block_state)


def ssd_output(
    values_ssm,
    input_map,
    output_map,
    step_size,
    log_decay,
    seg_here,
    seg_before,
    skip_gain,
    carried,
):
    row_count = seg_here.shape[0]
    cumulative = jnp.cumsum(log_decay, axis=0)
    order_idx = jnp.arange(row_count, dtype=jnp.int32)
    causal_same = (seg_here[:, None] == seg_here[None, :]) & (
        order_idx[:, None] >= order_idx[None, :]
    )
    keep_mask = causal_same[:, :, None]
    spread = cumulative[:, None, :] - cumulative[None, :, :]
    decay_mat = jnp.where(keep_mask, jnp.exp(jnp.where(keep_mask, spread, 0.0)), 0.0)
    pairing = jnp.dot(output_map, input_map.T, precision=highest)
    mixing = decay_mat * pairing[:, :, None] * step_size[None, :, :]
    result = jnp.einsum("tsh,shp->thp", mixing, values_ssm, precision=highest)
    entering = jnp.exp(cumulative) * (seg_here == seg_before).astype(jnp.float32)[:, None]
    result = result + entering[:, :, None] * jnp.einsum(
        "tn,phn->thp", output_map, carried, precision=highest
    )
    return (result + skip_gain[None, :, None] * values_ssm, entering)


def gate_norm(result, gate_z, mixer_gain):
    flat_rows = result.reshape(gate_z.shape) * jax.nn.silu(gate_z)
    return rms_scale(flat_rows, mixer_gain)


def head_forward(query_head, key_head, value_head, visible):
    scores = jnp.einsum("tgd,jd->gtj", query_head, key_head, preferred_element_type=jnp.float32)
    scores = jnp.where(visible[None], scores, masked_score)
    row_max = jnp.max(scores, axis=-1, keepdims=True)
    exp_scores = jnp.exp(scores - row_max)
    row_sum = jnp.sum(exp_scores, axis=-1, keepdims=True)
    prob_low = (exp_scores / row_sum).astype(jnp.bfloat16)
    attended = jnp.einsum("gtj,jd->tgd", prob_low, value_head, preferred_element_type=jnp.float32)
    return (attended, (row_max + jnp.log(row_sum))[..., 0])


def head_backward(query_head, key_head, value_head, grad_head, log_total, visible):
    scores = jnp.einsum("tgd,jd->gtj", query_head, key_head, preferred_element_type=jnp.float32)
    scores = jnp.where(visible[None], scores, masked_score)
    prob_full = jnp.where(visible[None], jnp.exp(scores - log_total[..., None]), 0.0)
    prob_low = prob_full.astype(jnp.bfloat16)
    grad_probs = jnp.einsum(
        "tgd,jd->gtj", grad_head, value_head, preferred_element_type=jnp.float32
    )
    inner_sum = jnp.sum(prob_full * grad_probs, axis=-1, keepdims=True)
    grad_scores = (prob_full * (grad_probs - inner_sum)).astype(jnp.bfloat16)
    grad_query = jnp.einsum(
        "gtj,jd->tgd", grad_scores, key_head, preferred_element_type=jnp.float32
    )
    grad_key = jnp.einsum(
        "gtj,tgd->jd", grad_scores, query_head, preferred_element_type=jnp.float32
    )
    grad_value = jnp.einsum("gtj,tgd->jd", prob_low, grad_head, preferred_element_type=jnp.float32)
    return (grad_query, grad_key, grad_value)


MESH = pl.DeviceIdType.MESH
CTX = 16
FSDP = 8
COLS = 4224
PAD_AT = 4096
CUT_COLS = 1792
CUT_ROWS = 192
OUT_ROWS = 512
HALF = 512
QUARTER = 32
QUARTER_A = CUT_ROWS // 4
QUARTER_B = (OUT_ROWS - CUT_ROWS) // 4
SMALL = 1577
CHUNK = SSM_DIM * SSM_HEADS // CTX
VMEM_LIMIT = 60 * 2**20


def place():
    f, c = lax.axis_index("fsdp"), lax.axis_index("ctx")
    return f, c, c // 4, (c // 2) % 2, c % 2


def at_ctx(y, low_z, core):
    return (y * 2 + low_z) * 2 + core


def meet(partners):
    barrier = pltpu.get_barrier_semaphore()
    for partner in partners:
        pl.semaphore_signal(barrier, inc=1, device_id=partner, device_id_type=MESH)
    pl.semaphore_wait(barrier, len(partners))


class Sender:
    def __init__(self, send_sem, recv_sem):
        self.send_sem, self.recv_sem, self.used, self.all = send_sem, recv_sem, 0, []

    def push(self, src, dst, partner):
        index = self.used
        self.used += 1
        copy = pltpu.make_async_remote_copy(
            src_ref=src,
            dst_ref=dst,
            send_sem=self.send_sem.at[index],
            recv_sem=self.recv_sem.at[index],
            device_id=partner,
            device_id_type=MESH,
        )
        copy.start()
        self.all.append(copy)
        return copy

    def drain(self):
        for copy in self.all:
            copy.wait_send()


def call_kernel(body, name, cid, outs, ins, sems, scratch=(), space=pltpu.VMEM, cost=0):
    return pl.pallas_call(
        body,
        name=name,
        out_shape=outs,
        in_specs=[pl.BlockSpec(memory_space=space)] * len(ins),
        out_specs=jax.tree.map(lambda _: pl.BlockSpec(memory_space=space), outs),
        scratch_shapes=[
            *scratch,
            pltpu.SemaphoreType.DMA((sems,)),
            pltpu.SemaphoreType.DMA((sems,)),
        ],
        compiler_params=pltpu.CompilerParams(
            collective_id=cid, has_side_effects=True, vmem_limit_bytes=VMEM_LIMIT
        ),
    )(*ins)


def shape_of(dims, kind):
    return jax.ShapeDtypeStruct(dims, kind)


def gather_body(in12, in3, out12, out3, own_sem, send_sem, recv_sem):
    f, c, y, low_z, core = place()
    peers = [{"fsdp": (f + d) % FSDP} for d in range(1, FSDP)]
    sources = [(f + FSDP - d) % FSDP for d in range(1, FSDP)]
    columns = [{"ctx": at_ctx((y + e) % 4, low_z, core)} for e in range(1, 4)]
    sibling = {"ctx": at_ctx(y, low_z, 1 - core)}
    meet(peers + columns + [sibling])
    net = Sender(send_sem, recv_sem)
    own = [
        pltpu.make_async_copy(in12.at[0], out12.at[0, f], own_sem.at[0]),
        pltpu.make_async_copy(in12.at[1], out12.at[1, f], own_sem.at[1]),
        pltpu.make_async_copy(in3, out3.at[f], own_sem.at[2]),
    ]
    half = pl.ds(pl.multiple_of(core * HALF, HALF), HALF)
    strip = pl.ds(pl.multiple_of(y * QUARTER, QUARTER), QUARTER)
    strip3 = pl.ds(pl.multiple_of(CUT_ROWS + y * QUARTER_B, 16), QUARTER_B)
    right = pl.ds(CUT_COLS, COLS - CUT_COLS)
    left = pl.ds(0, CUT_COLS)
    top = pl.ds(0, CUT_ROWS)
    below = pl.ds(CUT_ROWS, OUT_ROWS - CUT_ROWS)
    part_b = [
        (
            net.push(in12.at[core, strip, right], out12.at[core, f, strip, right], peer),
            net.push(in3.at[strip3, half], out3.at[f, strip3, half], peer),
        )
        for peer in peers
    ]
    part_a = [
        (
            net.push(in12.at[core, :, left], out12.at[core, f, :, left], peer),
            net.push(in3.at[top, half], out3.at[f, top, half], peer),
        )
        for peer in peers
    ]
    for copy in own:
        copy.start()
    passed = []
    for index, source in enumerate(sources):
        for copy in part_b[index]:
            copy.wait_recv()
        one, two = out12.at[core, source, strip, right], out3.at[source, strip3, half]
        passed.append([(net.push(one, one, to), net.push(two, two, to)) for to in columns])
    crossing = []
    for index, source in enumerate(sources):
        for copy in part_a[index]:
            copy.wait_recv()
        one, two = out12.at[core, source, :, left], out3.at[source, top, half]
        crossing += [net.push(one, one, sibling), net.push(two, two, sibling)]
    for index, source in enumerate(sources):
        for pair in passed[index]:
            for copy in pair:
                copy.wait_recv()
        one, two = out12.at[core, source, :, right], out3.at[source, below, half]
        crossing += [net.push(one, one, sibling), net.push(two, two, sibling)]
    for copy in crossing:
        copy.wait_recv()
    net.drain()
    for copy in own:
        copy.wait()


def gather_weights(in12, in3):
    return call_kernel(
        gather_body,
        "gather_weights",
        0,
        (
            shape_of((2, FSDP, 128, COLS), jnp.bfloat16),
            shape_of((FSDP, OUT_ROWS, 2 * HALF), jnp.bfloat16),
        ),
        (in12, in3),
        98,
        (pltpu.SemaphoreType.DMA((3,)),),
        pl.ANY,
    )


def ctx_peers(c):
    return [{"ctx": (c + e) % CTX} for e in range(1, CTX)]


def keys_body(kv, rim, seg, kv_all, rim_out, seg_all, send_sem, recv_sem):
    f, c, y, low_z, core = place()
    peers = ctx_peers(c)
    meet(peers)
    net = Sender(send_sem, recv_sem)
    copies = [net.push(rim, rim_out, peers[0])]
    for peer in peers:
        copies.append(net.push(kv, kv_all.at[c], peer))
        copies.append(net.push(seg, seg_all.at[c], peer))
    kv_all[c] = kv[...]
    seg_all[c] = seg[...]
    for copy in copies:
        copy.wait_recv()
    net.drain()


def gather_keys(kv, rim, seg):
    return call_kernel(
        keys_body,
        "gather_keys",
        1,
        (
            shape_of((CTX, *kv.shape), kv.dtype),
            shape_of(rim.shape, rim.dtype),
            shape_of((CTX, *seg.shape), seg.dtype),
        ),
        (kv, rim, seg),
        31,
    )


def scan_rows(order, decay_of, parts, carries):
    state = jnp.zeros((CHUNK, STATE), jnp.float32)
    for at in order:
        carries[at] = state.astype(jnp.bfloat16)
        decay = decay_of[at]
        whole = jnp.concatenate([decay] * (CHUNK // SSM_HEADS), axis=0)
        state = whole * state + parts[at].astype(jnp.float32)


def send_back(net, c, peers, carries, carried):
    copies = [
        net.push(carries.at[(c + e + 1) % CTX], carried.at[c], peer) for e, peer in enumerate(peers)
    ]
    carried[c] = carries[c]
    for copy in copies:
        copy.wait_recv()
    net.drain()


def forward_body(states, decay, carried, decays, parts, carries, send_sem, recv_sem):
    f, c, y, low_z, core = place()
    peers = ctx_peers(c)
    meet(peers)
    net = Sender(send_sem, recv_sem)
    copies = []
    for e, peer in enumerate(peers):
        copies.append(net.push(states.at[(c + e + 1) % CTX], parts.at[c], peer))
        copies.append(net.push(decay, decays.at[c], peer))
    parts[c] = states[c]
    decays[c] = decay[...]
    for copy in copies:
        copy.wait_recv()
    scan_rows(range(CTX), decays, parts, carries)
    send_back(net, c, peers, carries, carried)


def backward_body(states, decays, carried, parts, carries, send_sem, recv_sem):
    f, c, y, low_z, core = place()
    peers = ctx_peers(c)
    meet(peers)
    net = Sender(send_sem, recv_sem)
    copies = [
        net.push(states.at[(c + e + 1) % CTX], parts.at[c], peer) for e, peer in enumerate(peers)
    ]
    parts[c] = states[c]
    for copy in copies:
        copy.wait_recv()
    scan_rows(range(CTX - 1, -1, -1), decays, parts, carries)
    send_back(net, c, peers, carries, carried)


def scan_forward(states, decay):
    chunks = states.astype(jnp.bfloat16).reshape(CTX, CHUNK, STATE)
    wide = jnp.broadcast_to(decay[:, None], (SSM_HEADS, STATE))
    carried, decays = call_kernel(
        forward_body,
        "scan_forward",
        2,
        (
            shape_of((CTX, CHUNK, STATE), jnp.bfloat16),
            shape_of((CTX, SSM_HEADS, STATE), jnp.float32),
        ),
        (chunks, wide),
        45,
        (pltpu.VMEM((CTX, CHUNK, STATE), jnp.bfloat16),) * 2,
    )
    return carried.reshape(SSM_DIM, SSM_HEADS, STATE).astype(jnp.float32), decays


def scan_backward(states, decays):
    chunks = states.astype(jnp.bfloat16).reshape(CTX, CHUNK, STATE)
    carried = call_kernel(
        backward_body,
        "scan_backward",
        3,
        shape_of((CTX, CHUNK, STATE), jnp.bfloat16),
        (chunks, decays),
        30,
        (pltpu.VMEM((CTX, CHUNK, STATE), jnp.bfloat16),) * 2,
    )
    return carried.reshape(SSM_DIM, SSM_HEADS, STATE).astype(jnp.float32)


def key_grads_body(terms, rim, total, rim_out, parts, send_sem, recv_sem):
    f, c, y, low_z, core = place()
    peers = ctx_peers(c)
    meet(peers)
    net = Sender(send_sem, recv_sem)
    copies = [net.push(rim, rim_out, peers[-1])]
    for e, peer in enumerate(peers):
        copies.append(net.push(terms.at[(c + e + 1) % CTX], parts.at[e], peer))
    for copy in copies:
        copy.wait_recv()
    summed = terms[c].astype(jnp.float32)
    for e in range(CTX - 1):
        summed = summed + parts[e].astype(jnp.float32)
    total[...] = summed
    net.drain()


def sum_key_grads(terms, rim):
    return call_kernel(
        key_grads_body,
        "sum_key_grads",
        4,
        (shape_of(terms.shape[1:], jnp.float32), shape_of(rim.shape, rim.dtype)),
        (terms, rim),
        16,
        (pltpu.VMEM((CTX - 1, *terms.shape[1:]), terms.dtype),),
    )


def dot_rows(left, right):
    return lax.dot_general(
        left, right, (((0,), (0,)), ((), ())), preferred_element_type=jnp.float32
    ).astype(jnp.bfloat16)


def weight_grads_body(
    norms,
    grads12,
    acts,
    grads3,
    small,
    out12,
    out3,
    both_norm,
    both12,
    both_act,
    both3,
    small_in,
    own12,
    own3,
    a_in12,
    a_in3,
    y_in12,
    y_in3,
    mid12,
    mid3,
    f_in12,
    f_in3,
    full12,
    full3,
    ya_in12,
    ya_in3,
    z_out12,
    z_out3,
    z_in12,
    z_in3,
    send_sem,
    recv_sem,
):
    f, c, y, low_z, core = place()
    toks = norms.shape[1]
    columns = [(y + e) % 4 for e in range(1, 4)]
    to_y = [{"ctx": at_ctx(q, low_z, core)} for q in columns]
    sibling = {"ctx": at_ctx(y, low_z, 1 - core)}
    over_z = {"ctx": at_ctx(y, 1 - low_z, core)}
    peers = [{"fsdp": (f + d) % FSDP} for d in range(1, FSDP)]
    meet(peers + to_y + [sibling, over_z])
    net = Sender(send_sem.at[pl.ds(14, 64)], recv_sem.at[pl.ds(14, 64)])
    half = pl.ds(pl.multiple_of(core * HALF, HALF), HALF)
    other_half = pl.ds(pl.multiple_of((1 - core) * HALF, HALF), HALF)
    here, there = pl.ds(0, toks), pl.ds(toks, toks)
    first = [
        net.push(norms.at[1 - core], both_norm.at[there], sibling),
        net.push(grads12.at[1 - core], both12.at[there], sibling),
        net.push(acts, both_act.at[:, there], sibling),
        net.push(grads3.at[:, :, other_half], both3.at[:, there], sibling),
        net.push(small, small_in, sibling),
    ]
    both_norm[here] = norms[core]
    both12[here] = grads12[core]
    both_act[:, here] = acts[...]
    both3[:, here] = grads3[:, :, half]
    for copy in first:
        copy.wait_recv()

    def block(owner):
        features = both_norm[:, pl.ds(pl.multiple_of(owner * 128, 128), 128)]
        for piece in range(3):
            wide = COLS // 3
            at = pl.ds(piece * wide, wide)
            own12[owner, :, at] = dot_rows(features, both12[:, at])
        extra = (small[owner] + small_in[owner]) * core.astype(jnp.float32)
        tail = own12[owner, 0:16, PAD_AT:COLS].astype(jnp.float32)
        own12[owner, 0:16, PAD_AT:COLS] = (tail + extra).astype(jnp.bfloat16)
        own3[owner, 0:64] = dot_rows(both_act[owner, :, 0:64], both3[0])
        own3[owner, 64:256] = dot_rows(both_act[owner, :, 64:256], both3[1])
        own3[owner, 256:512] = dot_rows(both_act[owner, :, 256:512], both3[2])

    def a_copies(d, owner):
        peer = {"fsdp": owner}
        return [
            pltpu.make_async_remote_copy(
                src_ref=src,
                dst_ref=dst,
                send_sem=send_sem.at[2 * d + k],
                recv_sem=recv_sem.at[2 * d + k],
                device_id=peer,
                device_id_type=MESH,
            )
            for k, (src, dst) in enumerate(
                (
                    (own12.at[owner, :, pl.ds(0, CUT_COLS)], a_in12.at[d]),
                    (own3.at[owner, pl.ds(0, CUT_ROWS)], a_in3.at[d]),
                )
            )
        ]

    def turn(d, nothing):
        owner = (f + d + 1) % FSDP
        block(owner)
        for copy in a_copies(d, owner):
            copy.start()
        return nothing

    lax.fori_loop(0, FSDP - 1, turn, 0)
    block(f)
    right = pl.ds(CUT_COLS, COLS - CUT_COLS)
    by_y = []
    for e, q in enumerate(columns):
        rows = pl.ds(pl.multiple_of(q * QUARTER, QUARTER), QUARTER)
        rows3 = pl.ds(pl.multiple_of(CUT_ROWS + q * QUARTER_B, 16), QUARTER_B)
        by_y.append(net.push(own12.at[:, rows, right], y_in12.at[e], to_y[e]))
        by_y.append(net.push(own3.at[:, rows3], y_in3.at[e], to_y[e]))
    for copy in by_y:
        copy.wait_recv()

    def middle(owner, nothing):
        rows = pl.ds(pl.multiple_of(y * QUARTER, QUARTER), QUARTER)
        rows3 = pl.ds(pl.multiple_of(CUT_ROWS + y * QUARTER_B, 16), QUARTER_B)
        total = own12[owner, rows, CUT_COLS:COLS].astype(jnp.float32)
        total3 = own3[owner, rows3].astype(jnp.float32)
        for e in range(3):
            total = total + y_in12[e, owner].astype(jnp.float32)
            total3 = total3 + y_in3[e, owner].astype(jnp.float32)
        mid12[owner] = total.astype(jnp.bfloat16)
        mid3[owner] = total3.astype(jnp.bfloat16)
        return nothing

    lax.fori_loop(0, FSDP, middle, 0)
    by_f = []
    for d in range(FSDP - 1):
        owner = (f + d + 1) % FSDP
        by_f.append(net.push(mid12.at[owner], f_in12.at[d], peers[d]))
        by_f.append(net.push(mid3.at[owner], f_in3.at[d], peers[d]))
    for d in range(FSDP - 1):
        for copy in a_copies(d, (f + d + 1) % FSDP):
            copy.wait_recv()

    def whole(q, nothing):
        rows = pl.ds(pl.multiple_of(q * QUARTER, QUARTER), QUARTER)
        rows3 = pl.ds(pl.multiple_of(q * QUARTER_A, 16), QUARTER_A)
        total = own12[f, rows, 0:CUT_COLS].astype(jnp.float32)
        total3 = own3[f, rows3].astype(jnp.float32)
        for d in range(FSDP - 1):
            total = total + a_in12[d, rows].astype(jnp.float32)
            total3 = total3 + a_in3[d, rows3].astype(jnp.float32)
        full12[q] = total.astype(jnp.bfloat16)
        full3[q] = total3.astype(jnp.bfloat16)
        return nothing

    lax.fori_loop(0, 4, whole, 0)
    by_ya = []
    for e, q in enumerate(columns):
        by_ya.append(net.push(full12.at[q], ya_in12.at[e], to_y[e]))
        by_ya.append(net.push(full3.at[q], ya_in3.at[e], to_y[e]))
    for copy in by_f:
        copy.wait_recv()
    total = mid12[f].astype(jnp.float32)
    total3 = mid3[f].astype(jnp.float32)
    for d in range(FSDP - 1):
        total = total + f_in12[d].astype(jnp.float32)
        total3 = total3 + f_in3[d].astype(jnp.float32)
    z_out12[:, CUT_COLS:COLS] = total.astype(jnp.bfloat16)
    z_out3[QUARTER_A:] = total3.astype(jnp.bfloat16)
    for copy in by_ya:
        copy.wait_recv()
    total = full12[y].astype(jnp.float32)
    total3 = full3[y].astype(jnp.float32)
    for e in range(3):
        total = total + ya_in12[e].astype(jnp.float32)
        total3 = total3 + ya_in3[e].astype(jnp.float32)
    z_out12[:, 0:CUT_COLS] = total.astype(jnp.bfloat16)
    z_out3[0:QUARTER_A] = total3.astype(jnp.bfloat16)
    swap = [net.push(z_out12, z_in12, over_z), net.push(z_out3, z_in3, over_z)]
    for copy in swap:
        copy.wait_recv()
    mine = pl.ds(pl.multiple_of(y * QUARTER, QUARTER), QUARTER)
    mine_a = pl.ds(pl.multiple_of(y * QUARTER_A, 16), QUARTER_A)
    mine_b = pl.ds(pl.multiple_of(CUT_ROWS + y * QUARTER_B, 16), QUARTER_B)
    out12[core, mine] = (
        z_out12[...].astype(jnp.float32) + z_in12[...].astype(jnp.float32)
    ).astype(jnp.bfloat16)
    total3 = (z_out3[...].astype(jnp.float32) + z_in3[...].astype(jnp.float32)).astype(jnp.bfloat16)
    out3[mine_a, half] = total3[:QUARTER_A]
    out3[mine_b, half] = total3[QUARTER_A:]
    spread = []
    for to in to_y:
        for ref in (out12.at[core, mine], out3.at[mine_a, half], out3.at[mine_b, half]):
            spread.append(net.push(ref, ref, to))
    for copy in spread:
        copy.wait_recv()
    last = [
        net.push(out12.at[core], out12.at[core], sibling),
        net.push(out3.at[:, half], out3.at[:, half], sibling),
    ]
    for copy in last:
        copy.wait_recv()
    for d in range(FSDP - 1):
        for copy in a_copies(d, (f + d + 1) % FSDP):
            copy.wait_send()
    net.drain()


def sum_weight_grads(norms, grads12, acts, grads3, small):
    toks = norms.shape[1]
    low = jnp.bfloat16
    right, below = COLS - CUT_COLS, OUT_ROWS - CUT_ROWS
    scratch = [
        ((2 * toks, 1024), low),
        ((2 * toks, COLS), low),
        ((FSDP, 2 * toks, HALF), low),
        ((3, 2 * toks, HALF), low),
        (small.shape, jnp.float32),
        ((FSDP, 128, COLS), low),
        ((FSDP, OUT_ROWS, HALF), low),
        ((FSDP - 1, 128, CUT_COLS), low),
        ((FSDP - 1, CUT_ROWS, HALF), low),
        ((3, FSDP, QUARTER, right), low),
        ((3, FSDP, QUARTER_B, HALF), low),
        ((FSDP, QUARTER, right), low),
        ((FSDP, QUARTER_B, HALF), low),
        ((FSDP - 1, QUARTER, right), low),
        ((FSDP - 1, QUARTER_B, HALF), low),
        ((4, QUARTER, CUT_COLS), low),
        ((4, QUARTER_A, HALF), low),
        ((3, QUARTER, CUT_COLS), low),
        ((3, QUARTER_A, HALF), low),
        ((QUARTER, COLS), low),
        ((QUARTER_A + QUARTER_B, HALF), low),
        ((QUARTER, COLS), low),
        ((QUARTER_A + QUARTER_B, HALF), low),
    ]
    return call_kernel(
        weight_grads_body,
        "sum_weight_grads",
        5,
        (shape_of((2, 128, COLS), low), shape_of((OUT_ROWS, 2 * HALF), low)),
        (norms, grads12, acts, grads3, small),
        80,
        [pltpu.VMEM(dims, kind) for dims, kind in scratch],
    )


def local(
    layer_input,
    segment_ids,
    norm_gain,
    w_query,
    w_key,
    w_value,
    w_attn_out,
    w_gate_z,
    w_inner,
    w_step,
    conv_weight,
    conv_bias,
    step_bias,
    decay_log,
    skip_gain,
    mixer_gain,
    w_mixer_out,
    ffn_gain,
    w_gate,
    w_up,
    w_down,
    out_grad,
):
    low = jnp.bfloat16
    tok_rows = layer_input.shape[1]
    ctx_here = lax.axis_index("ctx")
    first_pos = ctx_here * tok_rows
    seg_here = segment_ids[0]
    pos_here = first_pos + jnp.arange(tok_rows, dtype=jnp.int32)
    residual_in = layer_input[0].astype(jnp.float32)
    grad_final = out_grad[0].astype(jnp.float32)
    group_size = HEADS // KV_HEADS
    kv_width = KV_HEADS * HEAD_DIM
    q_width = HEADS * HEAD_DIM
    width_inner = SSM_HEADS * SSM_DIM
    conv_width = width_inner + 2 * STATE
    z_at = q_width + 2 * kv_width
    inner_at = z_at + width_inner
    step_at = inner_at + conv_width

    small = jnp.concatenate(
        [
            norm_gain,
            conv_weight.reshape(-1),
            conv_bias,
            step_bias,
            decay_log,
            skip_gain,
            mixer_gain,
            ffn_gain,
            jnp.zeros((2048 - SMALL,), low),
        ]
    ).reshape(16, 128)
    in_one = jnp.concatenate(
        [w_query, w_key, w_value, w_gate_z, w_inner, jnp.pad(w_step, ((0, 0), (0, 104)))], axis=1
    )
    in_two = jnp.concatenate([w_gate, w_up, jnp.pad(small, ((0, 112), (0, 0)))], axis=1)
    in_three = jnp.concatenate([w_attn_out, w_mixer_out, w_down], axis=0)
    all12, all3 = gather_weights(jnp.stack([in_one, in_two]), in_three)
    full_one = all12[0].reshape(FSDP * 128, COLS)
    full_two = all12[1].reshape(FSDP * 128, COLS)
    attn_out_full = all3[:, 0:64].reshape(q_width, -1)
    mixer_out_full = all3[:, 64:256].reshape(width_inner, -1)
    down_full = all3[:, 256:512].reshape(FSDP * 256, -1)
    smalls = all12[1, :, 0:16, PAD_AT:COLS].reshape(FSDP, 2048).astype(jnp.float32)
    gain_one_f = smalls[:, 0:128].reshape(-1)
    conv_f = (
        smalls[:, 128:1024].reshape(FSDP, CONV, 224).transpose(1, 0, 2).reshape(CONV, conv_width)
    )
    conv_bias_f = smalls[:, 1024:1248].reshape(-1)
    step_bias_f = smalls[:, 1248:1251].reshape(-1)
    decay_f = smalls[:, 1251:1254].reshape(-1)
    skip_f = smalls[:, 1254:1257].reshape(-1)
    mixer_gain_f = smalls[:, 1257:1449].reshape(-1)
    gain_two_f = smalls[:, 1449:1577].reshape(-1)

    normed_low = rms_scale(residual_in, gain_one_f).astype(low)
    angle_cos, angle_sin = rope_tables(pos_here)
    projected = matmul_f32(normed_low, full_one)
    query_rot = rotate(
        projected[:, :q_width].reshape(tok_rows, HEADS, HEAD_DIM), angle_cos, angle_sin
    ) * HEAD_DIM ** (-0.5)
    key_rot = (
        rotate(
            projected[:, q_width : q_width + kv_width].reshape(tok_rows, KV_HEADS, HEAD_DIM),
            angle_cos,
            angle_sin,
        )
        * key_scale
    )
    value_proj = projected[:, q_width + kv_width : z_at]
    gate_z = projected[:, z_at:inner_at]
    inner_pre = projected[:, inner_at:step_at]
    step_raw = projected[:, step_at : step_at + SSM_HEADS]
    query_low = query_rot.astype(low)
    local_kv = jnp.concatenate(
        [key_rot.reshape(tok_rows, kv_width).astype(low), value_proj.astype(low)], axis=1
    )
    kv_all, rim_got, seg_got = gather_keys(
        local_kv, inner_pre[tok_rows - 8 :], jnp.broadcast_to(segment_ids, (8, tok_rows))
    )
    seq_total = CTX * tok_rows
    pos_all = jnp.arange(seq_total, dtype=jnp.int32)
    seg_all = seg_got[:, 0].reshape(seq_total)
    kv_all = kv_all.reshape(seq_total, 2 * kv_width)
    key_heads = kv_all[:, :kv_width].reshape(seq_total, KV_HEADS, HEAD_DIM).transpose(1, 0, 2)
    value_heads = kv_all[:, kv_width:].reshape(seq_total, KV_HEADS, HEAD_DIM).transpose(1, 0, 2)
    query_heads = query_low.reshape(tok_rows, KV_HEADS, group_size, HEAD_DIM).transpose(1, 0, 2, 3)
    visible = (pos_all[None, :] <= pos_here[:, None]) & (seg_all[None, :] == seg_here[:, None])
    attended, log_total = lax.map(
        lambda head_parts: head_forward(head_parts[0], head_parts[1], head_parts[2], visible),
        (query_heads, key_heads, value_heads),
    )
    attn_low = attended.transpose(1, 0, 2, 3).reshape(tok_rows, q_width).astype(low)
    attn_branch = matmul_f32(attn_low, attn_out_full) * attn_out_scale

    rim_rows = CONV - 1
    rim_in = jnp.where(ctx_here > 0, rim_got[8 - rim_rows :], 0.0)
    extended = jnp.concatenate([rim_in, inner_pre], axis=0)
    rim_start = jnp.maximum(first_pos - rim_rows, 0)
    seg_rim = lax.dynamic_slice_in_dim(seg_all, rim_start, rim_rows)
    seg_ext = jnp.concatenate([seg_rim, seg_here])
    seg_prior = lax.dynamic_index_in_dim(seg_all, jnp.maximum(first_pos - 1, 0), keepdims=False)
    seg_before = jnp.where(ctx_here > 0, seg_prior, -1)
    values_ssm, input_map, output_map, step_size, log_decay = mixer_features(
        extended, seg_ext, seg_here, step_raw, conv_f, conv_bias_f, step_bias_f, decay_f
    )
    block_decay, block_state = ssd_states(
        values_ssm, input_map, step_size, log_decay, seg_here, seg_before
    )
    carried, decays = scan_forward(block_state, block_decay)
    mixer_result, entering = ssd_output(
        values_ssm,
        input_map,
        output_map,
        step_size,
        log_decay,
        seg_here,
        seg_before,
        skip_f,
        carried,
    )
    mixer_low = gate_norm(mixer_result, gate_z, mixer_gain_f).astype(low)
    mixer_branch = matmul_f32(mixer_low, mixer_out_full) * mixer_out_scale
    middle = residual_in + attn_branch + mixer_branch
    normed_two_low = rms_scale(middle, gain_two_f).astype(low)
    both_pre = matmul_f32(normed_two_low, full_two)
    ff_width = FSDP * 256
    gate_pre = both_pre[:, :ff_width] * gate_scale
    up_pre = both_pre[:, ff_width : 2 * ff_width]
    hidden_low = (jax.nn.silu(gate_pre) * up_pre).astype(low)
    layer_out = middle + matmul_f32(hidden_low, down_full) * down_scale

    grad_down_in = (grad_final * down_scale).astype(low)
    grad_hidden = right_trans(grad_down_in, down_full)
    gate_sig = jax.nn.sigmoid(gate_pre)
    grad_gate_in = (
        grad_hidden * up_pre * gate_sig * (1.0 + gate_pre * (1.0 - gate_sig)) * gate_scale
    ).astype(low)
    grad_up_in = (grad_hidden * gate_pre * gate_sig).astype(low)
    grads_two = jnp.concatenate(
        [grad_gate_in, grad_up_in, jnp.zeros((tok_rows, COLS - PAD_AT), low)], axis=1
    )
    grad_normed_two = right_trans(grads_two, full_two)
    _, pull_two = jax.vjp(rms_scale, middle, gain_two_f)
    grad_mid_norm, grad_gain_two = pull_two(grad_normed_two)
    grad_middle = grad_final + grad_mid_norm
    grad_mixer_in = (grad_middle * mixer_out_scale).astype(low)
    grad_mixer_normed = right_trans(grad_mixer_in, mixer_out_full)
    _, pull_gate = jax.vjp(gate_norm, mixer_result, gate_z, mixer_gain_f)
    grad_result, grad_gate_z, grad_mixer_gain = pull_gate(grad_mixer_normed)
    grad_weighted = grad_result * entering[:, :, None]
    grad_carried = jnp.einsum("thp,tn->phn", grad_weighted, output_map, precision=highest)
    grad_out_state = scan_backward(grad_carried, decays)
    grad_block_decay = jnp.sum(grad_out_state * carried, axis=(0, 2))

    def mixer_core(
        core_ext,
        core_step,
        core_conv,
        core_conv_bias,
        core_step_bias,
        core_decay,
        core_skip,
        core_carried,
    ):
        core_values, core_input, core_output, core_size, core_log = mixer_features(
            core_ext,
            seg_ext,
            seg_here,
            core_step,
            core_conv,
            core_conv_bias,
            core_step_bias,
            core_decay,
        )
        core_block_decay, core_block_state = ssd_states(
            core_values, core_input, core_size, core_log, seg_here, seg_before
        )
        core_result, _ = ssd_output(
            core_values,
            core_input,
            core_output,
            core_size,
            core_log,
            seg_here,
            seg_before,
            core_skip,
            core_carried,
        )
        return (core_result, core_block_decay, core_block_state)

    _, pull_core = jax.vjp(
        mixer_core, extended, step_raw, conv_f, conv_bias_f, step_bias_f, decay_f, skip_f, carried
    )
    grad_ext, grad_step_raw, grad_conv, grad_conv_bias, grad_step_bias, grad_decay, grad_skip, _ = (
        pull_core((grad_result, grad_block_decay, grad_out_state))
    )

    grad_attn_in = (grad_middle * attn_out_scale).astype(low)
    grad_attended = right_trans(grad_attn_in, attn_out_full).astype(low)
    grad_heads = grad_attended.reshape(tok_rows, KV_HEADS, group_size, HEAD_DIM).transpose(
        1, 0, 2, 3
    )
    grad_query_h, grad_key_h, grad_value_h = lax.map(
        lambda head_parts: head_backward(
            head_parts[0], head_parts[1], head_parts[2], head_parts[3], head_parts[4], visible
        ),
        (query_heads, key_heads, value_heads, grad_heads, log_total),
    )
    grad_kv_terms = jnp.concatenate(
        [
            grad_key_h.transpose(1, 0, 2).reshape(seq_total, kv_width),
            grad_value_h.transpose(1, 0, 2).reshape(seq_total, kv_width),
        ],
        axis=1,
    )
    grad_kv, rim_back = sum_key_grads(
        grad_kv_terms.astype(low).reshape(CTX, tok_rows, 2 * kv_width), grad_ext[:8]
    )
    rim_back = jnp.where(ctx_here < CTX - 1, rim_back[:rim_rows], 0.0)
    grad_inner_pre = grad_ext[rim_rows:] + jnp.pad(rim_back, ((tok_rows - rim_rows, 0), (0, 0)))
    grad_key_rot = grad_kv[:, :kv_width].reshape(tok_rows, KV_HEADS, HEAD_DIM)
    grad_key_low = (
        (rotate_back(grad_key_rot, angle_cos, angle_sin) * key_scale)
        .reshape(tok_rows, kv_width)
        .astype(low)
    )
    grad_query = grad_query_h.transpose(1, 0, 2, 3).reshape(tok_rows, HEADS, HEAD_DIM)
    grad_query_low = (
        (rotate_back(grad_query, angle_cos, angle_sin) * HEAD_DIM ** (-0.5))
        .reshape(tok_rows, q_width)
        .astype(low)
    )
    grads_one = jnp.concatenate(
        [
            grad_query_low,
            grad_key_low,
            grad_kv[:, kv_width:].astype(low),
            grad_gate_z.astype(low),
            grad_inner_pre.astype(low),
            jnp.pad(grad_step_raw.astype(low), ((0, 0), (0, COLS - step_at - SSM_HEADS))),
        ],
        axis=1,
    )
    grad_normed_one = right_trans(grads_one, full_one)
    _, pull_one = jax.vjp(rms_scale, residual_in, gain_one_f)
    grad_in_norm, grad_gain_one = pull_one(grad_normed_one)
    input_grad = grad_middle + grad_in_norm

    acts = jnp.concatenate(
        [
            attn_low.reshape(tok_rows, FSDP, 64),
            mixer_low.reshape(tok_rows, FSDP, 192),
            hidden_low.reshape(tok_rows, FSDP, 256),
        ],
        axis=2,
    ).transpose(1, 0, 2)
    small_grads = jnp.concatenate(
        [
            grad_gain_one.reshape(FSDP, 128),
            grad_conv.reshape(CONV, FSDP, 224).transpose(1, 0, 2).reshape(FSDP, CONV * 224),
            grad_conv_bias.reshape(FSDP, 224),
            grad_step_bias.reshape(FSDP, 3),
            grad_decay.reshape(FSDP, 3),
            grad_skip.reshape(FSDP, 3),
            grad_mixer_gain.reshape(FSDP, 192),
            grad_gain_two.reshape(FSDP, 128),
            jnp.zeros((FSDP, 2048 - SMALL), jnp.float32),
        ],
        axis=1,
    ).reshape(FSDP, 16, 128)
    sum12, sum3 = sum_weight_grads(
        jnp.stack([normed_low, normed_two_low]),
        jnp.stack([grads_one, grads_two]),
        acts,
        jnp.stack([grad_attn_in, grad_mixer_in, grad_down_in]),
        small_grads,
    )
    one, two, three = (
        sum12[0].astype(jnp.float32),
        sum12[1].astype(jnp.float32),
        sum3.astype(jnp.float32),
    )
    tiny = two[0:16, PAD_AT:COLS].reshape(-1)
    return (
        layer_out.astype(low)[None],
        input_grad[None],
        tiny[0:128],
        one[:, :q_width],
        one[:, q_width : q_width + kv_width],
        one[:, q_width + kv_width : z_at],
        three[0:64],
        one[:, z_at:inner_at],
        one[:, inner_at:step_at],
        one[:, step_at : step_at + SSM_HEADS],
        tiny[128:1024].reshape(CONV, 224),
        tiny[1024:1248],
        tiny[1248:1251],
        tiny[1251:1254],
        tiny[1254:1257],
        tiny[1257:1449],
        three[64:256],
        tiny[1449:1577],
        two[:, :ff_width],
        two[:, ff_width : 2 * ff_width],
        three[256:512],
    )


def solution(mesh):
    in_specs = (
        P("fsdp", "ctx", None),
        P("fsdp", "ctx"),
        P("fsdp"),
        P("fsdp", None),
        P("fsdp", None),
        P("fsdp", None),
        P("fsdp", None),
        P("fsdp", None),
        P("fsdp", None),
        P("fsdp", None),
        P(None, "fsdp"),
        P("fsdp"),
        P("fsdp"),
        P("fsdp"),
        P("fsdp"),
        P("fsdp"),
        P("fsdp", None),
        P("fsdp"),
        P("fsdp", None),
        P("fsdp", None),
        P("fsdp", None),
        P("fsdp", "ctx", None),
    )
    out_specs = (
        P("fsdp", "ctx", None),
        P("fsdp", "ctx", None),
        P("fsdp"),
        P("fsdp", None),
        P("fsdp", None),
        P("fsdp", None),
        P("fsdp", None),
        P("fsdp", None),
        P("fsdp", None),
        P("fsdp", None),
        P(None, "fsdp"),
        P("fsdp"),
        P("fsdp"),
        P("fsdp"),
        P("fsdp"),
        P("fsdp"),
        P("fsdp", None),
        P("fsdp"),
        P("fsdp", None),
        P("fsdp", None),
        P("fsdp", None),
    )
    return jax.shard_map(local, mesh=mesh, in_specs=in_specs, out_specs=out_specs, check_vma=False)
```

```python
import jax
import jax.numpy as jnp
from jax import lax
from jax.experimental import pallas as pl
from jax.experimental.pallas import tpu as pltpu
from jax.sharding import PartitionSpec as P

HEADS = 8
KV_HEADS = 2
HEAD_DIM = 64
SSM_HEADS = 24
SSM_DIM = 64
STATE = 128
CONV = 4


epsilon = 1e-05
rope_base = 10000.0
key_scale = 0.5
attn_out_scale = 0.8
mixer_out_scale = 0.5
gate_scale = 0.75
down_scale = 0.8
masked_score = -1e30
highest = lax.Precision.HIGHEST


def matmul_f32(left_side, right_side):
    return jnp.dot(left_side, right_side, preferred_element_type=jnp.float32)


def right_trans(left_side, right_side):
    return lax.dot_general(
        left_side, right_side, (((1,), (1,)), ((), ())), preferred_element_type=jnp.float32
    )


def rms_scale(values, gain_vec):
    return (
        values * lax.rsqrt(jnp.mean(values * values, axis=-1, keepdims=True) + epsilon) * gain_vec
    )


def rope_tables(positions):
    half_dim = HEAD_DIM // 2
    inverse = rope_base ** (-jnp.arange(half_dim, dtype=jnp.float32) / half_dim)
    angles = positions.astype(jnp.float32)[:, None] * inverse[None, :]
    return (jnp.cos(angles)[:, None, :], jnp.sin(angles)[:, None, :])


def rotate(values, angle_cos, angle_sin):
    half_dim = values.shape[-1] // 2
    first_half = values[..., :half_dim]
    second_half = values[..., half_dim:]
    return jnp.concatenate(
        [
            first_half * angle_cos - second_half * angle_sin,
            second_half * angle_cos + first_half * angle_sin,
        ],
        axis=-1,
    )


def rotate_back(values, angle_cos, angle_sin):
    half_dim = values.shape[-1] // 2
    first_half = values[..., :half_dim]
    second_half = values[..., half_dim:]
    return jnp.concatenate(
        [
            first_half * angle_cos + second_half * angle_sin,
            second_half * angle_cos - first_half * angle_sin,
        ],
        axis=-1,
    )


def conv_mix(extended, seg_ext, seg_here, conv_weight, conv_bias):
    row_count = seg_here.shape[0]
    summed = jnp.broadcast_to(conv_bias[None, :], (row_count, conv_bias.shape[0]))
    for offset in range(conv_weight.shape[0]):
        same_doc = (seg_ext[offset : offset + row_count] == seg_here)[:, None]
        summed = summed + conv_weight[offset][None, :] * jnp.where(
            same_doc, extended[offset : offset + row_count], 0.0
        )
    return jax.nn.silu(summed)


def mixer_features(
    extended, seg_ext, seg_here, step_raw, conv_weight, conv_bias, step_bias, decay_log
):
    mixed_rows = conv_mix(extended, seg_ext, seg_here, conv_weight, conv_bias)
    row_count = seg_here.shape[0]
    width_inner = SSM_HEADS * SSM_DIM
    values_ssm = mixed_rows[:, :width_inner].reshape(row_count, SSM_HEADS, SSM_DIM)
    input_map = mixed_rows[:, width_inner : width_inner + STATE]
    output_map = mixed_rows[:, width_inner + STATE :]
    step_size = jax.nn.softplus(step_raw + step_bias[None, :])
    log_decay = -step_size * jnp.exp(decay_log)[None, :]
    return (values_ssm, input_map, output_map, step_size, log_decay)


def ssd_states(values_ssm, input_map, step_size, log_decay, seg_here, seg_before):
    cumulative = jnp.cumsum(log_decay, axis=0)
    last_seg = seg_here[-1]
    tail_weight = (
        jnp.where(
            (seg_here == last_seg)[:, None], jnp.exp(cumulative[-1][None, :] - cumulative), 0.0
        )
        * step_size
    )
    weighted = tail_weight[:, :, None] * values_ssm
    block_state = jnp.einsum("shp,sn->phn", weighted, input_map, precision=highest)
    block_decay = jnp.exp(cumulative[-1]) * (last_seg == seg_before).astype(jnp.float32)
    return (block_decay, block_state)


def ssd_output(
    values_ssm,
    input_map,
    output_map,
    step_size,
    log_decay,
    seg_here,
    seg_before,
    skip_gain,
    carried,
):
    row_count = seg_here.shape[0]
    cumulative = jnp.cumsum(log_decay, axis=0)
    order_idx = jnp.arange(row_count, dtype=jnp.int32)
    causal_same = (seg_here[:, None] == seg_here[None, :]) & (
        order_idx[:, None] >= order_idx[None, :]
    )
    keep_mask = causal_same[:, :, None]
    spread = cumulative[:, None, :] - cumulative[None, :, :]
    decay_mat = jnp.where(keep_mask, jnp.exp(jnp.where(keep_mask, spread, 0.0)), 0.0)
    pairing = jnp.dot(output_map, input_map.T, precision=highest)
    mixing = decay_mat * pairing[:, :, None] * step_size[None, :, :]
    result = jnp.einsum("tsh,shp->thp", mixing, values_ssm, precision=highest)
    entering = jnp.exp(cumulative) * (seg_here == seg_before).astype(jnp.float32)[:, None]
    result = result + entering[:, :, None] * jnp.einsum(
        "tn,phn->thp", output_map, carried, precision=highest
    )
    return (result + skip_gain[None, :, None] * values_ssm, entering)


def gate_norm(result, gate_z, mixer_gain):
    flat_rows = result.reshape(gate_z.shape) * jax.nn.silu(gate_z)
    return rms_scale(flat_rows, mixer_gain)


MESH = pl.DeviceIdType.MESH
CTX = 16
FSDP = 8
COLS = 4352
PAD_AT = 4224
HALVES = {"one": 2176, "two": 2048, "three": 512}
UNIT_ROWS = {"one": 16, "two": 16, "three": 64}
ORDERS = (("x", "y", "z"), ("y", "z", "x"), ("z", "x", "y"))
CUTS = {
    "one": (((0, 16), (0, 768)), ((0, 16), (768, 1536)), ((0, 16), (1536, 2176))),
    "two": (((0, 16), (0, 256)), ((0, 16), (256, 1152)), ((0, 16), (1152, 2048))),
    "three": (((0, 32), (0, 512)), ((32, 48), (0, 512)), ((48, 64), (0, 512))),
}
OUT_ROWS = 512
EVERYTHING = ("x", "y", "z")
SMALL = 1577
CHUNK = SSM_DIM * SSM_HEADS // CTX
VMEM_LIMIT = 60 * 2**20


def place():
    f, c = lax.axis_index("fsdp"), lax.axis_index("ctx")
    return f, c, c // 4, (c // 2) % 2, c % 2


def at_ctx(y, low_z, core):
    return (y * 2 + low_z) * 2 + core


def meet(partners):
    barrier = pltpu.get_barrier_semaphore()
    for partner in partners:
        pl.semaphore_signal(barrier, inc=1, device_id=partner, device_id_type=MESH)
    pl.semaphore_wait(barrier, len(partners))


class Sender:
    def __init__(self, send_sem, recv_sem):
        self.send_sem, self.recv_sem, self.used, self.all = send_sem, recv_sem, 0, []

    def push(self, src, dst, partner):
        index = self.used
        self.used += 1
        copy = pltpu.make_async_remote_copy(
            src_ref=src,
            dst_ref=dst,
            send_sem=self.send_sem.at[index],
            recv_sem=self.recv_sem.at[index],
            device_id=partner,
            device_id_type=MESH,
        )
        copy.start()
        self.all.append(copy)
        return copy

    def drain(self):
        for copy in self.all:
            copy.wait_send()


def call_kernel(body, name, cid, outs, ins, sems, scratch=(), far_in=(), far_out=(), aliases=None):
    def spec(far):
        return pl.BlockSpec(memory_space=pl.ANY if far else pltpu.VMEM)

    return pl.pallas_call(
        body,
        name=name,
        out_shape=outs,
        in_specs=[spec(k in far_in) for k in range(len(ins))],
        out_specs=tuple(spec(k in far_out) for k in range(len(outs))),
        scratch_shapes=[
            *scratch,
            pltpu.SemaphoreType.DMA((sems,)),
            pltpu.SemaphoreType.DMA((sems,)),
        ],
        input_output_aliases=aliases or {},
        compiler_params=pltpu.CompilerParams(
            collective_id=cid, has_side_effects=True, vmem_limit_bytes=VMEM_LIMIT
        ),
    )(*ins)


def shape_of(dims, kind):
    return jax.ShapeDtypeStruct(dims, kind)


AXES = (("x", "x"), ("zh", "z"), ("y", "y"), ("zl", "z"))
EXTENT = {"x": 4, "zh": 2, "y": 4, "zl": 2}


def coordinates():
    f, c, y, low_z, core = place()
    return {"x": f // 2, "zh": f % 2, "y": y, "zl": low_z}, core


def neighbours(here, core):
    z = here["zh"] * 2 + here["zl"]
    found = {"x": [], "y": [], "z": []}
    for e in range(1, 4):
        found["x"].append({**here, "x": (here["x"] + e) % 4})
        found["y"].append({**here, "y": (here["y"] + e) % 4})
        other = (z + e) % 4
        found["z"].append({**here, "zh": other // 2, "zl": other % 2})
    return found


def device_of(at, core):
    return {"fsdp": at["x"] * 2 + at["zh"], "ctx": at_ctx(at["y"], at["zl"], core)}


def index_of(kept, fixed, at):
    return tuple(
        at[axis] if axis_dim in fixed else slice(None)
        for axis, axis_dim in AXES
        if axis_dim in kept
    )


def extents(kept):
    return tuple(EXTENT[axis] for axis, axis_dim in AXES if axis_dim in kept)


def span(pair):
    return pl.ds(pair[0], pair[1] - pair[0])


def cut_of(kind, part, core):
    rows, cols = CUTS[kind][part]
    at = pl.multiple_of(core * HALVES[kind] + cols[0], 128)
    return span(rows), pl.ds(at, cols[1] - cols[0])


def all_near(near, core):
    return [device_of(at, core) for dim in EVERYTHING for at in near[dim]]


class Gather:
    def __init__(self, net, outs, here, near, core):
        self.net, self.outs, self.here, self.near, self.core = net, outs, here, near, core
        self.pending, self.crossing = [[], [], []], []
        self.sibling = device_of(here, 1 - core)

    def pieces(self, part, fixed, at):
        index = index_of(EVERYTHING, fixed, at)
        return [
            ref.at[(*index, *cut_of(kind, part, self.core))] for kind, ref in self.outs.items()
        ]

    def own(self, ins, sem):
        point = index_of(EVERYTHING, EVERYTHING, self.here)
        copies = []
        for k, (kind, ref) in enumerate(self.outs.items()):
            half = HALVES[kind]
            cols = pl.ds(pl.multiple_of(self.core * half, 128), half)
            copies.append(
                pltpu.make_async_copy(
                    ins[kind].at[self.here["y"], self.here["zl"], :, cols],
                    ref.at[(*point, slice(None), cols)],
                    sem.at[k],
                )
            )
        return copies

    def stage(self, number, ins=None):
        for part, order in enumerate(ORDERS):
            steps = order[::-1]
            dim, fixed = steps[number], steps[number:]
            for copy in self.pending[part]:
                copy.wait_recv()
            refs = self.pieces(part, fixed, self.here)
            sources = refs
            if ins is not None:
                sources = [
                    ins[kind].at[
                        (self.here["y"], self.here["zl"], *cut_of(kind, part, self.core))
                    ]
                    for kind in self.outs
                ]
            self.pending[part] = [
                self.net.push(src, ref, device_of(at, self.core))
                for at in self.near[dim]
                for src, ref in zip(sources, refs)
            ]
            if number == 2:
                self.crossing += [self.net.push(ref, ref, self.sibling) for ref in refs]

    def settle(self):
        for part in range(3):
            for copy in self.pending[part]:
                copy.wait_recv()
        self.pending = [[], [], []]

    def finish(self):
        kinds = len(self.outs)
        for e in range(3):
            for part, order in enumerate(ORDERS):
                for copy in self.pending[part][kinds * e : kinds * e + kinds]:
                    copy.wait_recv()
                source = self.near[order[0]][2 - e]
                self.crossing += [
                    self.net.push(ref, ref, self.sibling)
                    for ref in self.pieces(part, (order[0],), source)
                ]
        for copy in self.crossing:
            copy.wait_recv()


def gather_shapes(kinds):
    return [
        shape_of((4, 2, 4, 2, UNIT_ROWS[kind], 2 * HALVES[kind]), jnp.bfloat16) for kind in kinds
    ]


def gather_body(in_one, small, out_one, out_small, own_sem, send_sem, recv_sem):
    here, core = coordinates()
    near = neighbours(here, core)
    f = here["x"] * 2 + here["zh"]
    small_peers = [{"fsdp": (f + d) % FSDP} for d in range(1, FSDP)]
    meet(
        all_near(near, core)
        + [{"fsdp": (here["x"] + e) % 4 * 2 + 1 - here["zh"]} for e in range(1, 4)]
        + [device_of(here, 1 - core)]
    )
    net = Sender(send_sem, recv_sem)
    gather = Gather(net, {"one": out_one}, here, near, core)
    gather.stage(0, {"one": in_one})
    own = gather.own({"one": in_one}, own_sem)
    own.append(pltpu.make_async_copy(small, out_small.at[f], own_sem.at[1]))
    for copy in own:
        copy.start()
    tiny = [net.push(small, out_small.at[f], peer) for peer in small_peers]
    for copy in own:
        copy.wait()
    gather.stage(1)
    gather.stage(2)
    gather.finish()
    for copy in tiny:
        copy.wait_recv()
    net.drain()


def gather_weights(in_one, small):
    return call_kernel(
        gather_body,
        "gather_weights",
        0,
        (*gather_shapes(["one"]), shape_of((FSDP, 16, 128), jnp.bfloat16)),
        (in_one.reshape(4, 2, 16, COLS), small),
        46,
        (pltpu.SemaphoreType.DMA((2,)),),
        (0, 1),
        (0, 1),
    )


def ctx_peers(c):
    return [{"ctx": (c + e) % CTX} for e in range(1, CTX)]


def keys_body(
    kv,
    rim,
    seg,
    in_two,
    in_three,
    kv_all,
    rim_out,
    seg_all,
    out_two,
    out_three,
    own_sem,
    send_sem,
    recv_sem,
):
    here, core = coordinates()
    near = neighbours(here, core)
    c = at_ctx(here["y"], here["zl"], core)
    peers = ctx_peers(c)
    meet(peers + all_near(near, core))
    net = Sender(send_sem, recv_sem)
    copies = [net.push(rim, rim_out, peers[0])]
    for peer in peers:
        copies.append(net.push(kv, kv_all.at[c], peer))
        copies.append(net.push(seg, seg_all.at[c], peer))
    ins = {"two": in_two, "three": in_three}
    gather = Gather(net, {"two": out_two, "three": out_three}, here, near, core)
    gather.stage(0, ins)
    own = gather.own(ins, own_sem)
    for copy in own:
        copy.start()
    kv_all[c] = kv[...]
    seg_all[c] = seg[...]
    for copy in own:
        copy.wait()
    gather.stage(1)
    for copy in copies:
        copy.wait_recv()
    gather.settle()
    net.drain()


def gather_keys(kv, rim, seg, in_two, in_three):
    return call_kernel(
        keys_body,
        "gather_keys",
        1,
        (
            shape_of((CTX, *kv.shape), kv.dtype),
            shape_of(rim.shape, rim.dtype),
            shape_of((CTX, *seg.shape), seg.dtype),
            *gather_shapes(["two", "three"]),
        ),
        (
            kv,
            rim,
            seg,
            in_two.reshape(4, 2, 16, 2 * HALVES["two"]),
            in_three.reshape(4, 2, 64, 2 * HALVES["three"]),
        ),
        67,
        (pltpu.SemaphoreType.DMA((2,)),),
        (3, 4),
        (3, 4),
    )


def scan_rows(order, decay_of, parts, carries):
    state = jnp.zeros((CHUNK, STATE), jnp.float32)
    for at in order:
        carries[at] = state.astype(jnp.bfloat16)
        decay = decay_of[at]
        whole = jnp.concatenate([decay] * (CHUNK // SSM_HEADS), axis=0)
        state = whole * state + parts[at].astype(jnp.float32)


def send_back(net, c, peers, carries, carried):
    copies = [
        net.push(carries.at[(c + e + 1) % CTX], carried.at[c], peer) for e, peer in enumerate(peers)
    ]
    carried[c] = carries[c]
    return copies


def across(left, right):
    return lax.dot_general(
        left, right, (((1,), (1,)), ((), ())), preferred_element_type=jnp.float32
    )


def down(left, right):
    return lax.dot_general(
        left, right, (((0,), (0,)), ((), ())), preferred_element_type=jnp.float32
    )


def forward_body(
    states,
    decay,
    query,
    kv_all,
    hidden_mask,
    in_two,
    in_three,
    carried,
    decays,
    attended,
    log_total,
    out_two,
    out_three,
    parts,
    carries,
    send_sem,
    recv_sem,
):
    here, core = coordinates()
    near = neighbours(here, core)
    c = at_ctx(here["y"], here["zl"], core)
    peers = ctx_peers(c)
    meet(peers + all_near(near, core))
    net = Sender(send_sem, recv_sem)
    copies = []
    for e, peer in enumerate(peers):
        copies.append(net.push(states.at[(c + e + 1) % CTX], parts.at[c], peer))
        copies.append(net.push(decay, decays.at[c], peer))
    gather = Gather(net, {"two": out_two, "three": out_three}, here, near, core)
    gather.stage(2)
    parts[c] = states[c]
    decays[c] = decay[...]
    rows = kv_all.shape[1]

    def head(h, nothing):
        keys = kv_all[:, :, 0:128].reshape(CTX * rows, 128)
        values = kv_all[:, :, 128:256].reshape(CTX * rows, 128)
        scores = across(query[h], keys) + hidden_mask[...]
        row_max = jnp.max(scores, axis=-1, keepdims=True)
        weights = jnp.exp(scores - row_max)
        row_sum = jnp.sum(weights, axis=-1, keepdims=True)
        probs = (weights / row_sum).astype(jnp.bfloat16)
        attended[h] = jnp.dot(probs, values, preferred_element_type=jnp.float32).astype(
            jnp.bfloat16
        )
        log_total[h] = jnp.broadcast_to(row_max + jnp.log(row_sum), (rows, 128))
        return nothing

    lax.fori_loop(0, HEADS // 2, head, 0)
    for copy in copies:
        copy.wait_recv()
    scan_rows(range(CTX), decays, parts, carries)
    back = send_back(net, c, peers, carries, carried)
    lax.fori_loop(HEADS // 2, HEADS, head, 0)
    gather.finish()
    for copy in back:
        copy.wait_recv()
    net.drain()


def scan_forward(states, decay, query, kv_all, hidden_mask, all_two, all_three):
    chunks = states.astype(jnp.bfloat16).reshape(CTX, CHUNK, STATE)
    wide = jnp.broadcast_to(decay[:, None], (SSM_HEADS, STATE))
    rows = query.shape[1]
    carried, decays, attended, log_total, two, three = call_kernel(
        forward_body,
        "scan_forward",
        2,
        (
            shape_of((CTX, CHUNK, STATE), jnp.bfloat16),
            shape_of((CTX, SSM_HEADS, STATE), jnp.float32),
            shape_of((HEADS, rows, 128), jnp.bfloat16),
            shape_of((HEADS, rows, 128), jnp.float32),
            shape_of(all_two.shape, all_two.dtype),
            shape_of(all_three.shape, all_three.dtype),
        ),
        (chunks, wide, query, kv_all, hidden_mask, all_two, all_three),
        87,
        (pltpu.VMEM((CTX, CHUNK, STATE), jnp.bfloat16),) * 2,
        (5, 6),
        (4, 5),
        {5: 4, 6: 5},
    )
    carried = carried.reshape(SSM_DIM, SSM_HEADS, STATE).astype(jnp.float32)
    return carried, decays, attended, log_total, two, three


def dot_rows(left, right):
    return down(left, right).astype(jnp.bfloat16)


class Sums:
    def __init__(self, net, kinds, here, near, core, came, summed, own=None):
        self.net, self.kinds, self.here, self.near, self.core = net, kinds, here, near, core
        self.came, self.summed, self.own = came, summed, own
        self.pending = [None, None, None]

    def refs(self, part, stage, fixed, at):
        index = index_of(ORDERS[part][stage:], fixed, at)
        if stage:
            return [ref.at[index] for ref in self.summed[part, stage - 1]]
        return [
            ref.at[(*index, *(span(pair) for pair in CUTS[kind][part]))]
            for kind, ref in zip(self.kinds, self.own)
        ]

    def early(self, e, send_sem, recv_sem):
        at = {**self.here, "x": (self.here["x"] + e + 1) % 4}
        return [
            pltpu.make_async_remote_copy(
                src_ref=src,
                dst_ref=dst.at[e],
                send_sem=send_sem.at[len(self.kinds) * e + k],
                recv_sem=recv_sem.at[len(self.kinds) * e + k],
                device_id=device_of(at, self.core),
                device_id_type=MESH,
            )
            for k, (src, dst) in enumerate(
                zip(self.refs(0, 0, ("x",), at), self.came[0, 0])
            )
        ]

    def send(self, part, stage):
        dim = ORDERS[part][stage]
        self.pending[part] = [
            self.net.push(src, dst.at[e], device_of(at, self.core))
            for e, at in enumerate(self.near[dim])
            for src, dst in zip(self.refs(part, stage, (dim,), at), self.came[part, stage])
        ]

    def wait(self, part):
        for copy in self.pending[part] or ():
            copy.wait_recv()

    def add_up(self, part, stage):
        kept, rest = ORDERS[part][stage:], ORDERS[part][stage + 1 :]

        def unit(number, nothing):
            at, left = dict(self.here), number
            for axis, axis_dim in reversed(AXES):
                if axis_dim in rest:
                    at[axis] = left % EXTENT[axis]
                    left = left // EXTENT[axis]
            inner = index_of(rest, rest, at)
            own_refs = self.refs(part, stage, kept, at)
            for own, came, out in zip(
                own_refs, self.came[part, stage], self.summed[part, stage]
            ):
                total = own[...].astype(jnp.float32)
                for e in range(3):
                    total = total + came[(e, *inner)].astype(jnp.float32)
                out[inner if inner else Ellipsis] = total.astype(jnp.bfloat16)
            return nothing

        count = 1
        for size in extents(rest):
            count *= size
        if count == 1:
            unit(0, 0)
        else:
            lax.fori_loop(0, count, unit, 0)


def piece_shapes(kinds, part):
    return [
        tuple(pair[1] - pair[0] for pair in CUTS[kind][part]) for kind in kinds
    ]


def came_shapes(kinds, part, stage):
    rest = extents(ORDERS[part][stage + 1 :])
    return [(3, *rest, *shape) for shape in piece_shapes(kinds, part)]


def summed_shapes(kinds, part, stage):
    rest = extents(ORDERS[part][stage + 1 :])
    return [(*rest, *shape) for shape in piece_shapes(kinds, part)]


def stage_keys(stages):
    return [(part, stage) for part in range(3) for stage in stages]


def take(refs, keys, kinds):
    found = {}
    for key in keys:
        found[key], refs = refs[: len(kinds)], refs[len(kinds) :]
    return found, refs


def low_scratch(shapes):
    return [pltpu.VMEM(dims, jnp.bfloat16) for dims in shapes]


def half_of(core, kind):
    return pl.ds(pl.multiple_of(core * HALVES[kind], 128), HALVES[kind])


LATE = ("two", "three")


def backward_body(
    states,
    decays,
    query,
    grad_out,
    kv_all,
    hidden_mask,
    log_total,
    norm,
    grads_two,
    acts,
    grads_three,
    carried,
    grad_query,
    terms,
    *rest,
):
    summed, rest = take(rest, stage_keys([0]), LATE)
    came, rest = take(rest, stage_keys([0]), LATE)
    parts, carries, both_norm, both_two, both_act, both_three, own_two, own_three = rest[:8]
    key_sum, value_sum, send_sem, recv_sem = rest[8:]
    here, core = coordinates()
    near = neighbours(here, core)
    c = at_ctx(here["y"], here["zl"], core)
    peers = ctx_peers(c)
    meet(peers + all_near(near, core))
    net = Sender(send_sem.at[pl.ds(6, 46)], recv_sem.at[pl.ds(6, 46)])
    copies = [
        net.push(states.at[(c + e + 1) % CTX], parts.at[c], peer) for e, peer in enumerate(peers)
    ]
    sibling = device_of(here, 1 - core)
    toks = norm.shape[0]
    mine, theirs = pl.ds(0, toks), pl.ds(toks, toks)
    other = 1 - core
    first = [
        net.push(norm, both_norm.at[theirs], sibling),
        net.push(grads_two.at[:, half_of(other, "two")], both_two.at[theirs], sibling),
        net.push(acts, both_act.at[:, theirs], sibling),
        net.push(grads_three.at[:, :, half_of(other, "three")], both_three.at[:, theirs], sibling),
    ]
    parts[c] = states[c]
    both_norm[mine] = norm[...]
    both_two[mine] = grads_two[:, half_of(core, "two")]
    both_act[:, mine] = acts[...]
    both_three[:, mine] = grads_three[:, :, half_of(core, "three")]
    for copy in first:
        copy.wait_recv()

    def block(owner_x, owner_z):
        owner = owner_x * 2 + owner_z
        features = both_norm[:, pl.ds(pl.multiple_of(owner * 128, 128), 128)]
        wide = HALVES["two"] // 2
        for piece in range(2):
            at = pl.ds(piece * wide, wide)
            found = dot_rows(features, both_two[:, at])
            for unit in range(8):
                own_two[owner_x, owner_z, unit // 2, unit % 2, :, at] = found[
                    unit * 16 : unit * 16 + 16
                ]
        found = (
            dot_rows(both_act[owner, :, 0:64], both_three[0]),
            dot_rows(both_act[owner, :, 64:256], both_three[1]),
            dot_rows(both_act[owner, :, 256:512], both_three[2]),
        )
        for unit in range(8):
            source, at = (0, 0) if unit < 1 else (1, 64) if unit < 4 else (2, 256)
            own_three[owner_x, owner_z, unit // 2, unit % 2] = found[source][
                unit * 64 - at : unit * 64 - at + 64
            ]

    sums = Sums(net, LATE, here, near, core, came, summed, (own_two, own_three))

    def turn(e, nothing):
        owner_x = (here["x"] + e + 1) % 4
        block(owner_x, 0)
        block(owner_x, 1)
        for copy in sums.early(e, send_sem, recv_sem):
            copy.start()
        return nothing

    lax.fori_loop(0, 3, turn, 0)

    def own_turn(owner_z, nothing):
        block(here["x"], owner_z)
        return nothing

    lax.fori_loop(0, 2, own_turn, 0)
    sums.send(1, 0)
    sums.send(2, 0)
    for copy in copies:
        copy.wait_recv()
    scan_rows(range(CTX - 1, -1, -1), decays, parts, carries)
    back = send_back(net, c, peers, carries, carried)
    key_sum[...] = jnp.zeros_like(key_sum)
    value_sum[...] = jnp.zeros_like(value_sum)

    def head(h, nothing):
        keys = kv_all[:, :, 0:128].reshape(CTX * toks, 128)
        values = kv_all[:, :, 128:256].reshape(CTX * toks, 128)
        scores = across(query[h], keys) + hidden_mask[...]
        probs = jnp.exp(scores - log_total[h][:, 0:1])
        grad_probs = across(grad_out[h], values)
        inner = jnp.sum(probs * grad_probs, axis=-1, keepdims=True)
        grad_scores = (probs * (grad_probs - inner)).astype(jnp.bfloat16)
        grad_query[h] = jnp.dot(grad_scores, keys, preferred_element_type=jnp.float32)
        key_sum[...] += down(query[h], grad_scores)
        value_sum[...] += down(grad_out[h], probs.astype(jnp.bfloat16))
        return nothing

    lax.fori_loop(0, HEADS, head, 0)
    for k in range(CTX):
        at = pl.ds(k * toks, toks)
        terms[k, 0:128] = key_sum[:, at].astype(jnp.bfloat16)
        terms[k, 128:256] = value_sum[:, at].astype(jnp.bfloat16)
    for e in range(3):
        for copy in sums.early(e, send_sem, recv_sem):
            copy.wait_recv()
    for part in range(3):
        sums.wait(part)
        sums.add_up(part, 0)
    for copy in back:
        copy.wait_recv()
    for e in range(3):
        for copy in sums.early(e, send_sem, recv_sem):
            copy.wait_send()
    net.drain()


def scan_backward(
    states, decays, query, grad_out, kv_all, hidden_mask, log_total, norm, grads_two, acts, grads_three
):
    chunks = states.astype(jnp.bfloat16).reshape(CTX, CHUNK, STATE)
    low = jnp.bfloat16
    rows = query.shape[1]
    sums = [
        shape
        for part in range(3)
        for shape in summed_shapes(LATE, part, 0)
    ]
    scratch = [shape for part in range(3) for shape in came_shapes(LATE, part, 0)]
    scratch += [
        (CTX, CHUNK, STATE),
        (CTX, CHUNK, STATE),
        (2 * rows, 1024),
        (2 * rows, HALVES["two"]),
        (FSDP, 2 * rows, HALVES["three"]),
        (3, 2 * rows, HALVES["three"]),
        (4, 2, 4, 2, 16, HALVES["two"]),
        (4, 2, 4, 2, 64, HALVES["three"]),
    ]
    results = call_kernel(
        backward_body,
        "scan_backward",
        3,
        (
            shape_of((CTX, CHUNK, STATE), low),
            shape_of((HEADS, rows, 128), jnp.float32),
            shape_of((CTX, 256, rows), low),
            *[shape_of(dims, low) for dims in sums],
        ),
        (
            chunks,
            decays,
            query,
            grad_out,
            kv_all,
            hidden_mask,
            log_total,
            norm,
            grads_two,
            acts,
            grads_three,
        ),
        52,
        [*low_scratch(scratch), *[pltpu.VMEM((128, CTX * rows), jnp.float32)] * 2],
    )
    carried, grad_query, terms = results[:3]
    carried = carried.reshape(SSM_DIM, SSM_HEADS, STATE).astype(jnp.float32)
    return carried, grad_query, terms, results[3:]


def key_grads_body(terms, rim, *rest):
    before, rest = take(rest, stage_keys([0]), LATE)
    total, rim_out, out_two, out_three = rest[:4]
    came, rest = take(rest[4:], stage_keys([1, 2]), LATE)
    summed, rest = take(rest, stage_keys([1, 2]), LATE)
    parts, send_sem, recv_sem = rest
    here, core = coordinates()
    near = neighbours(here, core)
    c = at_ctx(here["y"], here["zl"], core)
    peers = ctx_peers(c)
    meet(peers + all_near(near, core))
    net = Sender(send_sem, recv_sem)
    copies = [net.push(rim, rim_out, peers[-1])]
    for e, peer in enumerate(peers):
        copies.append(net.push(terms.at[(c + e + 1) % CTX], parts.at[e], peer))
    sums = Sums(net, LATE, here, near, core, came, {**before, **summed})
    for part in range(3):
        sums.send(part, 1)
    for part in range(3):
        sums.wait(part)
        sums.add_up(part, 1)
        sums.send(part, 2)
    for copy in copies:
        copy.wait_recv()
    collected = terms[c].astype(jnp.float32)
    for e in range(CTX - 1):
        collected = collected + parts[e].astype(jnp.float32)
    total[...] = collected
    for part in range(3):
        sums.wait(part)
        sums.add_up(part, 2)
        for kind, out, ref in zip(LATE, (out_two, out_three), summed[part, 2]):
            out[tuple(span(pair) for pair in CUTS[kind][part])] = ref[...]
    net.drain()


def sum_key_grads(terms, rim, before):
    low = jnp.bfloat16
    scratch = [shape for key in stage_keys([1, 2]) for shape in came_shapes(LATE, *key)]
    scratch += [shape for key in stage_keys([1, 2]) for shape in summed_shapes(LATE, *key)]
    scratch += [(CTX - 1, *terms.shape[1:])]
    return call_kernel(
        key_grads_body,
        "sum_key_grads",
        4,
        (
            shape_of(terms.shape[1:], jnp.float32),
            shape_of(rim.shape, rim.dtype),
            shape_of((16, HALVES["two"]), low),
            shape_of((64, HALVES["three"]), low),
        ),
        (terms, rim, *before),
        52,
        low_scratch(scratch),
    )


FIRST = ("one",)


def weight_grads_body(
    norm, grads_one, small, unit_two, unit_three, out_one, out_two, out_three, *rest
):
    came, rest = take(rest, stage_keys(range(3)), FIRST)
    summed, rest = take(rest, stage_keys(range(3)), FIRST)
    both_norm, both_one, own_one, small_in, send_sem, recv_sem = rest
    here, core = coordinates()
    near = neighbours(here, core)
    toks = norm.shape[0]
    sibling = device_of(here, 1 - core)
    meet(all_near(near, core) + [sibling])
    net = Sender(send_sem.at[pl.ds(3, 42)], recv_sem.at[pl.ds(3, 42)])
    mine, theirs = pl.ds(0, toks), pl.ds(toks, toks)
    first = [
        net.push(norm, both_norm.at[theirs], sibling),
        net.push(grads_one.at[:, half_of(1 - core, "one")], both_one.at[theirs], sibling),
        net.push(small, small_in, sibling),
    ]
    both_norm[mine] = norm[...]
    both_one[mine] = grads_one[:, half_of(core, "one")]
    over_z = device_of({**here, "zl": 1 - here["zl"]}, core)
    y, low_z = here["y"], here["zl"]
    late = {"two": out_two, "three": out_three}
    out_two[y, low_z, :, half_of(core, "two")] = unit_two[...]
    out_three[y, low_z, :, half_of(core, "three")] = unit_three[...]

    def pass_on(kind, ref, at_y, at_z, targets):
        piece = ref.at[at_y, at_z, :, half_of(core, kind)]
        return [net.push(piece, piece, target) for target in targets]

    def late_step(at_y, at_z, targets):
        return [
            copy
            for kind, ref in late.items()
            for copy in pass_on(kind, ref, at_y, at_z, targets)
        ]

    to_y = [device_of(at, core) for at in near["y"]]
    late_copies = late_step(y, low_z, [over_z])
    for copy in first:
        copy.wait_recv()

    def block(owner_x, owner_z):
        owner = owner_x * 2 + owner_z
        features = both_norm[:, pl.ds(pl.multiple_of(owner * 128, 128), 128)]
        for low_at, high_at in ((0, 1024), (1024, 2176)):
            found = dot_rows(features, both_one[:, low_at:high_at])
            for unit in range(8):
                rows = found[unit * 16 : unit * 16 + 16]
                if unit == 0 and low_at:
                    extra = (small[owner] + small_in[owner]) * core.astype(jnp.float32)
                    tail = rows[:, 1024:].astype(jnp.float32) + extra
                    rows = jnp.concatenate([rows[:, :1024], tail.astype(jnp.bfloat16)], axis=1)
                own_one[owner_x, owner_z, unit // 2, unit % 2, :, low_at:high_at] = rows

    sums = Sums(net, FIRST, here, near, core, came, summed, (own_one,))

    def turn(e, nothing):
        owner_x = (here["x"] + e + 1) % 4
        block(owner_x, 0)
        block(owner_x, 1)
        for copy in sums.early(e, send_sem, recv_sem):
            copy.start()
        return nothing

    lax.fori_loop(0, 3, turn, 0)

    def own_turn(owner_z, nothing):
        block(here["x"], owner_z)
        return nothing

    lax.fori_loop(0, 2, own_turn, 0)
    sums.send(1, 0)
    sums.send(2, 0)
    for copy in late_copies:
        copy.wait_recv()
    late_copies = late_step(y, slice(None), to_y)
    for e in range(3):
        for copy in sums.early(e, send_sem, recv_sem):
            copy.wait_recv()
    for stage in range(3):
        for part in range(3):
            sums.wait(part)
            sums.add_up(part, stage)
            if stage < 2:
                sums.send(part, stage + 1)
        if stage == 1:
            for copy in late_copies:
                copy.wait_recv()
            late_copies = late_step(slice(None), slice(None), [sibling])
    for part in range(3):
        rows, cols = cut_of("one", part, core)
        out_one[y, low_z, rows, cols] = summed[part, 2][0][...]
    for step in (
        (y, low_z, [over_z]),
        (y, slice(None), to_y),
        (slice(None), slice(None), [sibling]),
    ):
        for copy in pass_on("one", out_one, *step):
            copy.wait_recv()
    for copy in late_copies:
        copy.wait_recv()
    for e in range(3):
        for copy in sums.early(e, send_sem, recv_sem):
            copy.wait_send()
    net.drain()


def sum_weight_grads(norm, grads_one, small, unit_two, unit_three):
    toks = norm.shape[0]
    low = jnp.bfloat16
    scratch = [shape for key in stage_keys(range(3)) for shape in came_shapes(FIRST, *key)]
    scratch += [shape for key in stage_keys(range(3)) for shape in summed_shapes(FIRST, *key)]
    scratch += [
        (2 * toks, 1024),
        (2 * toks, HALVES["one"]),
        (4, 2, 4, 2, 16, HALVES["one"]),
    ]
    return call_kernel(
        weight_grads_body,
        "sum_weight_grads",
        5,
        tuple(
            shape_of((4, 2, UNIT_ROWS[kind], 2 * HALVES[kind]), low)
            for kind in ("one", "two", "three")
        ),
        (norm, grads_one, small, unit_two, unit_three),
        45,
        [*low_scratch(scratch), pltpu.VMEM(small.shape, jnp.float32)],
    )


def spread_heads(values):
    by_head = values.transpose(1, 0, 2)
    group = jnp.arange(HEADS)[:, None, None] // (HEADS // KV_HEADS)
    empty = jnp.zeros_like(by_head)
    return jnp.concatenate(
        [jnp.where(group == 0, by_head, empty), jnp.where(group == 1, by_head, empty)], axis=2
    )


def join_heads(values):
    group = jnp.arange(HEADS)[:, None, None] // (HEADS // KV_HEADS)
    joined = jnp.where(group == 0, values[:, :, :HEAD_DIM], values[:, :, HEAD_DIM:])
    return joined.transpose(1, 0, 2)


def local(
    layer_input,
    segment_ids,
    norm_gain,
    w_query,
    w_key,
    w_value,
    w_attn_out,
    w_gate_z,
    w_inner,
    w_step,
    conv_weight,
    conv_bias,
    step_bias,
    decay_log,
    skip_gain,
    mixer_gain,
    w_mixer_out,
    ffn_gain,
    w_gate,
    w_up,
    w_down,
    out_grad,
):
    low = jnp.bfloat16
    tok_rows = layer_input.shape[1]
    ctx_here = lax.axis_index("ctx")
    first_pos = ctx_here * tok_rows
    seg_here = segment_ids[0]
    pos_here = first_pos + jnp.arange(tok_rows, dtype=jnp.int32)
    residual_in = layer_input[0].astype(jnp.float32)
    grad_final = out_grad[0].astype(jnp.float32)
    kv_width = KV_HEADS * HEAD_DIM
    q_width = HEADS * HEAD_DIM
    width_inner = SSM_HEADS * SSM_DIM
    conv_width = width_inner + 2 * STATE
    z_at = q_width + 2 * kv_width
    inner_at = z_at + width_inner
    step_at = inner_at + conv_width

    small = jnp.concatenate(
        [
            norm_gain,
            conv_weight.reshape(-1),
            conv_bias,
            step_bias,
            decay_log,
            skip_gain,
            mixer_gain,
            ffn_gain,
            jnp.zeros((2048 - SMALL,), low),
        ]
    ).reshape(16, 128)
    in_one = jnp.concatenate(
        [w_query, w_key, w_value, w_gate_z, w_inner, jnp.pad(w_step, ((0, 0), (0, 232)))], axis=1
    )
    all_one, all_small = gather_weights(in_one, small)
    full_one = all_one.reshape(FSDP * 128, COLS)
    smalls = all_small.reshape(FSDP, 2048).astype(jnp.float32)
    gain_one_f = smalls[:, 0:128].reshape(-1)
    conv_f = (
        smalls[:, 128:1024].reshape(FSDP, CONV, 224).transpose(1, 0, 2).reshape(CONV, conv_width)
    )
    conv_bias_f = smalls[:, 1024:1248].reshape(-1)
    step_bias_f = smalls[:, 1248:1251].reshape(-1)
    decay_f = smalls[:, 1251:1254].reshape(-1)
    skip_f = smalls[:, 1254:1257].reshape(-1)
    mixer_gain_f = smalls[:, 1257:1449].reshape(-1)
    gain_two_f = smalls[:, 1449:1577].reshape(-1)

    normed_low = rms_scale(residual_in, gain_one_f).astype(low)
    angle_cos, angle_sin = rope_tables(pos_here)
    projected = matmul_f32(normed_low, full_one)
    query_rot = rotate(
        projected[:, :q_width].reshape(tok_rows, HEADS, HEAD_DIM), angle_cos, angle_sin
    ) * HEAD_DIM ** (-0.5)
    key_rot = (
        rotate(
            projected[:, q_width : q_width + kv_width].reshape(tok_rows, KV_HEADS, HEAD_DIM),
            angle_cos,
            angle_sin,
        )
        * key_scale
    )
    value_proj = projected[:, q_width + kv_width : z_at]
    gate_z = projected[:, z_at:inner_at]
    inner_pre = projected[:, inner_at:step_at]
    step_raw = projected[:, step_at : step_at + SSM_HEADS]
    query_low = query_rot.astype(low)
    local_kv = jnp.concatenate(
        [key_rot.reshape(tok_rows, kv_width).astype(low), value_proj.astype(low)], axis=1
    )
    kv_all, rim_got, seg_got, all_two, all_three = gather_keys(
        local_kv,
        inner_pre[tok_rows - 8 :],
        jnp.broadcast_to(segment_ids, (8, tok_rows)),
        jnp.concatenate([w_gate, w_up], axis=1),
        jnp.concatenate([w_attn_out, w_mixer_out, w_down], axis=0),
    )
    seq_total = CTX * tok_rows
    pos_all = jnp.arange(seq_total, dtype=jnp.int32)
    seg_all = seg_got[:, 0].reshape(seq_total)
    visible = (pos_all[None, :] <= pos_here[:, None]) & (seg_all[None, :] == seg_here[:, None])
    hidden_mask = jnp.where(visible, 0.0, masked_score)

    rim_rows = CONV - 1
    rim_in = jnp.where(ctx_here > 0, rim_got[8 - rim_rows :], 0.0)
    extended = jnp.concatenate([rim_in, inner_pre], axis=0)
    rim_start = jnp.maximum(first_pos - rim_rows, 0)
    seg_rim = lax.dynamic_slice_in_dim(seg_all, rim_start, rim_rows)
    seg_ext = jnp.concatenate([seg_rim, seg_here])
    seg_prior = lax.dynamic_index_in_dim(seg_all, jnp.maximum(first_pos - 1, 0), keepdims=False)
    seg_before = jnp.where(ctx_here > 0, seg_prior, -1)
    values_ssm, input_map, output_map, step_size, log_decay = mixer_features(
        extended, seg_ext, seg_here, step_raw, conv_f, conv_bias_f, step_bias_f, decay_f
    )
    block_decay, block_state = ssd_states(
        values_ssm, input_map, step_size, log_decay, seg_here, seg_before
    )
    carried, decays, attended, log_total, all_two, all_three = scan_forward(
        block_state,
        block_decay,
        spread_heads(query_low.reshape(tok_rows, HEADS, HEAD_DIM)),
        kv_all,
        hidden_mask,
        all_two,
        all_three,
    )
    full_two = all_two.reshape(FSDP * 128, 2 * HALVES["two"])
    all_three = all_three.reshape(FSDP, OUT_ROWS, 2 * HALVES["three"])
    attn_out_full = all_three[:, 0:64].reshape(q_width, -1)
    mixer_out_full = all_three[:, 64:256].reshape(width_inner, -1)
    down_full = all_three[:, 256:512].reshape(FSDP * 256, -1)
    attn_low = join_heads(attended).reshape(tok_rows, q_width)
    attn_branch = matmul_f32(attn_low, attn_out_full) * attn_out_scale
    mixer_result, entering = ssd_output(
        values_ssm,
        input_map,
        output_map,
        step_size,
        log_decay,
        seg_here,
        seg_before,
        skip_f,
        carried,
    )
    mixer_low = gate_norm(mixer_result, gate_z, mixer_gain_f).astype(low)
    mixer_branch = matmul_f32(mixer_low, mixer_out_full) * mixer_out_scale
    middle = residual_in + attn_branch + mixer_branch
    normed_two_low = rms_scale(middle, gain_two_f).astype(low)
    both_pre = matmul_f32(normed_two_low, full_two)
    ff_width = FSDP * 256
    gate_pre = both_pre[:, :ff_width] * gate_scale
    up_pre = both_pre[:, ff_width : 2 * ff_width]
    hidden_low = (jax.nn.silu(gate_pre) * up_pre).astype(low)
    layer_out = middle + matmul_f32(hidden_low, down_full) * down_scale

    grad_down_in = (grad_final * down_scale).astype(low)
    grad_hidden = right_trans(grad_down_in, down_full)
    gate_sig = jax.nn.sigmoid(gate_pre)
    grad_gate_in = (
        grad_hidden * up_pre * gate_sig * (1.0 + gate_pre * (1.0 - gate_sig)) * gate_scale
    ).astype(low)
    grad_up_in = (grad_hidden * gate_pre * gate_sig).astype(low)
    grads_two = jnp.concatenate([grad_gate_in, grad_up_in], axis=1)
    grad_normed_two = right_trans(grads_two, full_two)
    _, pull_two = jax.vjp(rms_scale, middle, gain_two_f)
    grad_mid_norm, grad_gain_two = pull_two(grad_normed_two)
    grad_middle = grad_final + grad_mid_norm
    grad_mixer_in = (grad_middle * mixer_out_scale).astype(low)
    grad_mixer_normed = right_trans(grad_mixer_in, mixer_out_full)
    _, pull_gate = jax.vjp(gate_norm, mixer_result, gate_z, mixer_gain_f)
    grad_result, grad_gate_z, grad_mixer_gain = pull_gate(grad_mixer_normed)
    grad_weighted = grad_result * entering[:, :, None]
    grad_carried = jnp.einsum("thp,tn->phn", grad_weighted, output_map, precision=highest)
    grad_attn_in = (grad_middle * attn_out_scale).astype(low)
    grad_attended = right_trans(grad_attn_in, attn_out_full).astype(low)
    acts = jnp.concatenate(
        [
            attn_low.reshape(tok_rows, FSDP, 64),
            mixer_low.reshape(tok_rows, FSDP, 192),
            hidden_low.reshape(tok_rows, FSDP, 256),
        ],
        axis=2,
    ).transpose(1, 0, 2)
    grad_out_state, grad_query_h, grad_terms, sums_before = scan_backward(
        grad_carried,
        decays,
        spread_heads(query_low.reshape(tok_rows, HEADS, HEAD_DIM)),
        spread_heads(grad_attended.reshape(tok_rows, HEADS, HEAD_DIM)),
        kv_all,
        hidden_mask,
        log_total,
        normed_two_low,
        grads_two,
        acts,
        jnp.stack([grad_attn_in, grad_mixer_in, grad_down_in]),
    )
    grad_block_decay = jnp.sum(grad_out_state * carried, axis=(0, 2))

    def mixer_core(
        core_ext,
        core_step,
        core_conv,
        core_conv_bias,
        core_step_bias,
        core_decay,
        core_skip,
        core_carried,
    ):
        core_values, core_input, core_output, core_size, core_log = mixer_features(
            core_ext,
            seg_ext,
            seg_here,
            core_step,
            core_conv,
            core_conv_bias,
            core_step_bias,
            core_decay,
        )
        core_block_decay, core_block_state = ssd_states(
            core_values, core_input, core_size, core_log, seg_here, seg_before
        )
        core_result, _ = ssd_output(
            core_values,
            core_input,
            core_output,
            core_size,
            core_log,
            seg_here,
            seg_before,
            core_skip,
            core_carried,
        )
        return (core_result, core_block_decay, core_block_state)

    _, pull_core = jax.vjp(
        mixer_core, extended, step_raw, conv_f, conv_bias_f, step_bias_f, decay_f, skip_f, carried
    )
    grad_ext, grad_step_raw, grad_conv, grad_conv_bias, grad_step_bias, grad_decay, grad_skip, _ = (
        pull_core((grad_result, grad_block_decay, grad_out_state))
    )

    grad_kv, rim_back, unit_two, unit_three = sum_key_grads(grad_terms, grad_ext[:8], sums_before)
    grad_kv = grad_kv.T
    rim_back = jnp.where(ctx_here < CTX - 1, rim_back[:rim_rows], 0.0)
    grad_inner_pre = grad_ext[rim_rows:] + jnp.pad(rim_back, ((tok_rows - rim_rows, 0), (0, 0)))
    grad_key_rot = grad_kv[:, :kv_width].reshape(tok_rows, KV_HEADS, HEAD_DIM)
    grad_key_low = (
        (rotate_back(grad_key_rot, angle_cos, angle_sin) * key_scale)
        .reshape(tok_rows, kv_width)
        .astype(low)
    )
    grad_query = join_heads(grad_query_h)
    grad_query_low = (
        (rotate_back(grad_query, angle_cos, angle_sin) * HEAD_DIM ** (-0.5))
        .reshape(tok_rows, q_width)
        .astype(low)
    )
    grads_one = jnp.concatenate(
        [
            grad_query_low,
            grad_key_low,
            grad_kv[:, kv_width:].astype(low),
            grad_gate_z.astype(low),
            grad_inner_pre.astype(low),
            jnp.pad(grad_step_raw.astype(low), ((0, 0), (0, COLS - step_at - SSM_HEADS))),
        ],
        axis=1,
    )
    grad_normed_one = right_trans(grads_one, full_one)
    _, pull_one = jax.vjp(rms_scale, residual_in, gain_one_f)
    grad_in_norm, grad_gain_one = pull_one(grad_normed_one)
    input_grad = grad_middle + grad_in_norm

    small_grads = jnp.concatenate(
        [
            grad_gain_one.reshape(FSDP, 128),
            grad_conv.reshape(CONV, FSDP, 224).transpose(1, 0, 2).reshape(FSDP, CONV * 224),
            grad_conv_bias.reshape(FSDP, 224),
            grad_step_bias.reshape(FSDP, 3),
            grad_decay.reshape(FSDP, 3),
            grad_skip.reshape(FSDP, 3),
            grad_mixer_gain.reshape(FSDP, 192),
            grad_gain_two.reshape(FSDP, 128),
            jnp.zeros((FSDP, 2048 - SMALL), jnp.float32),
        ],
        axis=1,
    ).reshape(FSDP, 16, 128)
    sum_one, sum_two, sum_three = sum_weight_grads(
        normed_low, grads_one, small_grads, unit_two, unit_three
    )
    one = sum_one.reshape(128, COLS).astype(jnp.float32)
    two = sum_two.reshape(128, 2 * HALVES["two"]).astype(jnp.float32)
    three = sum_three.reshape(OUT_ROWS, 2 * HALVES["three"]).astype(jnp.float32)
    tiny = one[0:16, PAD_AT:COLS].reshape(-1)
    return (
        layer_out.astype(low)[None],
        input_grad[None],
        tiny[0:128],
        one[:, :q_width],
        one[:, q_width : q_width + kv_width],
        one[:, q_width + kv_width : z_at],
        three[0:64],
        one[:, z_at:inner_at],
        one[:, inner_at:step_at],
        one[:, step_at : step_at + SSM_HEADS],
        tiny[128:1024].reshape(CONV, 224),
        tiny[1024:1248],
        tiny[1248:1251],
        tiny[1251:1254],
        tiny[1254:1257],
        tiny[1257:1449],
        three[64:256],
        tiny[1449:1577],
        two[:, :ff_width],
        two[:, ff_width : 2 * ff_width],
        three[256:512],
    )


def solution(mesh):
    in_specs = (
        P("fsdp", "ctx", None),
        P("fsdp", "ctx"),
        P("fsdp"),
        P("fsdp", None),
        P("fsdp", None),
        P("fsdp", None),
        P("fsdp", None),
        P("fsdp", None),
        P("fsdp", None),
        P("fsdp", None),
        P(None, "fsdp"),
        P("fsdp"),
        P("fsdp"),
        P("fsdp"),
        P("fsdp"),
        P("fsdp"),
        P("fsdp", None),
        P("fsdp"),
        P("fsdp", None),
        P("fsdp", None),
        P("fsdp", None),
        P("fsdp", "ctx", None),
    )
    out_specs = (
        P("fsdp", "ctx", None),
        P("fsdp", "ctx", None),
        P("fsdp"),
        P("fsdp", None),
        P("fsdp", None),
        P("fsdp", None),
        P("fsdp", None),
        P("fsdp", None),
        P("fsdp", None),
        P("fsdp", None),
        P(None, "fsdp"),
        P("fsdp"),
        P("fsdp"),
        P("fsdp"),
        P("fsdp"),
        P("fsdp"),
        P("fsdp", None),
        P("fsdp"),
        P("fsdp", None),
        P("fsdp", None),
        P("fsdp", None),
    )
    return jax.shard_map(local, mesh=mesh, in_specs=in_specs, out_specs=out_specs, check_vma=False)
```

```python
import jax
import jax.numpy as jnp
from jax import lax
from jax.experimental import pallas as pl
from jax.experimental.pallas import tpu as pltpu
from jax.sharding import PartitionSpec as P

HEADS = 8
KV_HEADS = 2
HEAD_DIM = 64
SSM_HEADS = 24
SSM_DIM = 64
STATE = 128
CONV = 4


epsilon = 1e-05
rope_base = 10000.0
key_scale = 0.5
attn_out_scale = 0.8
mixer_out_scale = 0.5
gate_scale = 0.75
down_scale = 0.8
masked_score = -1e30
highest = lax.Precision.HIGHEST


def matmul_f32(left_side, right_side):
    return jnp.dot(left_side, right_side, preferred_element_type=jnp.float32)


def right_trans(left_side, right_side):
    return lax.dot_general(
        left_side, right_side, (((1,), (1,)), ((), ())), preferred_element_type=jnp.float32
    )


def rms_scale(values, gain_vec):
    return (
        values * lax.rsqrt(jnp.mean(values * values, axis=-1, keepdims=True) + epsilon) * gain_vec
    )


MESH = pl.DeviceIdType.MESH
CTX = 16
FSDP = 8
COLS = 4352
PAD_AT = 4224
HALVES = {"one": 2176, "two": 2048, "three": 512}
UNIT_ROWS = {"one": 16, "two": 16, "three": 64}
ORDERS = (("x", "y", "z"), ("y", "z", "x"), ("z", "x", "y"))
CUTS = {
    "one": (((0, 16), (0, 768)), ((0, 16), (768, 1536)), ((0, 16), (1536, 2176))),
    "two": (((0, 16), (0, 256)), ((0, 16), (256, 1152)), ((0, 16), (1152, 2048))),
    "three": (((0, 32), (0, 512)), ((32, 48), (0, 512)), ((48, 64), (0, 512))),
}
OUT_ROWS = 512
EVERYTHING = ("x", "y", "z")
SMALL = 1577
WIDTH = SSM_DIM * SSM_HEADS
HALF_WIDTH = WIDTH // 2
CONV_WIDTH = WIDTH + 2 * STATE
VMEM_LIMIT = 60 * 2**20


def place():
    f, c = lax.axis_index("fsdp"), lax.axis_index("ctx")
    return f, c, c // 4, (c // 2) % 2, c % 2


def at_ctx(y, low_z, core):
    return (y * 2 + low_z) * 2 + core


def meet(partners):
    barrier = pltpu.get_barrier_semaphore()
    for partner in partners:
        pl.semaphore_signal(barrier, inc=1, device_id=partner, device_id_type=MESH)
    pl.semaphore_wait(barrier, len(partners))


class Sender:
    def __init__(self, send_sem, recv_sem):
        self.send_sem, self.recv_sem, self.used, self.all = send_sem, recv_sem, 0, []

    def push(self, src, dst, partner):
        index = self.used
        self.used += 1
        copy = pltpu.make_async_remote_copy(
            src_ref=src,
            dst_ref=dst,
            send_sem=self.send_sem.at[index],
            recv_sem=self.recv_sem.at[index],
            device_id=partner,
            device_id_type=MESH,
        )
        copy.start()
        self.all.append(copy)
        return copy

    def drain(self):
        for copy in self.all:
            copy.wait_send()


def call_kernel(body, name, cid, outs, ins, sems, scratch=(), far_in=(), far_out=(), aliases=None):
    def spec(far):
        return pl.BlockSpec(memory_space=pl.ANY if far else pltpu.VMEM)

    return pl.pallas_call(
        body,
        name=name,
        out_shape=outs,
        in_specs=[spec(k in far_in) for k in range(len(ins))],
        out_specs=tuple(spec(k in far_out) for k in range(len(outs))),
        scratch_shapes=[
            *scratch,
            pltpu.SemaphoreType.DMA((sems,)),
            pltpu.SemaphoreType.DMA((sems,)),
        ],
        input_output_aliases=aliases or {},
        compiler_params=pltpu.CompilerParams(
            collective_id=cid, has_side_effects=True, vmem_limit_bytes=VMEM_LIMIT
        ),
    )(*ins)


def shape_of(dims, kind):
    return jax.ShapeDtypeStruct(dims, kind)


AXES = (("x", "x"), ("zh", "z"), ("y", "y"), ("zl", "z"))
EXTENT = {"x": 4, "zh": 2, "y": 4, "zl": 2}


def coordinates():
    f, c, y, low_z, core = place()
    return {"x": f // 2, "zh": f % 2, "y": y, "zl": low_z}, core


def neighbours(here, core):
    z = here["zh"] * 2 + here["zl"]
    found = {"x": [], "y": [], "z": []}
    for e in range(1, 4):
        found["x"].append({**here, "x": (here["x"] + e) % 4})
        found["y"].append({**here, "y": (here["y"] + e) % 4})
        other = (z + e) % 4
        found["z"].append({**here, "zh": other // 2, "zl": other % 2})
    return found


def device_of(at, core):
    return {"fsdp": at["x"] * 2 + at["zh"], "ctx": at_ctx(at["y"], at["zl"], core)}


def index_of(kept, fixed, at):
    return tuple(
        at[axis] if axis_dim in fixed else slice(None)
        for axis, axis_dim in AXES
        if axis_dim in kept
    )


def extents(kept):
    return tuple(EXTENT[axis] for axis, axis_dim in AXES if axis_dim in kept)


def span(pair):
    return pl.ds(pair[0], pair[1] - pair[0])


def cut_of(kind, part, core):
    rows, cols = CUTS[kind][part]
    at = pl.multiple_of(core * HALVES[kind] + cols[0], 128)
    return span(rows), pl.ds(at, cols[1] - cols[0])


def all_near(near, core):
    return [device_of(at, core) for dim in EVERYTHING for at in near[dim]]


class Gather:
    def __init__(self, net, outs, here, near, core):
        self.net, self.outs, self.here, self.near, self.core = net, outs, here, near, core
        self.pending, self.crossing = [[], [], []], []
        self.sibling = device_of(here, 1 - core)

    def pieces(self, part, fixed, at):
        index = index_of(EVERYTHING, fixed, at)
        return [
            ref.at[(*index, *cut_of(kind, part, self.core))] for kind, ref in self.outs.items()
        ]

    def own(self, ins, sem):
        point = index_of(EVERYTHING, EVERYTHING, self.here)
        copies = []
        for k, (kind, ref) in enumerate(self.outs.items()):
            half = HALVES[kind]
            cols = pl.ds(pl.multiple_of(self.core * half, 128), half)
            copies.append(
                pltpu.make_async_copy(
                    ins[kind].at[self.here["y"], self.here["zl"], :, cols],
                    ref.at[(*point, slice(None), cols)],
                    sem.at[k],
                )
            )
        return copies

    def stage(self, number, ins=None):
        for part, order in enumerate(ORDERS):
            steps = order[::-1]
            dim, fixed = steps[number], steps[number:]
            for copy in self.pending[part]:
                copy.wait_recv()
            refs = self.pieces(part, fixed, self.here)
            sources = refs
            if ins is not None:
                sources = [
                    ins[kind].at[
                        (self.here["y"], self.here["zl"], *cut_of(kind, part, self.core))
                    ]
                    for kind in self.outs
                ]
            self.pending[part] = [
                self.net.push(src, ref, device_of(at, self.core))
                for at in self.near[dim]
                for src, ref in zip(sources, refs)
            ]
            if number == 2:
                self.crossing += [self.net.push(ref, ref, self.sibling) for ref in refs]

    def settle(self):
        for part in range(3):
            for copy in self.pending[part]:
                copy.wait_recv()
        self.pending = [[], [], []]

    def finish(self):
        kinds = len(self.outs)
        for e in range(3):
            for part, order in enumerate(ORDERS):
                for copy in self.pending[part][kinds * e : kinds * e + kinds]:
                    copy.wait_recv()
                source = self.near[order[0]][2 - e]
                self.crossing += [
                    self.net.push(ref, ref, self.sibling)
                    for ref in self.pieces(part, (order[0],), source)
                ]
        for copy in self.crossing:
            copy.wait_recv()


def gather_shapes(kinds):
    return [
        shape_of((4, 2, 4, 2, UNIT_ROWS[kind], 2 * HALVES[kind]), jnp.bfloat16) for kind in kinds
    ]


def gather_body(in_one, small, seg, out_one, table, seg_all, got_small, own_sem, send_sem, recv_sem):
    here, core = coordinates()
    near = neighbours(here, core)
    f = here["x"] * 2 + here["zh"]
    c = at_ctx(here["y"], here["zl"], core)
    small_peers = [{"fsdp": (f + d) % FSDP} for d in range(1, FSDP)]
    meet(
        all_near(near, core)
        + [{"fsdp": (here["x"] + e) % 4 * 2 + 1 - here["zh"]} for e in range(1, 4)]
        + ctx_peers(c)
    )
    net = Sender(send_sem, recv_sem)
    gather = Gather(net, {"one": out_one}, here, near, core)
    gather.stage(0, {"one": in_one})
    own = gather.own({"one": in_one}, own_sem)
    for copy in own:
        copy.start()
    tiny = [net.push(small, got_small.at[f], peer) for peer in small_peers]
    got_small[f] = small[...]
    tiny += [net.push(seg, seg_all.at[c], peer) for peer in ctx_peers(c)]
    seg_all[c] = seg[...]
    for copy in own:
        copy.wait()
    gather.stage(1)
    gather.stage(2)
    for copy in tiny:
        copy.wait_recv()
    table[...] = jnp.zeros_like(table)
    for k in range(FSDP):
        piece = got_small[k].astype(jnp.float32)
        for first, last, width in TABLE:
            table[first:last, k * width : k * width + width] = piece[first:last, :width]
    table[9:10] = jnp.exp(table[9:10])
    table[11:12, :WIDTH] = expand(table[10:11, 0:128])
    gather.finish()
    net.drain()


TABLE = ((0, 5, 224), (5, 6, 192), (6, 8, 128), (8, 11, 3))


def gather_weights(in_one, small, seg):
    return call_kernel(
        gather_body,
        "gather_weights",
        0,
        (
            *gather_shapes(["one"]),
            shape_of((16, CONV_WIDTH), jnp.float32),
            shape_of((CTX, *seg.shape), seg.dtype),
        ),
        (in_one.reshape(4, 2, 16, COLS), small, seg),
        61,
        (pltpu.VMEM((FSDP, 16, 256), jnp.bfloat16), pltpu.SemaphoreType.DMA((2,))),
        (0,),
        (0,),
    )


def ctx_peers(c):
    return [{"ctx": (c + e) % CTX} for e in range(1, CTX)]


def expand(per_head):
    rows = per_head.shape[0]
    lane = lax.broadcasted_iota(jnp.int32, (rows, 128), 1)
    return jnp.concatenate(
        [
            jnp.where(
                lane < SSM_DIM,
                jnp.broadcast_to(per_head[:, 2 * j : 2 * j + 1], (rows, 128)),
                jnp.broadcast_to(per_head[:, 2 * j + 1 : 2 * j + 2], (rows, 128)),
            )
            for j in range(SSM_HEADS // 2)
        ],
        axis=1,
    )


def pack(states, chunks):
    for k in range(CTX):
        rows = states[8 * k : 8 * k + 8]
        chunks[k] = jnp.concatenate([rows[:, :HALF_WIDTH], rows[:, HALF_WIDTH:]], axis=0).astype(
            jnp.bfloat16
        )


def unpack(chunks, states):
    for k in range(CTX):
        rows = chunks[k].astype(jnp.float32)
        states[8 * k : 8 * k + 8] = jnp.concatenate([rows[:8], rows[8:]], axis=1)


def scan_rows(order, decay_of, parts, carries):
    wide = expand(jnp.concatenate([decay_of[k, 0:1] for k in range(CTX)], axis=0))
    state = jnp.zeros((16, HALF_WIDTH), jnp.float32)
    for at in order:
        carries[at] = state.astype(jnp.bfloat16)
        decay = jnp.concatenate(
            [
                jnp.broadcast_to(wide[at : at + 1, :HALF_WIDTH], (8, HALF_WIDTH)),
                jnp.broadcast_to(wide[at : at + 1, HALF_WIDTH:], (8, HALF_WIDTH)),
            ],
            axis=0,
        )
        state = decay * state + parts[at].astype(jnp.float32)


def send_back(net, c, peers, carries, carried):
    copies = [
        net.push(carries.at[(c + e + 1) % CTX], carried.at[c], peer) for e, peer in enumerate(peers)
    ]
    carried[c] = carries[c]
    return copies


def across(left, right):
    return lax.dot_general(
        left, right, (((1,), (1,)), ((), ())), preferred_element_type=jnp.float32
    )


def down(left, right):
    return lax.dot_general(
        left, right, (((0,), (0,)), ((), ())), preferred_element_type=jnp.float32
    )


def forward_body(
    query,
    kv,
    hidden_mask,
    inner,
    steps,
    masks,
    intra,
    table,
    in_two,
    in_three,
    kv_all,
    rim_all,
    mixed,
    cumulative,
    sizes,
    entering,
    carried,
    result,
    decays,
    attended,
    log_total,
    out_two,
    out_three,
    states,
    inside,
    extended,
    wide_states,
    parts,
    carries,
    came_back,
    decay,
    own_sem,
    send_sem,
    recv_sem,
):
    here, core = coordinates()
    near = neighbours(here, core)
    c = at_ctx(here["y"], here["zl"], core)
    peers = ctx_peers(c)
    rows = kv_all.shape[1]
    meet(peers + all_near(near, core))
    net = Sender(send_sem, recv_sem)
    rim_copy = net.push(inner.at[pl.ds(rows - 8, 8)], rim_all, peers[0])
    key_copies = [net.push(kv, kv_all.at[c], peer) for peer in peers]
    ins = {"two": in_two, "three": in_three}
    gather = Gather(net, {"two": out_two, "three": out_three}, here, near, core)
    gather.stage(0, ins)
    own = gather.own(ins, own_sem)
    for copy in own:
        copy.start()
    kv_all[c] = kv[...]
    for copy in own:
        copy.wait()
    gather.stage(1)
    rim_copy.wait_recv()
    mixer_parts_body(
        inner,
        rim_all,
        steps,
        masks,
        intra,
        table,
        mixed,
        cumulative,
        sizes,
        states,
        decay,
        entering,
        inside,
        extended,
        wide_states,
    )
    copies = []
    for e, peer in enumerate(peers):
        copies.append(net.push(states.at[(c + e + 1) % CTX], parts.at[c], peer))
        copies.append(net.push(decay, decays.at[c], peer))
    parts[c] = states[c]
    decays[c] = decay[...]
    gather.stage(2)
    for copy in key_copies:
        copy.wait_recv()

    def head(h, nothing):
        keys = kv_all[:, :, 0:128].reshape(CTX * rows, 128)
        values = kv_all[:, :, 128:256].reshape(CTX * rows, 128)
        scores = across(query[h], keys) + hidden_mask[...]
        row_max = jnp.max(scores, axis=-1, keepdims=True)
        weights = jnp.exp(scores - row_max)
        row_sum = jnp.sum(weights, axis=-1, keepdims=True)
        probs = (weights * (1.0 / row_sum)).astype(jnp.bfloat16)
        attended[h] = jnp.dot(probs, values, preferred_element_type=jnp.float32).astype(
            jnp.bfloat16
        )
        log_total[h] = jnp.broadcast_to(row_max + jnp.log(row_sum), (rows, 128))
        return nothing

    lax.fori_loop(0, 3, head, 0)
    for copy in copies:
        copy.wait_recv()
    scan_rows(range(CTX), decays, parts, carries)
    back = send_back(net, c, peers, carries, came_back)
    lax.fori_loop(3, HEADS, head, 0)
    for copy in back:
        copy.wait_recv()
    unpack(came_back, carried)
    output_map = mixed[:, WIDTH + STATE :].astype(jnp.bfloat16)
    result[...] = inside[...] + expand(entering[...]) * jnp.dot(
        output_map, carried[...].astype(jnp.bfloat16), preferred_element_type=jnp.float32
    )
    gather.finish()
    net.drain()


def forward(query, kv, hidden_mask, inner, steps, masks, intra, table, two, three):
    rows = query.shape[1]
    f32, low = jnp.float32, jnp.bfloat16
    return call_kernel(
        forward_body,
        "forward",
        1,
        (
            shape_of((CTX, *kv.shape), kv.dtype),
            shape_of((8, CONV_WIDTH), f32),
            shape_of((rows, CONV_WIDTH), f32),
            shape_of((rows, 128), f32),
            shape_of((rows, 128), f32),
            shape_of((rows, 128), f32),
            shape_of((STATE, WIDTH), f32),
            shape_of((rows, WIDTH), f32),
            shape_of((CTX, 8, 128), f32),
            shape_of((HEADS, rows, 128), low),
            shape_of((HEADS, rows, 128), f32),
            *gather_shapes(["two", "three"]),
        ),
        (
            query,
            kv,
            hidden_mask,
            inner,
            steps,
            masks,
            intra,
            table,
            two.reshape(4, 2, 16, 2 * HALVES["two"]),
            three.reshape(4, 2, 64, 2 * HALVES["three"]),
        ),
        139,
        (
            pltpu.VMEM((CTX, 16, HALF_WIDTH), low),
            pltpu.VMEM((rows, WIDTH), f32),
            pltpu.VMEM((rows + 8, CONV_WIDTH), f32),
            pltpu.VMEM((STATE, WIDTH), f32),
            *[pltpu.VMEM((CTX, 16, HALF_WIDTH), low)] * 3,
            pltpu.VMEM((8, 128), f32),
            pltpu.SemaphoreType.DMA((2,)),
        ),
        (8, 9),
        (11, 12),
    )


def plain_kernel(body, name, outs, ins, scratch=()):
    return pl.pallas_call(
        body,
        name=name,
        out_shape=outs,
        in_specs=[pl.BlockSpec(memory_space=pltpu.VMEM)] * len(ins),
        out_specs=tuple(pl.BlockSpec(memory_space=pltpu.VMEM) for _ in outs),
        scratch_shapes=list(scratch),
        compiler_params=pltpu.CompilerParams(vmem_limit_bytes=VMEM_LIMIT),
    )(*ins)


TAP_ROWS = 8 - CONV + 1


def conv_sum(extended, masks, conv_par, at):
    rows = masks.shape[0]
    total = jnp.broadcast_to(conv_par[CONV : CONV + 1, at], (rows, conv_par[0:1, at].shape[1]))
    for tap in range(CONV):
        first = TAP_ROWS + tap
        term = conv_par[tap : tap + 1, at] * extended[first : first + rows, at]
        total = total + (term * masks[:, tap : tap + 1] if tap < CONV - 1 else term)
    return total


def lower_ones(rows):
    at = lax.broadcasted_iota(jnp.int32, (rows, rows), 0)
    return (at >= lax.broadcasted_iota(jnp.int32, (rows, rows), 1)).astype(jnp.float32)


def exact(left, right, contract):
    return lax.dot_general(
        left,
        right,
        ((contract[0], contract[1]), ((), ())),
        precision=highest,
        preferred_element_type=jnp.float32,
    )


def swap_quarters(values):
    lane = lax.broadcasted_iota(jnp.int32, values.shape, 1)
    quarter = HEAD_DIM // 2
    ahead = jnp.concatenate([values[:, quarter:], values[:, :quarter]], axis=1)
    behind = jnp.concatenate([values[:, 128 - quarter :], values[:, : 128 - quarter]], axis=1)
    return jnp.where(lane % HEAD_DIM < quarter, ahead, behind)


def split_pair(both, j, out):
    lane = lax.broadcasted_iota(jnp.int32, both.shape, 1)
    turned = shift_half(both)
    low = jnp.bfloat16
    if j < HEADS // 4:
        out[2 * j] = jnp.where(lane < HEAD_DIM, both, 0.0).astype(low)
        out[2 * j + 1] = jnp.where(lane < HEAD_DIM, turned, 0.0).astype(low)
    else:
        out[2 * j] = jnp.where(lane < HEAD_DIM, 0.0, turned).astype(low)
        out[2 * j + 1] = jnp.where(lane < HEAD_DIM, 0.0, both).astype(low)


def join_pair(values, j):
    first, second = values[2 * j].astype(jnp.float32), values[2 * j + 1].astype(jnp.float32)
    if j < HEADS // 4:
        second = shift_half(second)
    else:
        first = shift_half(first)
    lane = lax.broadcasted_iota(jnp.int32, first.shape, 1)
    return jnp.where(lane < HEAD_DIM, first, second)


Z_AT = HEADS * HEAD_DIM + 2 * KV_HEADS * HEAD_DIM
INNER_AT = Z_AT + WIDTH
STEP_AT = INNER_AT + CONV_WIDTH


def project_body(row_in, table, cosine, sine, weights, norm_low, query, kv, gate_z, inner, steps):
    values = row_in[...]
    scale = lax.rsqrt(mean_last(values * values) + epsilon)
    normed = (values * scale * table[7:8, 0 : values.shape[1]]).astype(jnp.bfloat16)
    norm_low[...] = normed

    def part(first, last):
        return jnp.dot(normed, weights[:, first:last], preferred_element_type=jnp.float32)

    def turn(both):
        return both * cosine[...] + swap_quarters(both) * sine[...]

    for j in range(HEADS // 2):
        split_pair(turn(part(128 * j, 128 * j + 128)) * HEAD_DIM ** (-0.5), j, query)
    key_at = HEADS * HEAD_DIM
    kv[:, 0:128] = (turn(part(key_at, key_at + 128)) * key_scale).astype(jnp.bfloat16)
    kv[:, 128:256] = part(key_at + 128, key_at + 256).astype(jnp.bfloat16)
    for at in range(0, WIDTH, 512):
        gate_z[:, at : at + 512] = part(Z_AT + at, Z_AT + at + 512)
    for at in range(0, CONV_WIDTH, 256):
        inner[:, at : at + 256] = part(INNER_AT + at, INNER_AT + at + 256)
    steps[...] = part(STEP_AT, STEP_AT + 128)


def project(row_in, table, cosine, sine, weights):
    rows, dim = row_in.shape
    f32, low = jnp.float32, jnp.bfloat16
    return plain_kernel(
        project_body,
        "project",
        (
            shape_of((rows, dim), low),
            shape_of((HEADS, rows, 128), low),
            shape_of((rows, 256), low),
            shape_of((rows, WIDTH), f32),
            shape_of((rows, CONV_WIDTH), f32),
            shape_of((rows, 128), f32),
        ),
        (row_in, table, cosine, sine, weights),
    )


def mixer_parts_body(
    inner,
    rim,
    steps,
    masks,
    intra,
    table,
    mixed,
    cumulative,
    sizes,
    chunks,
    decay,
    entering,
    inside,
    extended,
    states,
):
    rows = inner.shape[0]
    low = jnp.bfloat16
    extended[0:8] = rim[...]
    extended[8:] = inner[...]
    for piece in range(CONV_WIDTH // 256):
        at = slice(piece * 256, piece * 256 + 256)
        total = conv_sum(extended, masks, table, at)
        mixed[:, at] = total / (1.0 + jnp.exp(-total))
    raw = steps[...] + table[8:9, 0:128]
    size = jnp.maximum(raw, 0.0) + jnp.log1p(jnp.exp(-jnp.abs(raw)))
    sums = exact(lower_ones(rows), -size * table[9:10, 0:128], ((1,), (0,)))
    cumulative[...] = sums
    sizes[...] = size
    last = sums[rows - 1 : rows]
    entering[...] = jnp.exp(sums) * masks[:, 3:4]
    decay[...] = jnp.broadcast_to(jnp.exp(last) * masks[0:1, 5:6], (8, 128))
    tail = masks[:, 4:5] * jnp.exp(last - sums) * size
    weighted = (expand(tail) * mixed[:, :WIDTH]).astype(low)
    input_map = mixed[:, WIDTH : WIDTH + STATE]
    output_map = mixed[:, WIDTH + STATE :]
    states[...] = down(input_map.astype(low), weighted)
    pack(states, chunks)
    pairing = exact(output_map, input_map, ((1,), (1,))) * intra[...]
    sums_t, size_t = sums.T, size.T
    lane = lax.broadcasted_iota(jnp.int32, (rows, 128), 1)
    for j in range(SSM_HEADS // 2):
        at = slice(128 * j, 128 * j + 128)
        values = mixed[:, at]
        found = []
        for h in (2 * j, 2 * j + 1):
            spread = jnp.minimum(sums[:, h : h + 1] - sums_t[h : h + 1], 0.0)
            mixing = (jnp.exp(spread) * pairing * size_t[h : h + 1]).astype(low)
            found.append(jnp.dot(mixing, values.astype(low), preferred_element_type=jnp.float32))
        inside[:, at] = jnp.where(lane < SSM_DIM, found[0], found[1]) + table[11:12, at] * values


def mean_last(values):
    return jnp.mean(values, axis=-1, keepdims=True)


def pair_of(weights, j, first, last):
    return jnp.concatenate([weights[2 * j, first:last], weights[2 * j + 1, first:last]], axis=0)


def shift_half(values):
    return jnp.concatenate([values[:, HEAD_DIM:], values[:, :HEAD_DIM]], axis=1)


def middle_body(
    row_in,
    row_grad,
    attended,
    result,
    gate_z,
    table,
    w_two,
    w_three,
    row_out,
    grad_middle,
    attn_low,
    mixer_low,
    hidden_low,
    norm_low,
    grads_two,
    grads_three,
    grad_out,
    grad_result,
    grad_z,
    grad_ffn_gain,
    grad_mixer_gain,
    down_sum,
    norm_sum,
    grad_flat,
):
    low, f32 = jnp.bfloat16, jnp.float32
    attn_sum = jnp.zeros(row_in.shape, f32)
    for j in range(HEADS // 2):
        both = join_pair(attended, j).astype(low)
        attn_low[:, 128 * j : 128 * j + 128] = both
        attn_sum = attn_sum + jnp.dot(
            both, pair_of(w_three, j, 0, 64), preferred_element_type=f32
        )
    z, mixed_out = gate_z[...], result[...]
    sig_z = 1.0 / (1.0 + jnp.exp(-z))
    flat = mixed_out * (z * sig_z)
    scale = lax.rsqrt(mean_last(flat * flat) + epsilon)
    normed = (flat * scale * table[5:6, 0:WIDTH]).astype(low)
    mixer_low[...] = normed
    mixer_sum = jnp.zeros(row_in.shape, f32)
    for j in range(4):
        mixer_sum = mixer_sum + jnp.dot(
            normed[:, 384 * j : 384 * j + 384],
            pair_of(w_three, j, 64, 256),
            preferred_element_type=f32,
        )
    middle = row_in[...] + attn_sum * attn_out_scale + mixer_sum * mixer_out_scale
    scale_two = lax.rsqrt(mean_last(middle * middle) + epsilon)
    norm_low[...] = (middle * scale_two * table[6:7, 0 : row_in.shape[1]]).astype(low)
    grad_down = (row_grad[...] * down_scale).astype(low)
    grads_three[2] = grad_down
    down_sum[...] = jnp.zeros_like(down_sum)
    norm_sum[...] = jnp.zeros_like(norm_sum)
    ff_width = FSDP * 256

    def chunk(f, nothing):
        at = pl.ds(pl.multiple_of(f * 256, 256), 256)
        at_up = pl.ds(pl.multiple_of(ff_width + f * 256, 256), 256)
        w_gate, w_up, w_down = w_two[:, at], w_two[:, at_up], w_three[f, 256:512]
        gate = jnp.dot(norm_low[...], w_gate, preferred_element_type=f32) * gate_scale
        up = jnp.dot(norm_low[...], w_up, preferred_element_type=f32)
        sig = 1.0 / (1.0 + jnp.exp(-gate))
        hidden = (gate * sig * up).astype(low)
        hidden_low[:, at] = hidden
        down_sum[...] += jnp.dot(hidden, w_down, preferred_element_type=f32)
        grad_hidden = across(grad_down, w_down)
        grad_gate = (
            grad_hidden * up * sig * (1.0 + gate * (1.0 - sig)) * gate_scale
        ).astype(low)
        grad_up = (grad_hidden * gate * sig).astype(low)
        grads_two[:, at] = grad_gate
        grads_two[:, at_up] = grad_up
        norm_sum[...] += across(grad_gate, w_gate) + across(grad_up, w_up)
        return nothing

    lax.fori_loop(0, FSDP, chunk, 0)
    row_out[...] = (middle + down_sum[...] * down_scale).astype(low)
    grad_norm = norm_sum[...]
    weighted = grad_norm * table[6:7, 0 : row_in.shape[1]]
    grad_mid = (
        row_grad[...]
        + scale_two * weighted
        - middle * (scale_two * scale_two * scale_two) * mean_last(middle * weighted)
    )
    grad_middle[...] = grad_mid
    grad_ffn_gain[...] = jnp.broadcast_to(
        jnp.sum(grad_norm * middle * scale_two, axis=0, keepdims=True), grad_ffn_gain.shape
    )
    grad_attn = (grad_mid * attn_out_scale).astype(low)
    grad_mix = (grad_mid * mixer_out_scale).astype(low)
    grads_three[0] = grad_attn
    grads_three[1] = grad_mix
    for j in range(HEADS // 2):
        split_pair(across(grad_attn, pair_of(w_three, j, 0, 64)), j, grad_out)
    for j in range(4):
        grad_flat[:, 384 * j : 384 * j + 384] = across(grad_mix, pair_of(w_three, j, 64, 256))
    grad_normed = grad_flat[...]
    weighted = grad_normed * table[5:6, 0:WIDTH]
    grad_mixer_gain[...] = jnp.broadcast_to(
        jnp.sum(grad_normed * flat * scale, axis=0, keepdims=True), grad_mixer_gain.shape
    )
    grad_gated = scale * weighted - flat * (scale * scale * scale) * mean_last(flat * weighted)
    grad_result[...] = grad_gated * (z * sig_z)
    grad_z[...] = (grad_gated * mixed_out * sig_z * (1.0 + z * (1.0 - sig_z))).astype(low)


def middle_part(row_in, row_grad, attended, result, gate_z, table, w_two, w_three):
    rows, dim = row_in.shape
    f32, low = jnp.float32, jnp.bfloat16
    return plain_kernel(
        middle_body,
        "middle_part",
        (
            shape_of((rows, dim), low),
            shape_of((rows, dim), f32),
            shape_of((rows, HEADS * HEAD_DIM), low),
            shape_of((rows, WIDTH), low),
            shape_of((rows, FSDP * 256), low),
            shape_of((rows, dim), low),
            shape_of((rows, 2 * FSDP * 256), low),
            shape_of((3, rows, dim), low),
            shape_of((HEADS, rows, 128), low),
            shape_of((rows, WIDTH), f32),
            shape_of((rows, WIDTH), low),
            shape_of((8, dim), f32),
            shape_of((8, WIDTH), f32),
        ),
        (row_in, row_grad, attended, result, gate_z, table, w_two, w_three),
        (
            pltpu.VMEM((rows, dim), f32),
            pltpu.VMEM((rows, dim), f32),
            pltpu.VMEM((rows, WIDTH), f32),
        ),
    )


def mixer_grads_body(
    grad,
    leaving,
    carried,
    mixed,
    cumulative,
    sizes,
    entering,
    inner,
    rim,
    steps,
    masks,
    intra,
    table,
    grad_inner,
    grad_rim,
    grad_steps,
    grad_conv,
    grad_heads,
    extended,
    grad_ext,
    grad_mixed,
):
    rows = inner.shape[0]
    low = jnp.bfloat16
    sums, size = cumulative[...], sizes[...]
    last = sums[rows - 1 : rows]
    input_map = mixed[:, WIDTH : WIDTH + STATE]
    output_map = mixed[:, WIDTH + STATE :]
    gather_head = (
        lax.broadcasted_iota(jnp.int32, (WIDTH, 128), 0) // SSM_DIM
        == lax.broadcasted_iota(jnp.int32, (WIDTH, 128), 1)
    ).astype(jnp.float32)

    def per_head(wide):
        return exact(wide, gather_head, ((1,), (0,)))

    tail_decay = masks[:, 4:5] * jnp.exp(last - sums)
    tail = tail_decay * size
    leaving_low, carried_low = leaving[...].astype(low), carried[...].astype(low)
    from_state = jnp.dot(input_map.astype(low), leaving_low, preferred_element_type=jnp.float32)
    to_output = jnp.dot(output_map.astype(low), carried_low, preferred_element_type=jnp.float32)
    wide_tail = expand(tail)
    values_all, grad_all = mixed[:, :WIDTH], grad[...]
    grad_tail = per_head(values_all * from_state)
    grad_entering = per_head(grad_all * to_output)
    grad_skip = per_head(jnp.sum(grad_all * values_all, axis=0, keepdims=True))
    grad_block = per_head(jnp.sum(leaving[...] * carried[...], axis=0, keepdims=True))
    grad_input = across((wide_tail * values_all).astype(low), leaving_low)
    grad_output = across((expand(entering[...]) * grad_all).astype(low), carried_low)
    grad_mixed[:, :WIDTH] = wide_tail * from_state + table[11:12, 0:WIDTH] * grad_all

    pairing = exact(output_map, input_map, ((1,), (1,)))
    sums_t, size_t = sums.T, size.T
    lane = lax.broadcasted_iota(jnp.int32, (rows, 128), 1)
    grad_pairing = jnp.zeros((rows, rows), jnp.float32)
    row_sums = jnp.zeros((rows, 128), jnp.float32)
    size_rows = []
    for j in range(SSM_HEADS // 2):
        at = slice(128 * j, 128 * j + 128)
        values, grads = mixed[:, at].astype(low), grad[:, at]
        found = []
        for h in (2 * j, 2 * j + 1):
            own_lanes = lane < SSM_DIM if h == 2 * j else lane >= SSM_DIM
            spread = jnp.minimum(sums[:, h : h + 1] - sums_t[h : h + 1], 0.0)
            decays = jnp.exp(spread) * intra[...]
            inner_part = decays * pairing
            mixing = inner_part * size_t[h : h + 1]
            found.append(down(mixing.astype(low), grads.astype(low)))
            grad_mixing = across(jnp.where(own_lanes, grads, 0.0).astype(low), values)
            grad_pairing = grad_pairing + grad_mixing * decays * size_t[h : h + 1]
            by_size = grad_mixing * inner_part
            size_rows.append(jnp.sum(by_size, axis=0, keepdims=True))
            row_sum = jnp.sum(by_size * size_t[h : h + 1], axis=1, keepdims=True)
            row_sums = jnp.where(lane == h, row_sum, row_sums)
        grad_mixed[:, at] += jnp.where(lane < SSM_DIM, found[0], found[1])
    size_rows.append(jnp.zeros((128 - SSM_HEADS, rows), jnp.float32))
    grad_size = jnp.concatenate(size_rows, axis=0).T
    grad_sums = row_sums - size * grad_size
    grad_size = grad_size + grad_tail * tail_decay
    by_tail = grad_tail * tail
    grad_sums = grad_sums - by_tail + grad_entering * entering[...]
    grad_last = jnp.sum(by_tail, axis=0, keepdims=True) + grad_block * (
        jnp.exp(last) * masks[0:1, 5:6]
    )
    row = lax.broadcasted_iota(jnp.int32, (rows, 128), 0)
    grad_sums = grad_sums + jnp.where(row == rows - 1, grad_last, 0.0)
    grad_log = exact(lower_ones(rows), grad_sums, ((0,), (0,)))
    rate = table[9:10, 0:128]
    grad_size = grad_size - rate * grad_log
    raw = steps[...] + table[8:9, 0:128]
    grad_raw = grad_size / (1.0 + jnp.exp(-raw))
    grad_steps[...] = grad_raw
    grad_heads[...] = jnp.concatenate(
        [
            jnp.sum(grad_raw, axis=0, keepdims=True),
            jnp.sum(-grad_log * size * rate, axis=0, keepdims=True),
            grad_skip,
            jnp.zeros((5, 128), jnp.float32),
        ],
        axis=0,
    )
    grad_pairing = grad_pairing.astype(low)
    grad_mixed[:, WIDTH : WIDTH + STATE] = grad_input + down(grad_pairing, output_map.astype(low))
    grad_mixed[:, WIDTH + STATE :] = grad_output + jnp.dot(
        grad_pairing, input_map.astype(low), preferred_element_type=jnp.float32
    )

    extended[0:8] = rim[...]
    extended[8:] = inner[...]
    grad_ext[...] = jnp.zeros_like(grad_ext)
    for piece in range(CONV_WIDTH // 256):
        at = slice(piece * 256, piece * 256 + 256)
        total = conv_sum(extended, masks, table, at)
        sig = 1.0 / (1.0 + jnp.exp(-total))
        grad_total = grad_mixed[:, at] * sig * (1.0 + total * (1.0 - sig))
        taps = []
        for tap in range(CONV):
            first = TAP_ROWS + tap
            kept = grad_total * masks[:, tap : tap + 1] if tap < CONV - 1 else grad_total
            taps.append(jnp.sum(kept * extended[first : first + rows, at], axis=0, keepdims=True))
            grad_ext[first : first + rows, at] += table[tap : tap + 1, at] * kept
        taps.append(jnp.sum(grad_total, axis=0, keepdims=True))
        taps.append(jnp.zeros((8 - CONV - 1, 256), jnp.float32))
        grad_conv[:, at] = jnp.concatenate(taps, axis=0)
    grad_rim[...] = grad_ext[0:8]
    grad_inner[...] = grad_ext[8:]


def dot_rows(left, right):
    return down(left, right).astype(jnp.bfloat16)


class Sums:
    def __init__(self, net, kinds, here, near, core, came, summed, own=None):
        self.net, self.kinds, self.here, self.near, self.core = net, kinds, here, near, core
        self.came, self.summed, self.own = came, summed, own
        self.pending = [None, None, None]

    def refs(self, part, stage, fixed, at):
        index = index_of(ORDERS[part][stage:], fixed, at)
        if stage:
            return [ref.at[index] for ref in self.summed[part, stage - 1]]
        return [
            ref.at[(*index, *(span(pair) for pair in CUTS[kind][part]))]
            for kind, ref in zip(self.kinds, self.own)
        ]

    def early(self, e, send_sem, recv_sem):
        at = {**self.here, "x": (self.here["x"] + e + 1) % 4}
        return [
            pltpu.make_async_remote_copy(
                src_ref=src,
                dst_ref=dst.at[e],
                send_sem=send_sem.at[len(self.kinds) * e + k],
                recv_sem=recv_sem.at[len(self.kinds) * e + k],
                device_id=device_of(at, self.core),
                device_id_type=MESH,
            )
            for k, (src, dst) in enumerate(
                zip(self.refs(0, 0, ("x",), at), self.came[0, 0])
            )
        ]

    def send(self, part, stage):
        dim = ORDERS[part][stage]
        self.pending[part] = [
            self.net.push(src, dst.at[e], device_of(at, self.core))
            for e, at in enumerate(self.near[dim])
            for src, dst in zip(self.refs(part, stage, (dim,), at), self.came[part, stage])
        ]

    def wait(self, part):
        for copy in self.pending[part] or ():
            copy.wait_recv()

    def add_up(self, part, stage):
        kept, rest = ORDERS[part][stage:], ORDERS[part][stage + 1 :]

        def unit(number, nothing):
            at, left = dict(self.here), number
            for axis, axis_dim in reversed(AXES):
                if axis_dim in rest:
                    at[axis] = left % EXTENT[axis]
                    left = left // EXTENT[axis]
            inner = index_of(rest, rest, at)
            own_refs = self.refs(part, stage, kept, at)
            for own, came, out in zip(
                own_refs, self.came[part, stage], self.summed[part, stage]
            ):
                total = own[...].astype(jnp.float32)
                for e in range(3):
                    total = total + came[(e, *inner)].astype(jnp.float32)
                out[inner if inner else Ellipsis] = total.astype(jnp.bfloat16)
            return nothing

        count = 1
        for size in extents(rest):
            count *= size
        if count == 1:
            unit(0, 0)
        else:
            lax.fori_loop(0, count, unit, 0)


def piece_shapes(kinds, part):
    return [
        tuple(pair[1] - pair[0] for pair in CUTS[kind][part]) for kind in kinds
    ]


def came_shapes(kinds, part, stage):
    rest = extents(ORDERS[part][stage + 1 :])
    return [(3, *rest, *shape) for shape in piece_shapes(kinds, part)]


def summed_shapes(kinds, part, stage):
    rest = extents(ORDERS[part][stage + 1 :])
    return [(*rest, *shape) for shape in piece_shapes(kinds, part)]


def stage_keys(stages):
    return [(part, stage) for part in range(3) for stage in stages]


def take(refs, keys, kinds):
    found = {}
    for key in keys:
        found[key], refs = refs[: len(kinds)], refs[len(kinds) :]
    return found, refs


def low_scratch(shapes):
    return [pltpu.VMEM(dims, jnp.bfloat16) for dims in shapes]


def half_of(core, kind):
    return pl.ds(pl.multiple_of(core * HALVES[kind], 128), HALVES[kind])


LATE = ("two", "three")


def backward_body(
    grad,
    mixed,
    entering,
    decays,
    query,
    grad_out,
    kv_all,
    hidden_mask,
    log_total,
    norm,
    grads_two,
    acts_attn,
    acts_mixer,
    acts_hidden,
    grads_three,
    carried,
    cumulative,
    sizes,
    inner,
    rim,
    steps,
    masks,
    intra,
    table,
    cosine,
    sine,
    grad_z,
    grads_one,
    grad_conv,
    grad_heads,
    out_two,
    out_three,
    *rest,
):
    came, rest = take(rest, stage_keys(range(3)), LATE)
    summed, rest = take(rest, stage_keys(range(3)), LATE)
    states, parts, carries, came_back, terms, term_parts = rest[:6]
    both_norm, both_two, both_act, both_three, own_two, own_three = rest[6:12]
    key_sum, value_sum, wide_states, leaving, grad_query, grad_inner, grad_rim, rim_back = rest[12:20]
    extended, grad_ext, grad_mixed, grad_steps, send_sem, recv_sem = rest[20:]
    here, core = coordinates()
    near = neighbours(here, core)
    c = at_ctx(here["y"], here["zl"], core)
    peers = ctx_peers(c)
    meet(peers + all_near(near, core))
    net = Sender(send_sem.at[pl.ds(6, 100)], recv_sem.at[pl.ds(6, 100)])
    sibling = device_of(here, 1 - core)
    toks = norm.shape[0]
    mine, theirs = pl.ds(0, toks), pl.ds(toks, toks)
    other = 1 - core
    first = [
        net.push(norm, both_norm.at[theirs], sibling),
        net.push(grads_two.at[:, half_of(other, "two")], both_two.at[theirs], sibling),
        net.push(acts_attn, both_act.at[theirs, pl.ds(0, 512)], sibling),
        net.push(acts_mixer, both_act.at[theirs, pl.ds(512, 1536)], sibling),
        net.push(acts_hidden, both_act.at[theirs, pl.ds(2048, 2048)], sibling),
        net.push(grads_three.at[:, :, half_of(other, "three")], both_three.at[:, theirs], sibling),
    ]
    both_norm[mine] = norm[...]
    both_two[mine] = grads_two[:, half_of(core, "two")]
    both_act[mine, 0:512] = acts_attn[...]
    both_act[mine, 512:2048] = acts_mixer[...]
    both_act[mine, 2048:4096] = acts_hidden[...]
    both_three[:, mine] = grads_three[:, :, half_of(core, "three")]
    output_map = mixed[:, WIDTH + STATE :].astype(jnp.bfloat16)
    wide_states[...] = down(
        output_map, (expand(entering[...]) * grad[...]).astype(jnp.bfloat16)
    )
    pack(wide_states, states)
    copies = [
        net.push(states.at[(c + e + 1) % CTX], parts.at[c], peer) for e, peer in enumerate(peers)
    ]
    parts[c] = states[c]
    for copy in first:
        copy.wait_recv()

    def block(owner_x):
        features = both_norm[:, pl.ds(pl.multiple_of(owner_x * 256, 256), 256)]
        wide = HALVES["two"] // 2
        for piece in range(2):
            at = pl.ds(piece * wide, wide)
            found = dot_rows(features, both_two[:, at])
            for unit in range(16):
                own_two[owner_x, unit // 8, unit // 2 % 4, unit % 2, :, at] = found[
                    unit * 16 : unit * 16 + 16
                ]
        found = []
        for source, (start, size) in enumerate(((0, 128), (512, 384), (2048, 512))):
            at = pl.ds(pl.multiple_of(start + owner_x * size, 128), size)
            found.append(dot_rows(both_act[:, at], both_three[source]))
        for owner_z in range(2):
            for unit in range(8):
                source = 0 if unit < 1 else 1 if unit < 4 else 2
                at = (unit - (0, 1, 4)[source]) * 64 + owner_z * (64, 192, 256)[source]
                own_three[owner_x, owner_z, unit // 2, unit % 2] = found[source][at : at + 64]

    sums = Sums(net, LATE, here, near, core, came, summed, (own_two, own_three))

    def turn(e, nothing):
        block((here["x"] + e + 1) % 4)
        for copy in sums.early(e, send_sem, recv_sem):
            copy.start()
        return nothing

    lax.fori_loop(0, 3, turn, 0)
    block(here["x"])
    sums.send(1, 0)
    sums.send(2, 0)
    for copy in copies:
        copy.wait_recv()
    scan_rows(range(CTX - 1, -1, -1), decays, parts, carries)
    back = send_back(net, c, peers, carries, came_back)
    key_sum[...] = jnp.zeros_like(key_sum)
    value_sum[...] = jnp.zeros_like(value_sum)

    def head(h, nothing):
        keys = kv_all[:, :, 0:128].reshape(CTX * toks, 128)
        values = kv_all[:, :, 128:256].reshape(CTX * toks, 128)
        scores = across(query[h], keys) + hidden_mask[...]
        probs = jnp.exp(scores - log_total[h][:, 0:1])
        grad_probs = across(grad_out[h], values)
        inner_sum = jnp.sum(probs * grad_probs, axis=-1, keepdims=True)
        grad_scores = (probs * (grad_probs - inner_sum)).astype(jnp.bfloat16)
        grad_query[h] = jnp.dot(grad_scores, keys, preferred_element_type=jnp.float32)
        key_sum[...] += down(query[h], grad_scores)
        value_sum[...] += down(grad_out[h], probs.astype(jnp.bfloat16))
        return nothing

    lax.fori_loop(0, HEADS, head, 0)
    for k in range(CTX):
        at = pl.ds(k * toks, toks)
        terms[k, 0:128] = key_sum[:, at].astype(jnp.bfloat16)
        terms[k, 128:256] = value_sum[:, at].astype(jnp.bfloat16)
    key_copies = [
        net.push(terms.at[(c + e + 1) % CTX], term_parts.at[e], peer)
        for e, peer in enumerate(peers)
    ]
    for copy in back:
        copy.wait_recv()
    unpack(came_back, leaving)
    mixer_grads_body(
        grad,
        leaving,
        carried,
        mixed,
        cumulative,
        sizes,
        entering,
        inner,
        rim,
        steps,
        masks,
        intra,
        table,
        grad_inner,
        grad_rim,
        grad_steps,
        grad_conv,
        grad_heads,
        extended,
        grad_ext,
        grad_mixed,
    )
    rim_copy = net.push(grad_rim, rim_back, peers[-1])
    for e in range(3):
        for copy in sums.early(e, send_sem, recv_sem):
            copy.wait_recv()
    for part in range(3):
        sums.wait(part)
        sums.add_up(part, 0)
        sums.send(part, 1)

    def turn_back(both):
        return both * cosine[...] - swap_quarters(both) * sine[...]

    low = jnp.bfloat16
    for j in range(HEADS // 2):
        grads_one[:, 128 * j : 128 * j + 128] = (
            turn_back(join_pair(grad_query, j)) * HEAD_DIM ** (-0.5)
        ).astype(low)
    for copy in key_copies:
        copy.wait_recv()
    collected = terms[c].astype(jnp.float32)
    for e in range(CTX - 1):
        collected = collected + term_parts[e].astype(jnp.float32)
    key_at = HEADS * HEAD_DIM
    grads_one[:, key_at : key_at + 128] = (turn_back(collected[0:128].T) * key_scale).astype(low)
    grads_one[:, key_at + 128 : Z_AT] = collected[128:256].T.astype(low)
    grads_one[:, Z_AT:INNER_AT] = grad_z[...]
    rim_copy.wait_recv()
    grad_inner[toks - 8 :] = grad_inner[toks - 8 :] + rim_back[...]
    grads_one[:, INNER_AT:STEP_AT] = grad_inner[...].astype(low)
    grads_one[:, STEP_AT : STEP_AT + 128] = grad_steps[...].astype(low)
    grads_one[:, PAD_AT:COLS] = jnp.zeros((toks, COLS - PAD_AT), low)
    for part in range(3):
        sums.wait(part)
        sums.add_up(part, 1)
        sums.send(part, 2)
    for part in range(3):
        sums.wait(part)
        sums.add_up(part, 2)
        for kind, out, ref in zip(LATE, (out_two, out_three), summed[part, 2]):
            out[tuple(span(pair) for pair in CUTS[kind][part])] = ref[...]
    for e in range(3):
        for copy in sums.early(e, send_sem, recv_sem):
            copy.wait_send()
    net.drain()


def backward(*ins):
    low, f32 = jnp.bfloat16, jnp.float32
    rows = ins[0].shape[0]
    scratch = [shape for key in stage_keys(range(3)) for shape in came_shapes(LATE, *key)]
    scratch += [shape for key in stage_keys(range(3)) for shape in summed_shapes(LATE, *key)]
    scratch += [
        *[(CTX, 16, HALF_WIDTH)] * 4,
        (CTX, 256, rows),
        (CTX - 1, 256, rows),
        (2 * rows, 1024),
        (2 * rows, HALVES["two"]),
        (2 * rows, 4096),
        (3, 2 * rows, HALVES["three"]),
        (4, 2, 4, 2, 16, HALVES["two"]),
        (4, 2, 4, 2, 64, HALVES["three"]),
    ]
    wide = [
        (128, CTX * rows),
        (128, CTX * rows),
        (STATE, WIDTH),
        (STATE, WIDTH),
        (HEADS, rows, 128),
        (rows, CONV_WIDTH),
        (8, CONV_WIDTH),
        (8, CONV_WIDTH),
        (rows + 8, CONV_WIDTH),
        (rows + 8, CONV_WIDTH),
        (rows, CONV_WIDTH),
        (rows, 128),
    ]
    return call_kernel(
        backward_body,
        "backward",
        3,
        (
            shape_of((rows, COLS), low),
            shape_of((8, CONV_WIDTH), f32),
            shape_of((8, 128), f32),
            shape_of((16, HALVES["two"]), low),
            shape_of((64, HALVES["three"]), low),
        ),
        ins,
        106,
        [*low_scratch(scratch), *[pltpu.VMEM(dims, f32) for dims in wide]],
    )


FIRST = ("one",)


def weight_grads_body(
    norm, grads_one, small, unit_two, unit_three, out_one, out_two, out_three, *rest
):
    came, rest = take(rest, stage_keys(range(3)), FIRST)
    summed, rest = take(rest, stage_keys(range(3)), FIRST)
    both_norm, both_one, own_one, small_in, send_sem, recv_sem = rest
    here, core = coordinates()
    near = neighbours(here, core)
    toks = norm.shape[0]
    sibling = device_of(here, 1 - core)
    meet(all_near(near, core) + [sibling])
    net = Sender(send_sem.at[pl.ds(3, 42)], recv_sem.at[pl.ds(3, 42)])
    mine, theirs = pl.ds(0, toks), pl.ds(toks, toks)
    first = [
        net.push(norm, both_norm.at[theirs], sibling),
        net.push(grads_one.at[:, half_of(1 - core, "one")], both_one.at[theirs], sibling),
        net.push(small, small_in, sibling),
    ]
    both_norm[mine] = norm[...]
    both_one[mine] = grads_one[:, half_of(core, "one")]
    over_z = device_of({**here, "zl": 1 - here["zl"]}, core)
    y, low_z = here["y"], here["zl"]
    late = {"two": out_two, "three": out_three}
    out_two[y, low_z, :, half_of(core, "two")] = unit_two[...]
    out_three[y, low_z, :, half_of(core, "three")] = unit_three[...]

    def pass_on(kind, ref, at_y, at_z, targets):
        piece = ref.at[at_y, at_z, :, half_of(core, kind)]
        return [net.push(piece, piece, target) for target in targets]

    def late_step(at_y, at_z, targets):
        return [
            copy
            for kind, ref in late.items()
            for copy in pass_on(kind, ref, at_y, at_z, targets)
        ]

    to_y = [device_of(at, core) for at in near["y"]]
    late_copies = late_step(y, low_z, [over_z])
    for copy in first:
        copy.wait_recv()

    def block(owner_x, owner_z):
        owner = owner_x * 2 + owner_z
        features = both_norm[:, pl.ds(pl.multiple_of(owner * 128, 128), 128)]
        for low_at, high_at in ((0, 1024), (1024, 2176)):
            found = dot_rows(features, both_one[:, low_at:high_at])
            for unit in range(8):
                rows = found[unit * 16 : unit * 16 + 16]
                if unit == 0 and low_at:
                    extra = (small[owner] + small_in[owner]) * core.astype(jnp.float32)
                    tail = rows[:, 1024:].astype(jnp.float32) + extra
                    rows = jnp.concatenate([rows[:, :1024], tail.astype(jnp.bfloat16)], axis=1)
                own_one[owner_x, owner_z, unit // 2, unit % 2, :, low_at:high_at] = rows

    sums = Sums(net, FIRST, here, near, core, came, summed, (own_one,))

    def turn(e, nothing):
        owner_x = (here["x"] + e + 1) % 4
        block(owner_x, 0)
        block(owner_x, 1)
        for copy in sums.early(e, send_sem, recv_sem):
            copy.start()
        return nothing

    lax.fori_loop(0, 3, turn, 0)

    def own_turn(owner_z, nothing):
        block(here["x"], owner_z)
        return nothing

    lax.fori_loop(0, 2, own_turn, 0)
    sums.send(1, 0)
    sums.send(2, 0)
    for copy in late_copies:
        copy.wait_recv()
    late_copies = late_step(y, slice(None), to_y)
    for e in range(3):
        for copy in sums.early(e, send_sem, recv_sem):
            copy.wait_recv()
    for stage in range(3):
        for part in range(3):
            sums.wait(part)
            sums.add_up(part, stage)
            if stage < 2:
                sums.send(part, stage + 1)
        if stage == 1:
            for copy in late_copies:
                copy.wait_recv()
            late_copies = late_step(slice(None), slice(None), [sibling])
    for part in range(3):
        rows, cols = cut_of("one", part, core)
        out_one[y, low_z, rows, cols] = summed[part, 2][0][...]
    for step in (
        (y, low_z, [over_z]),
        (y, slice(None), to_y),
        (slice(None), slice(None), [sibling]),
    ):
        for copy in pass_on("one", out_one, *step):
            copy.wait_recv()
    for copy in late_copies:
        copy.wait_recv()
    for e in range(3):
        for copy in sums.early(e, send_sem, recv_sem):
            copy.wait_send()
    net.drain()


def sum_weight_grads(norm, grads_one, small, unit_two, unit_three):
    toks = norm.shape[0]
    low = jnp.bfloat16
    scratch = [shape for key in stage_keys(range(3)) for shape in came_shapes(FIRST, *key)]
    scratch += [shape for key in stage_keys(range(3)) for shape in summed_shapes(FIRST, *key)]
    scratch += [
        (2 * toks, 1024),
        (2 * toks, HALVES["one"]),
        (4, 2, 4, 2, 16, HALVES["one"]),
    ]
    return call_kernel(
        weight_grads_body,
        "sum_weight_grads",
        5,
        tuple(
            shape_of((4, 2, UNIT_ROWS[kind], 2 * HALVES[kind]), low)
            for kind in ("one", "two", "three")
        ),
        (norm, grads_one, small, unit_two, unit_three),
        45,
        [*low_scratch(scratch), pltpu.VMEM(small.shape, jnp.float32)],
    )


def local(
    layer_input,
    segment_ids,
    norm_gain,
    w_query,
    w_key,
    w_value,
    w_attn_out,
    w_gate_z,
    w_inner,
    w_step,
    conv_weight,
    conv_bias,
    step_bias,
    decay_log,
    skip_gain,
    mixer_gain,
    w_mixer_out,
    ffn_gain,
    w_gate,
    w_up,
    w_down,
    out_grad,
):
    low = jnp.bfloat16
    tok_rows = layer_input.shape[1]
    ctx_here = lax.axis_index("ctx")
    first_pos = ctx_here * tok_rows
    seg_here = segment_ids[0]
    pos_here = first_pos + jnp.arange(tok_rows, dtype=jnp.int32)
    residual_in = layer_input[0].astype(jnp.float32)
    grad_final = out_grad[0].astype(jnp.float32)
    kv_width = KV_HEADS * HEAD_DIM
    q_width = HEADS * HEAD_DIM
    width_inner = SSM_HEADS * SSM_DIM
    conv_width = width_inner + 2 * STATE
    z_at = q_width + 2 * kv_width
    inner_at = z_at + width_inner
    step_at = inner_at + conv_width

    small = jnp.stack(
        [
            jnp.pad(row, (0, 256 - row.shape[0]))
            for row in (
                *conv_weight,
                conv_bias,
                mixer_gain,
                ffn_gain,
                norm_gain,
                step_bias,
                decay_log,
                skip_gain,
                *[jnp.zeros((256,), low)] * 5,
            )
        ]
    )
    in_one = jnp.concatenate(
        [w_query, w_key, w_value, w_gate_z, w_inner, jnp.pad(w_step, ((0, 0), (0, 232)))], axis=1
    )
    all_one, table, seg_got = gather_weights(
        in_one, small, jnp.broadcast_to(segment_ids, (8, tok_rows))
    )
    full_one = all_one.reshape(FSDP * 128, COLS)
    half_dim = HEAD_DIM // 2
    inverse = rope_base ** (-jnp.arange(half_dim, dtype=jnp.float32) / half_dim)
    angles = pos_here.astype(jnp.float32)[:, None] * inverse[None, :]
    cosine = jnp.tile(jnp.cos(angles), (1, 4))
    sine = jnp.sin(angles)
    sine = jnp.concatenate([-sine, sine, -sine, sine], axis=1)
    normed_low, query, local_kv, gate_z, inner_pre, steps = project(
        residual_in, table, cosine, sine, full_one
    )
    seq_total = CTX * tok_rows
    pos_all = jnp.arange(seq_total, dtype=jnp.int32)
    seg_all = seg_got[:, 0].reshape(seq_total)
    visible = (pos_all[None, :] <= pos_here[:, None]) & (seg_all[None, :] == seg_here[:, None])
    hidden_mask = jnp.where(visible, 0.0, masked_score)

    seg_prior = lax.dynamic_slice_in_dim(seg_all, jnp.maximum(first_pos - 3, 0), 3)
    seg_before = jnp.where(ctx_here > 0, seg_prior, -1)
    seg_ext = jnp.concatenate([seg_before, seg_here])
    columns = [seg_ext[k : k + tok_rows] == seg_here for k in range(CONV - 1)]
    columns += [seg_here == seg_before[2], seg_here == seg_here[-1]]
    columns += [jnp.broadcast_to(seg_here[-1] == seg_before[2], (tok_rows,))]
    masks = jnp.pad(jnp.stack(columns, axis=1).astype(jnp.float32), ((0, 0), (0, 122)))
    order_idx = jnp.arange(tok_rows, dtype=jnp.int32)
    intra = (
        (seg_here[:, None] == seg_here[None, :]) & (order_idx[:, None] >= order_idx[None, :])
    ).astype(jnp.float32)
    (
        kv_all,
        rim_got,
        mixed,
        cumulative,
        sizes,
        entering,
        carried,
        mixer_result,
        decays,
        attended,
        log_total,
        all_two,
        all_three,
    ) = forward(
        query,
        local_kv,
        hidden_mask,
        inner_pre,
        steps,
        masks,
        intra,
        table,
        jnp.concatenate([w_gate, w_up], axis=1),
        jnp.concatenate([w_attn_out, w_mixer_out, w_down], axis=0),
    )
    (
        layer_out,
        grad_middle,
        attn_low,
        mixer_low,
        hidden_low,
        normed_two_low,
        grads_two,
        grads_three,
        grad_out_wide,
        grad_result,
        grad_z,
        grad_gain_two,
        grad_mixer_gain,
    ) = middle_part(
        residual_in,
        grad_final,
        attended,
        mixer_result,
        gate_z,
        table,
        all_two.reshape(FSDP * 128, 2 * HALVES["two"]),
        all_three.reshape(FSDP, OUT_ROWS, 2 * HALVES["three"]),
    )
    grad_gain_two, grad_mixer_gain = grad_gain_two[0], grad_mixer_gain[0]
    grads_one, grad_conv_all, grad_heads, unit_two, unit_three = backward(
        grad_result,
        mixed,
        entering,
        decays,
        query,
        grad_out_wide,
        kv_all,
        hidden_mask,
        log_total,
        normed_two_low,
        grads_two,
        attn_low,
        mixer_low,
        hidden_low,
        grads_three,
        carried,
        cumulative,
        sizes,
        inner_pre,
        rim_got,
        steps,
        masks,
        intra,
        table,
        cosine,
        sine,
        grad_z,
    )
    grad_conv, grad_conv_bias = grad_conv_all[:CONV], grad_conv_all[CONV]
    grad_step_bias = grad_heads[0, :SSM_HEADS]
    grad_decay = grad_heads[1, :SSM_HEADS]
    grad_skip = grad_heads[2, :SSM_HEADS]
    grad_normed_one = right_trans(grads_one, full_one)
    _, pull_one = jax.vjp(rms_scale, residual_in, table[7, : residual_in.shape[1]])
    grad_in_norm, grad_gain_one = pull_one(grad_normed_one)
    input_grad = grad_middle + grad_in_norm

    small_grads = jnp.concatenate(
        [
            grad_gain_one.reshape(FSDP, 128),
            grad_conv.reshape(CONV, FSDP, 224).transpose(1, 0, 2).reshape(FSDP, CONV * 224),
            grad_conv_bias.reshape(FSDP, 224),
            grad_step_bias.reshape(FSDP, 3),
            grad_decay.reshape(FSDP, 3),
            grad_skip.reshape(FSDP, 3),
            grad_mixer_gain.reshape(FSDP, 192),
            grad_gain_two.reshape(FSDP, 128),
            jnp.zeros((FSDP, 2048 - SMALL), jnp.float32),
        ],
        axis=1,
    ).reshape(FSDP, 16, 128)
    sum_one, sum_two, sum_three = sum_weight_grads(
        normed_low, grads_one, small_grads, unit_two, unit_three
    )
    one = sum_one.reshape(128, COLS).astype(jnp.float32)
    two = sum_two.reshape(128, 2 * HALVES["two"]).astype(jnp.float32)
    three = sum_three.reshape(OUT_ROWS, 2 * HALVES["three"]).astype(jnp.float32)
    tiny = one[0:16, PAD_AT:COLS].reshape(-1)
    return (
        layer_out[None],
        input_grad[None],
        tiny[0:128],
        one[:, :q_width],
        one[:, q_width : q_width + kv_width],
        one[:, q_width + kv_width : z_at],
        three[0:64],
        one[:, z_at:inner_at],
        one[:, inner_at:step_at],
        one[:, step_at : step_at + SSM_HEADS],
        tiny[128:1024].reshape(CONV, 224),
        tiny[1024:1248],
        tiny[1248:1251],
        tiny[1251:1254],
        tiny[1254:1257],
        tiny[1257:1449],
        three[64:256],
        tiny[1449:1577],
        two[:, : HALVES["two"]],
        two[:, HALVES["two"] :],
        three[256:512],
    )


def solution(mesh):
    in_specs = (
        P("fsdp", "ctx", None),
        P("fsdp", "ctx"),
        P("fsdp"),
        P("fsdp", None),
        P("fsdp", None),
        P("fsdp", None),
        P("fsdp", None),
        P("fsdp", None),
        P("fsdp", None),
        P("fsdp", None),
        P(None, "fsdp"),
        P("fsdp"),
        P("fsdp"),
        P("fsdp"),
        P("fsdp"),
        P("fsdp"),
        P("fsdp", None),
        P("fsdp"),
        P("fsdp", None),
        P("fsdp", None),
        P("fsdp", None),
        P("fsdp", "ctx", None),
    )
    out_specs = (
        P("fsdp", "ctx", None),
        P("fsdp", "ctx", None),
        P("fsdp"),
        P("fsdp", None),
        P("fsdp", None),
        P("fsdp", None),
        P("fsdp", None),
        P("fsdp", None),
        P("fsdp", None),
        P("fsdp", None),
        P(None, "fsdp"),
        P("fsdp"),
        P("fsdp"),
        P("fsdp"),
        P("fsdp"),
        P("fsdp"),
        P("fsdp", None),
        P("fsdp"),
        P("fsdp", None),
        P("fsdp", None),
        P("fsdp", None),
    )
    return jax.shard_map(local, mesh=mesh, in_specs=in_specs, out_specs=out_specs, check_vma=False)
```

```python
import jax
import jax.numpy as jnp
from jax import lax
from jax.experimental import pallas as pl
from jax.experimental.pallas import tpu as pltpu
from jax.sharding import PartitionSpec as P

HEADS = 8
KV_HEADS = 2
HEAD_DIM = 64
SSM_HEADS = 24
SSM_DIM = 64
STATE = 128
CONV = 4


epsilon = 1e-05
rope_base = 10000.0
key_scale = 0.5
attn_out_scale = 0.8
mixer_out_scale = 0.5
gate_scale = 0.75
down_scale = 0.8
masked_score = -1e30
highest = lax.Precision.HIGHEST


def matmul_f32(left_side, right_side):
    return jnp.dot(left_side, right_side, preferred_element_type=jnp.float32)


def right_trans(left_side, right_side):
    return lax.dot_general(
        left_side, right_side, (((1,), (1,)), ((), ())), preferred_element_type=jnp.float32
    )


def rms_scale(values, gain_vec):
    return (
        values * lax.rsqrt(jnp.mean(values * values, axis=-1, keepdims=True) + epsilon) * gain_vec
    )


MESH = pl.DeviceIdType.MESH
CTX = 16
FSDP = 8
COLS = 4352
PAD_AT = 4224
HALVES = {"one": 2176, "two": 2048, "three": 512}
UNIT_ROWS = {"one": 16, "two": 16, "three": 64}
ORDERS = (("x", "y", "z"), ("y", "z", "x"), ("z", "x", "y"))
CUTS = {
    "one": (((0, 16), (0, 768)), ((0, 16), (768, 1536)), ((0, 16), (1536, 2176))),
    "two": (((0, 16), (0, 256)), ((0, 16), (256, 1152)), ((0, 16), (1152, 2048))),
    "three": (((0, 32), (0, 512)), ((32, 48), (0, 512)), ((48, 64), (0, 512))),
}
OUT_ROWS = 512
EVERYTHING = ("x", "y", "z")
SMALL = 1577
WIDTH = SSM_DIM * SSM_HEADS
HALF_WIDTH = WIDTH // 2
CONV_WIDTH = WIDTH + 2 * STATE
VMEM_LIMIT = 60 * 2**20


def place():
    f, c = lax.axis_index("fsdp"), lax.axis_index("ctx")
    return f, c, c // 4, (c // 2) % 2, c % 2


def at_ctx(y, low_z, core):
    return (y * 2 + low_z) * 2 + core


def meet(partners):
    barrier = pltpu.get_barrier_semaphore()
    for partner in partners:
        pl.semaphore_signal(barrier, inc=1, device_id=partner, device_id_type=MESH)
    pl.semaphore_wait(barrier, len(partners))


class Sender:
    def __init__(self, send_sem, recv_sem):
        self.send_sem, self.recv_sem, self.used, self.all = send_sem, recv_sem, 0, []

    def push(self, src, dst, partner):
        index = self.used
        self.used += 1
        copy = pltpu.make_async_remote_copy(
            src_ref=src,
            dst_ref=dst,
            send_sem=self.send_sem.at[index],
            recv_sem=self.recv_sem.at[index],
            device_id=partner,
            device_id_type=MESH,
        )
        copy.start()
        self.all.append(copy)
        return copy

    def drain(self):
        for copy in self.all:
            copy.wait_send()


def call_kernel(body, name, cid, outs, ins, sems, scratch=(), far_in=(), far_out=(), aliases=None):
    def spec(far):
        return pl.BlockSpec(memory_space=pl.ANY if far else pltpu.VMEM)

    return pl.pallas_call(
        body,
        name=name,
        out_shape=outs,
        in_specs=[spec(k in far_in) for k in range(len(ins))],
        out_specs=tuple(spec(k in far_out) for k in range(len(outs))),
        scratch_shapes=[
            *scratch,
            pltpu.SemaphoreType.DMA((sems,)),
            pltpu.SemaphoreType.DMA((sems,)),
        ],
        input_output_aliases=aliases or {},
        compiler_params=pltpu.CompilerParams(
            collective_id=cid, has_side_effects=True, vmem_limit_bytes=VMEM_LIMIT
        ),
    )(*ins)


def shape_of(dims, kind):
    return jax.ShapeDtypeStruct(dims, kind)


AXES = (("x", "x"), ("zh", "z"), ("y", "y"), ("zl", "z"))
EXTENT = {"x": 4, "zh": 2, "y": 4, "zl": 2}


def coordinates():
    f, c, y, low_z, core = place()
    return {"x": f // 2, "zh": f % 2, "y": y, "zl": low_z}, core


def neighbours(here, core):
    z = here["zh"] * 2 + here["zl"]
    found = {"x": [], "y": [], "z": []}
    for e in range(1, 4):
        found["x"].append({**here, "x": (here["x"] + e) % 4})
        found["y"].append({**here, "y": (here["y"] + e) % 4})
        other = (z + e) % 4
        found["z"].append({**here, "zh": other // 2, "zl": other % 2})
    return found


def device_of(at, core):
    return {"fsdp": at["x"] * 2 + at["zh"], "ctx": at_ctx(at["y"], at["zl"], core)}


def index_of(kept, fixed, at):
    return tuple(
        at[axis] if axis_dim in fixed else slice(None)
        for axis, axis_dim in AXES
        if axis_dim in kept
    )


def extents(kept):
    return tuple(EXTENT[axis] for axis, axis_dim in AXES if axis_dim in kept)


def span(pair):
    return pl.ds(pair[0], pair[1] - pair[0])


def cut_of(kind, part, core):
    rows, cols = CUTS[kind][part]
    at = pl.multiple_of(core * HALVES[kind] + cols[0], 128)
    return span(rows), pl.ds(at, cols[1] - cols[0])


def all_near(near, core):
    return [device_of(at, core) for dim in EVERYTHING for at in near[dim]]


class Gather:
    def __init__(self, net, outs, here, near, core):
        self.net, self.outs, self.here, self.near, self.core = net, outs, here, near, core
        self.pending, self.crossing = [[], [], []], []
        self.sibling = device_of(here, 1 - core)

    def pieces(self, part, fixed, at):
        index = index_of(EVERYTHING, fixed, at)
        return [
            ref.at[(*index, *cut_of(kind, part, self.core))] for kind, ref in self.outs.items()
        ]

    def own(self, ins, sem):
        point = index_of(EVERYTHING, EVERYTHING, self.here)
        copies = []
        for k, (kind, ref) in enumerate(self.outs.items()):
            half = HALVES[kind]
            cols = pl.ds(pl.multiple_of(self.core * half, 128), half)
            copies.append(
                pltpu.make_async_copy(
                    ins[kind].at[self.here["y"], self.here["zl"], :, cols],
                    ref.at[(*point, slice(None), cols)],
                    sem.at[k],
                )
            )
        return copies

    def stage(self, number, ins=None):
        jobs = []
        for part, order in enumerate(ORDERS):
            steps = order[::-1]
            dim, fixed = steps[number], steps[number:]
            for copy in self.pending[part]:
                copy.wait_recv()
            refs = self.pieces(part, fixed, self.here)
            sources = refs
            if ins is not None:
                sources = [
                    ins[kind].at[
                        (self.here["y"], self.here["zl"], *cut_of(kind, part, self.core))
                    ]
                    for kind in self.outs
                ]
            jobs.append((self.near[dim], sources, refs))
            self.pending[part] = []
        for e in range(3):
            for part, (near, sources, refs) in enumerate(jobs):
                self.pending[part] += [
                    self.net.push(src, ref, device_of(near[e], self.core))
                    for src, ref in zip(sources, refs)
                ]
        if number == 2:
            for _, _, refs in jobs:
                self.crossing += [self.net.push(ref, ref, self.sibling) for ref in refs]

    def finish(self):
        kinds = len(self.outs)
        for e in range(3):
            for part, order in enumerate(ORDERS):
                for copy in self.pending[part][kinds * e : kinds * e + kinds]:
                    copy.wait_recv()
                source = self.near[order[0]][2 - e]
                self.crossing += [
                    self.net.push(ref, ref, self.sibling)
                    for ref in self.pieces(part, (order[0],), source)
                ]
        for copy in self.crossing:
            copy.wait_recv()


def gather_shapes(kinds):
    return [
        shape_of((4, 2, 4, 2, UNIT_ROWS[kind], 2 * HALVES[kind]), jnp.bfloat16) for kind in kinds
    ]


TABLE = ((0, 5, 224), (5, 6, 192), (6, 8, 128), (8, 11, 3))


def ctx_peers(c):
    return [{"ctx": (c + e) % CTX} for e in range(1, CTX)]


def expand(per_head):
    rows = per_head.shape[0]
    lane = lax.broadcasted_iota(jnp.int32, (rows, 128), 1)
    return jnp.concatenate(
        [
            jnp.where(
                lane < SSM_DIM,
                jnp.broadcast_to(per_head[:, 2 * j : 2 * j + 1], (rows, 128)),
                jnp.broadcast_to(per_head[:, 2 * j + 1 : 2 * j + 2], (rows, 128)),
            )
            for j in range(SSM_HEADS // 2)
        ],
        axis=1,
    )


def pack(states, chunks):
    for k in range(CTX):
        rows = states[8 * k : 8 * k + 8]
        chunks[k] = jnp.concatenate([rows[:, :HALF_WIDTH], rows[:, HALF_WIDTH:]], axis=0).astype(
            jnp.bfloat16
        )


def unpack(chunks, states):
    for k in range(CTX):
        rows = chunks[k].astype(jnp.float32)
        states[8 * k : 8 * k + 8] = jnp.concatenate([rows[:8], rows[8:]], axis=1)


def scan_rows(order, decay_of, parts, carries):
    wide = expand(jnp.concatenate([decay_of[k, 0:1] for k in range(CTX)], axis=0))
    state = jnp.zeros((16, HALF_WIDTH), jnp.float32)
    for at in order:
        carries[at] = state.astype(jnp.bfloat16)
        decay = jnp.concatenate(
            [
                jnp.broadcast_to(wide[at : at + 1, :HALF_WIDTH], (8, HALF_WIDTH)),
                jnp.broadcast_to(wide[at : at + 1, HALF_WIDTH:], (8, HALF_WIDTH)),
            ],
            axis=0,
        )
        state = decay * state + parts[at].astype(jnp.float32)


def send_back(net, c, peers, carries, carried):
    copies = [
        net.push(carries.at[(c + e + 1) % CTX], carried.at[c], peer) for e, peer in enumerate(peers)
    ]
    carried[c] = carries[c]
    return copies


def across(left, right):
    return lax.dot_general(
        left, right, (((1,), (1,)), ((), ())), preferred_element_type=jnp.float32
    )


def down(left, right):
    return lax.dot_general(
        left, right, (((0,), (0,)), ((), ())), preferred_element_type=jnp.float32
    )


def masks_from(seg, seg_cols, seg_all, c, hidden_mask, masks, intra):
    rows = seg_cols.shape[0]
    row = lax.broadcasted_iota(jnp.int32, (rows, 128), 0)
    lane = lax.broadcasted_iota(jnp.int32, (rows, 128), 1)
    here = seg_cols[:, 3:4]
    before = jnp.where(c > 0, seg_all[(c + CTX - 1) % CTX][0:1], -1)
    found = jnp.zeros((rows, 128), jnp.float32)
    for tap in range(CONV - 1):
        earlier = jnp.broadcast_to(seg_cols[:, tap : tap + 1], (rows, 128))
        for t in range(CONV - 1 - tap):
            at = 125 + t + tap
            earlier = jnp.where(row == t, before[:, at : at + 1], earlier)
        found = jnp.where((lane == tap) & (earlier == here), 1.0, found)
    last, prior = seg[0:1, 127:128], before[:, 127:128]
    found = jnp.where((lane == 3) & (here == prior), 1.0, found)
    found = jnp.where((lane == 4) & (here == last), 1.0, found)
    masks[...] = jnp.where((lane == 5) & (last == prior), 1.0, found)
    intra[...] = jnp.where((row >= lane) & (here == seg[0:1]), 1.0, 0.0)
    for k in range(CTX):
        seen = (here == seg_all[k][0:1]) & (lane + k * rows <= row + c * rows)
        hidden_mask[:, k * rows : (k + 1) * rows] = jnp.where(seen, 0.0, masked_score)


def forward_body(
    row_in,
    cosine,
    sine,
    small,
    seg,
    seg_cols,
    in_one,
    in_two,
    in_three,
    norm_low,
    query,
    gate_z,
    inner,
    steps,
    table,
    hidden_mask,
    masks,
    intra,
    kv_all,
    rim_all,
    mixed,
    cumulative,
    sizes,
    entering,
    carried,
    result,
    decays,
    attended,
    log_total,
    out_one,
    out_two,
    out_three,
    kv,
    got_small,
    seg_all,
    states,
    inside,
    extended,
    wide_states,
    parts,
    carries,
    came_back,
    decay,
    own_sem,
    send_sem,
    recv_sem,
):
    here, core = coordinates()
    near = neighbours(here, core)
    y, low_z = here["y"], here["zl"]
    c = at_ctx(y, low_z, core)
    f = here["x"] * 2 + here["zh"]
    peers = ctx_peers(c)
    rows = row_in.shape[0]
    small_peers = [{"fsdp": (f + d) % FSDP} for d in range(1, FSDP)]
    meet(
        peers
        + all_near(near, core)
        + [{"fsdp": (here["x"] + e) % 4 * 2 + 1 - here["zh"]} for e in range(1, 4)]
    )
    net = Sender(send_sem, recv_sem)
    early = Gather(net, {"one": out_one}, here, near, core)
    early.stage(0, {"one": in_one})
    tiny = [net.push(small, got_small.at[f], peer) for peer in small_peers]
    tiny += [net.push(seg, seg_all.at[c], peer) for peer in peers]
    ins = {"two": in_two, "three": in_three}
    late = Gather(net, {"two": out_two, "three": out_three}, here, near, core)
    own = early.own({"one": in_one}, own_sem.at[pl.ds(0, 1)])
    own_late = late.own(ins, own_sem.at[pl.ds(1, 2)])
    for copy in own + own_late:
        copy.start()
    got_small[f] = small[...]
    seg_all[c] = seg[...]
    for copy in own:
        copy.wait()
    early.stage(1)
    early.stage(2)
    late.stage(0, ins)
    for copy in tiny:
        copy.wait_recv()
    table[...] = jnp.zeros_like(table)
    for k in range(FSDP):
        piece = got_small[k].astype(jnp.float32)
        for first, last, width in TABLE:
            table[first:last, k * width : k * width + width] = piece[first:last, :width]
    table[9:10] = jnp.exp(table[9:10])
    table[11:12, :WIDTH] = expand(table[10:11, 0:128])
    masks_from(seg, seg_cols, seg_all, c, hidden_mask, masks, intra)
    early.finish()
    for copy in own_late:
        copy.wait()
    late.stage(1)
    project_body(
        row_in, table, cosine, sine, out_one, norm_low, query, kv, gate_z, inner, steps
    )
    rim_copy = net.push(inner.at[pl.ds(rows - 8, 8)], rim_all, peers[0])
    over_z = device_of({**here, "zl": 1 - low_z}, core)
    sibling = device_of(here, 1 - core)
    kv_all[y, low_z, core] = kv[...]
    to_z = net.push(kv, kv_all.at[y, low_z, core], over_z)
    rim_copy.wait_recv()
    mixer_parts_body(
        inner,
        rim_all,
        steps,
        masks,
        intra,
        table,
        mixed,
        cumulative,
        sizes,
        states,
        decay,
        entering,
        inside,
        extended,
        wide_states,
    )
    copies = []
    for e, peer in enumerate(peers):
        copies.append(net.push(states.at[(c + e + 1) % CTX], parts.at[c], peer))
        copies.append(net.push(decay, decays.at[c], peer))
    parts[c] = states[c]
    decays[c] = decay[...]
    to_z.wait_recv()
    pair = kv_all.at[y, :, core]
    to_y = [net.push(pair, pair, device_of(at, core)) for at in near["y"]]
    for copy in to_y:
        copy.wait_recv()
    whole = kv_all.at[:, :, core]
    net.push(whole, whole, sibling).wait_recv()

    def head(h, nothing):
        keys = kv_all[:, :, :, :, 0:128].reshape(CTX * rows, 128)
        values = kv_all[:, :, :, :, 128:256].reshape(CTX * rows, 128)
        scores = across(query[h], keys) + hidden_mask[...]
        row_max = jnp.max(scores, axis=-1, keepdims=True)
        weights = jnp.exp(scores - row_max)
        row_sum = jnp.sum(weights, axis=-1, keepdims=True)
        probs = (weights * (1.0 / row_sum)).astype(jnp.bfloat16)
        attended[h] = jnp.dot(probs, values, preferred_element_type=jnp.float32).astype(
            jnp.bfloat16
        )
        log_total[h] = jnp.broadcast_to(row_max + jnp.log(row_sum), (rows, 128))
        return nothing

    for copy in copies:
        copy.wait_recv()
    scan_rows(range(CTX), decays, parts, carries)
    back = send_back(net, c, peers, carries, came_back)
    late.stage(2)
    lax.fori_loop(0, HEADS, head, 0)
    for copy in back:
        copy.wait_recv()
    unpack(came_back, carried)
    output_map = mixed[:, WIDTH + STATE :].astype(jnp.bfloat16)
    result[...] = inside[...] + expand(entering[...]) * jnp.dot(
        output_map, carried[...].astype(jnp.bfloat16), preferred_element_type=jnp.float32
    )
    late.finish()
    net.drain()


def forward(row_in, cosine, sine, small, seg, seg_cols, one, two, three):
    rows, dim = row_in.shape
    f32, low = jnp.float32, jnp.bfloat16
    return call_kernel(
        forward_body,
        "forward",
        1,
        (
            shape_of((rows, dim), low),
            shape_of((HEADS, rows, 128), low),
            shape_of((rows, WIDTH), f32),
            shape_of((rows, CONV_WIDTH), f32),
            shape_of((rows, 128), f32),
            shape_of((16, CONV_WIDTH), f32),
            shape_of((rows, CTX * rows), f32),
            shape_of((rows, 128), f32),
            shape_of((rows, rows), f32),
            shape_of((4, 2, 2, rows, 256), low),
            shape_of((8, CONV_WIDTH), f32),
            shape_of((rows, CONV_WIDTH), f32),
            shape_of((rows, 128), f32),
            shape_of((rows, 128), f32),
            shape_of((rows, 128), f32),
            shape_of((STATE, WIDTH), f32),
            shape_of((rows, WIDTH), f32),
            shape_of((CTX, 8, 128), f32),
            shape_of((HEADS, rows, 128), low),
            shape_of((HEADS, rows, 128), f32),
            *gather_shapes(["one", "two", "three"]),
        ),
        (
            row_in,
            cosine,
            sine,
            small,
            seg,
            seg_cols,
            one.reshape(4, 2, 16, 2 * HALVES["one"]),
            two.reshape(4, 2, 16, 2 * HALVES["two"]),
            three.reshape(4, 2, 64, 2 * HALVES["three"]),
        ),
        190,
        (
            pltpu.VMEM((rows, 256), low),
            pltpu.VMEM((FSDP, 16, 256), low),
            pltpu.VMEM((CTX, 8, 128), jnp.int32),
            pltpu.VMEM((CTX, 16, HALF_WIDTH), low),
            pltpu.VMEM((rows, WIDTH), f32),
            pltpu.VMEM((rows + 8, CONV_WIDTH), f32),
            pltpu.VMEM((STATE, WIDTH), f32),
            *[pltpu.VMEM((CTX, 16, HALF_WIDTH), low)] * 3,
            pltpu.VMEM((8, 128), f32),
            pltpu.SemaphoreType.DMA((3,)),
        ),
        (6, 7, 8),
        (21, 22),
    )


def plain_kernel(body, name, outs, ins, scratch=()):
    return pl.pallas_call(
        body,
        name=name,
        out_shape=outs,
        in_specs=[pl.BlockSpec(memory_space=pltpu.VMEM)] * len(ins),
        out_specs=tuple(pl.BlockSpec(memory_space=pltpu.VMEM) for _ in outs),
        scratch_shapes=list(scratch),
        compiler_params=pltpu.CompilerParams(vmem_limit_bytes=VMEM_LIMIT),
    )(*ins)


TAP_ROWS = 8 - CONV + 1


def conv_sum(extended, masks, conv_par, at):
    rows = masks.shape[0]
    total = jnp.broadcast_to(conv_par[CONV : CONV + 1, at], (rows, conv_par[0:1, at].shape[1]))
    for tap in range(CONV):
        first = TAP_ROWS + tap
        term = conv_par[tap : tap + 1, at] * extended[first : first + rows, at]
        total = total + (term * masks[:, tap : tap + 1] if tap < CONV - 1 else term)
    return total


def lower_ones(rows):
    at = lax.broadcasted_iota(jnp.int32, (rows, rows), 0)
    return (at >= lax.broadcasted_iota(jnp.int32, (rows, rows), 1)).astype(jnp.float32)


def exact(left, right, contract):
    return lax.dot_general(
        left,
        right,
        ((contract[0], contract[1]), ((), ())),
        precision=highest,
        preferred_element_type=jnp.float32,
    )


def swap_quarters(values):
    lane = lax.broadcasted_iota(jnp.int32, values.shape, 1)
    quarter = HEAD_DIM // 2
    ahead = jnp.concatenate([values[:, quarter:], values[:, :quarter]], axis=1)
    behind = jnp.concatenate([values[:, 128 - quarter :], values[:, : 128 - quarter]], axis=1)
    return jnp.where(lane % HEAD_DIM < quarter, ahead, behind)


def split_pair(both, j, out):
    lane = lax.broadcasted_iota(jnp.int32, both.shape, 1)
    turned = shift_half(both)
    low = jnp.bfloat16
    if j < HEADS // 4:
        out[2 * j] = jnp.where(lane < HEAD_DIM, both, 0.0).astype(low)
        out[2 * j + 1] = jnp.where(lane < HEAD_DIM, turned, 0.0).astype(low)
    else:
        out[2 * j] = jnp.where(lane < HEAD_DIM, 0.0, turned).astype(low)
        out[2 * j + 1] = jnp.where(lane < HEAD_DIM, 0.0, both).astype(low)


def join_pair(values, j):
    first, second = values[2 * j].astype(jnp.float32), values[2 * j + 1].astype(jnp.float32)
    if j < HEADS // 4:
        second = shift_half(second)
    else:
        first = shift_half(first)
    lane = lax.broadcasted_iota(jnp.int32, first.shape, 1)
    return jnp.where(lane < HEAD_DIM, first, second)


Z_AT = HEADS * HEAD_DIM + 2 * KV_HEADS * HEAD_DIM
INNER_AT = Z_AT + WIDTH
STEP_AT = INNER_AT + CONV_WIDTH


def project_body(row_in, table, cosine, sine, weights, norm_low, query, kv, gate_z, inner, steps):
    values = row_in[...]
    scale = lax.rsqrt(mean_last(values * values) + epsilon)
    normed = (values * scale * table[7:8, 0 : values.shape[1]]).astype(jnp.bfloat16)
    norm_low[...] = normed

    def part(first, last):
        piece = weights[:, :, :, :, :, first:last].reshape(values.shape[1], last - first)
        return jnp.dot(normed, piece, preferred_element_type=jnp.float32)

    def turn(both):
        return both * cosine[...] + swap_quarters(both) * sine[...]

    for j in range(HEADS // 2):
        split_pair(turn(part(128 * j, 128 * j + 128)) * HEAD_DIM ** (-0.5), j, query)
    key_at = HEADS * HEAD_DIM
    kv[:, 0:128] = (turn(part(key_at, key_at + 128)) * key_scale).astype(jnp.bfloat16)
    kv[:, 128:256] = part(key_at + 128, key_at + 256).astype(jnp.bfloat16)
    for at in range(0, WIDTH, 512):
        gate_z[:, at : at + 512] = part(Z_AT + at, Z_AT + at + 512)
    for at in range(0, CONV_WIDTH, 256):
        inner[:, at : at + 256] = part(INNER_AT + at, INNER_AT + at + 256)
    steps[...] = part(STEP_AT, STEP_AT + 128)


def mixer_parts_body(
    inner,
    rim,
    steps,
    masks,
    intra,
    table,
    mixed,
    cumulative,
    sizes,
    chunks,
    decay,
    entering,
    inside,
    extended,
    states,
):
    rows = inner.shape[0]
    low = jnp.bfloat16
    extended[0:8] = rim[...]
    extended[8:] = inner[...]
    for piece in range(CONV_WIDTH // 256):
        at = slice(piece * 256, piece * 256 + 256)
        total = conv_sum(extended, masks, table, at)
        mixed[:, at] = total / (1.0 + jnp.exp(-total))
    raw = steps[...] + table[8:9, 0:128]
    size = jnp.maximum(raw, 0.0) + jnp.log1p(jnp.exp(-jnp.abs(raw)))
    sums = exact(lower_ones(rows), -size * table[9:10, 0:128], ((1,), (0,)))
    cumulative[...] = sums
    sizes[...] = size
    last = sums[rows - 1 : rows]
    entering[...] = jnp.exp(sums) * masks[:, 3:4]
    decay[...] = jnp.broadcast_to(jnp.exp(last) * masks[0:1, 5:6], (8, 128))
    tail = masks[:, 4:5] * jnp.exp(last - sums) * size
    weighted = (expand(tail) * mixed[:, :WIDTH]).astype(low)
    input_map = mixed[:, WIDTH : WIDTH + STATE]
    output_map = mixed[:, WIDTH + STATE :]
    states[...] = down(input_map.astype(low), weighted)
    pack(states, chunks)
    pairing = exact(output_map, input_map, ((1,), (1,))) * intra[...]
    sums_t, size_t = sums.T, size.T
    lane = lax.broadcasted_iota(jnp.int32, (rows, 128), 1)
    for j in range(SSM_HEADS // 2):
        at = slice(128 * j, 128 * j + 128)
        values = mixed[:, at]
        found = []
        for h in (2 * j, 2 * j + 1):
            spread = jnp.minimum(sums[:, h : h + 1] - sums_t[h : h + 1], 0.0)
            mixing = (jnp.exp(spread) * pairing * size_t[h : h + 1]).astype(low)
            found.append(jnp.dot(mixing, values.astype(low), preferred_element_type=jnp.float32))
        inside[:, at] = jnp.where(lane < SSM_DIM, found[0], found[1]) + table[11:12, at] * values


def mean_last(values):
    return jnp.mean(values, axis=-1, keepdims=True)


def pair_of(weights, j, first, last):
    return jnp.concatenate([weights[2 * j, first:last], weights[2 * j + 1, first:last]], axis=0)


def shift_half(values):
    return jnp.concatenate([values[:, HEAD_DIM:], values[:, :HEAD_DIM]], axis=1)


def middle_body(
    row_in,
    row_grad,
    attended,
    result,
    gate_z,
    table,
    w_two,
    w_three,
    row_out,
    grad_middle,
    attn_low,
    mixer_low,
    hidden_low,
    norm_low,
    grads_two,
    grads_three,
    grad_out,
    grad_result,
    grad_z,
    grad_ffn_gain,
    grad_mixer_gain,
    down_sum,
    norm_sum,
    grad_flat,
):
    low, f32 = jnp.bfloat16, jnp.float32
    attn_sum = jnp.zeros(row_in.shape, f32)
    for j in range(HEADS // 2):
        both = join_pair(attended, j).astype(low)
        attn_low[:, 128 * j : 128 * j + 128] = both
        attn_sum = attn_sum + jnp.dot(
            both, pair_of(w_three, j, 0, 64), preferred_element_type=f32
        )
    z, mixed_out = gate_z[...], result[...]
    sig_z = 1.0 / (1.0 + jnp.exp(-z))
    flat = mixed_out * (z * sig_z)
    scale = lax.rsqrt(mean_last(flat * flat) + epsilon)
    normed = (flat * scale * table[5:6, 0:WIDTH]).astype(low)
    mixer_low[...] = normed
    mixer_sum = jnp.zeros(row_in.shape, f32)
    for j in range(4):
        mixer_sum = mixer_sum + jnp.dot(
            normed[:, 384 * j : 384 * j + 384],
            pair_of(w_three, j, 64, 256),
            preferred_element_type=f32,
        )
    middle = row_in[...] + attn_sum * attn_out_scale + mixer_sum * mixer_out_scale
    scale_two = lax.rsqrt(mean_last(middle * middle) + epsilon)
    norm_low[...] = (middle * scale_two * table[6:7, 0 : row_in.shape[1]]).astype(low)
    grad_down = (row_grad[...] * down_scale).astype(low)
    grads_three[2] = grad_down
    down_sum[...] = jnp.zeros_like(down_sum)
    norm_sum[...] = jnp.zeros_like(norm_sum)
    ff_width = FSDP * 256

    def chunk(f, nothing):
        at = pl.ds(pl.multiple_of(f * 256, 256), 256)
        at_up = pl.ds(pl.multiple_of(ff_width + f * 256, 256), 256)
        w_gate, w_up, w_down = w_two[:, at], w_two[:, at_up], w_three[f, 256:512]
        gate = jnp.dot(norm_low[...], w_gate, preferred_element_type=f32) * gate_scale
        up = jnp.dot(norm_low[...], w_up, preferred_element_type=f32)
        sig = 1.0 / (1.0 + jnp.exp(-gate))
        hidden = (gate * sig * up).astype(low)
        hidden_low[:, at] = hidden
        down_sum[...] += jnp.dot(hidden, w_down, preferred_element_type=f32)
        grad_hidden = across(grad_down, w_down)
        grad_gate = (
            grad_hidden * up * sig * (1.0 + gate * (1.0 - sig)) * gate_scale
        ).astype(low)
        grad_up = (grad_hidden * gate * sig).astype(low)
        grads_two[:, at] = grad_gate
        grads_two[:, at_up] = grad_up
        norm_sum[...] += across(grad_gate, w_gate) + across(grad_up, w_up)
        return nothing

    lax.fori_loop(0, FSDP, chunk, 0)
    row_out[...] = (middle + down_sum[...] * down_scale).astype(low)
    grad_norm = norm_sum[...]
    weighted = grad_norm * table[6:7, 0 : row_in.shape[1]]
    grad_mid = (
        row_grad[...]
        + scale_two * weighted
        - middle * (scale_two * scale_two * scale_two) * mean_last(middle * weighted)
    )
    grad_middle[...] = grad_mid
    grad_ffn_gain[...] = jnp.broadcast_to(
        jnp.sum(grad_norm * middle * scale_two, axis=0, keepdims=True), grad_ffn_gain.shape
    )
    grad_attn = (grad_mid * attn_out_scale).astype(low)
    grad_mix = (grad_mid * mixer_out_scale).astype(low)
    grads_three[0] = grad_attn
    grads_three[1] = grad_mix
    for j in range(HEADS // 2):
        split_pair(across(grad_attn, pair_of(w_three, j, 0, 64)), j, grad_out)
    for j in range(4):
        grad_flat[:, 384 * j : 384 * j + 384] = across(grad_mix, pair_of(w_three, j, 64, 256))
    grad_normed = grad_flat[...]
    weighted = grad_normed * table[5:6, 0:WIDTH]
    grad_mixer_gain[...] = jnp.broadcast_to(
        jnp.sum(grad_normed * flat * scale, axis=0, keepdims=True), grad_mixer_gain.shape
    )
    grad_gated = scale * weighted - flat * (scale * scale * scale) * mean_last(flat * weighted)
    grad_result[...] = grad_gated * (z * sig_z)
    grad_z[...] = (grad_gated * mixed_out * sig_z * (1.0 + z * (1.0 - sig_z))).astype(low)


def middle_part(row_in, row_grad, attended, result, gate_z, table, w_two, w_three):
    rows, dim = row_in.shape
    f32, low = jnp.float32, jnp.bfloat16
    return plain_kernel(
        middle_body,
        "middle_part",
        (
            shape_of((rows, dim), low),
            shape_of((rows, dim), f32),
            shape_of((rows, HEADS * HEAD_DIM), low),
            shape_of((rows, WIDTH), low),
            shape_of((rows, FSDP * 256), low),
            shape_of((rows, dim), low),
            shape_of((rows, 2 * FSDP * 256), low),
            shape_of((3, rows, dim), low),
            shape_of((HEADS, rows, 128), low),
            shape_of((rows, WIDTH), f32),
            shape_of((rows, WIDTH), low),
            shape_of((8, dim), f32),
            shape_of((8, WIDTH), f32),
        ),
        (row_in, row_grad, attended, result, gate_z, table, w_two, w_three),
        (
            pltpu.VMEM((rows, dim), f32),
            pltpu.VMEM((rows, dim), f32),
            pltpu.VMEM((rows, WIDTH), f32),
        ),
    )


def mixer_grads_body(
    grad,
    leaving,
    carried,
    mixed,
    cumulative,
    sizes,
    entering,
    inner,
    rim,
    steps,
    masks,
    intra,
    table,
    grad_inner,
    grad_rim,
    grad_steps,
    grad_conv,
    grad_heads,
    extended,
    grad_ext,
    grad_mixed,
):
    rows = inner.shape[0]
    low = jnp.bfloat16
    sums, size = cumulative[...], sizes[...]
    last = sums[rows - 1 : rows]
    input_map = mixed[:, WIDTH : WIDTH + STATE]
    output_map = mixed[:, WIDTH + STATE :]
    gather_head = (
        lax.broadcasted_iota(jnp.int32, (WIDTH, 128), 0) // SSM_DIM
        == lax.broadcasted_iota(jnp.int32, (WIDTH, 128), 1)
    ).astype(jnp.float32)

    def per_head(wide):
        return exact(wide, gather_head, ((1,), (0,)))

    tail_decay = masks[:, 4:5] * jnp.exp(last - sums)
    tail = tail_decay * size
    leaving_low, carried_low = leaving[...].astype(low), carried[...].astype(low)
    from_state = jnp.dot(input_map.astype(low), leaving_low, preferred_element_type=jnp.float32)
    to_output = jnp.dot(output_map.astype(low), carried_low, preferred_element_type=jnp.float32)
    wide_tail = expand(tail)
    values_all, grad_all = mixed[:, :WIDTH], grad[...]
    grad_tail = per_head(values_all * from_state)
    grad_entering = per_head(grad_all * to_output)
    grad_skip = per_head(jnp.sum(grad_all * values_all, axis=0, keepdims=True))
    grad_block = per_head(jnp.sum(leaving[...] * carried[...], axis=0, keepdims=True))
    grad_input = across((wide_tail * values_all).astype(low), leaving_low)
    grad_output = across((expand(entering[...]) * grad_all).astype(low), carried_low)
    grad_mixed[:, :WIDTH] = wide_tail * from_state + table[11:12, 0:WIDTH] * grad_all

    pairing = exact(output_map, input_map, ((1,), (1,)))
    sums_t, size_t = sums.T, size.T
    lane = lax.broadcasted_iota(jnp.int32, (rows, 128), 1)
    grad_pairing = jnp.zeros((rows, rows), jnp.float32)
    row_sums = jnp.zeros((rows, 128), jnp.float32)
    size_rows = []
    for j in range(SSM_HEADS // 2):
        at = slice(128 * j, 128 * j + 128)
        values, grads = mixed[:, at].astype(low), grad[:, at]
        found = []
        for h in (2 * j, 2 * j + 1):
            own_lanes = lane < SSM_DIM if h == 2 * j else lane >= SSM_DIM
            spread = jnp.minimum(sums[:, h : h + 1] - sums_t[h : h + 1], 0.0)
            decays = jnp.exp(spread) * intra[...]
            inner_part = decays * pairing
            mixing = inner_part * size_t[h : h + 1]
            found.append(down(mixing.astype(low), grads.astype(low)))
            grad_mixing = across(jnp.where(own_lanes, grads, 0.0).astype(low), values)
            grad_pairing = grad_pairing + grad_mixing * decays * size_t[h : h + 1]
            by_size = grad_mixing * inner_part
            size_rows.append(jnp.sum(by_size, axis=0, keepdims=True))
            row_sum = jnp.sum(by_size * size_t[h : h + 1], axis=1, keepdims=True)
            row_sums = jnp.where(lane == h, row_sum, row_sums)
        grad_mixed[:, at] += jnp.where(lane < SSM_DIM, found[0], found[1])
    size_rows.append(jnp.zeros((128 - SSM_HEADS, rows), jnp.float32))
    grad_size = jnp.concatenate(size_rows, axis=0).T
    grad_sums = row_sums - size * grad_size
    grad_size = grad_size + grad_tail * tail_decay
    by_tail = grad_tail * tail
    grad_sums = grad_sums - by_tail + grad_entering * entering[...]
    grad_last = jnp.sum(by_tail, axis=0, keepdims=True) + grad_block * (
        jnp.exp(last) * masks[0:1, 5:6]
    )
    row = lax.broadcasted_iota(jnp.int32, (rows, 128), 0)
    grad_sums = grad_sums + jnp.where(row == rows - 1, grad_last, 0.0)
    grad_log = exact(lower_ones(rows), grad_sums, ((0,), (0,)))
    rate = table[9:10, 0:128]
    grad_size = grad_size - rate * grad_log
    raw = steps[...] + table[8:9, 0:128]
    grad_raw = grad_size / (1.0 + jnp.exp(-raw))
    grad_steps[...] = grad_raw
    grad_heads[...] = jnp.concatenate(
        [
            jnp.sum(grad_raw, axis=0, keepdims=True),
            jnp.sum(-grad_log * size * rate, axis=0, keepdims=True),
            grad_skip,
            jnp.zeros((5, 128), jnp.float32),
        ],
        axis=0,
    )
    grad_pairing = grad_pairing.astype(low)
    grad_mixed[:, WIDTH : WIDTH + STATE] = grad_input + down(grad_pairing, output_map.astype(low))
    grad_mixed[:, WIDTH + STATE :] = grad_output + jnp.dot(
        grad_pairing, input_map.astype(low), preferred_element_type=jnp.float32
    )

    extended[0:8] = rim[...]
    extended[8:] = inner[...]
    grad_ext[...] = jnp.zeros_like(grad_ext)
    for piece in range(CONV_WIDTH // 256):
        at = slice(piece * 256, piece * 256 + 256)
        total = conv_sum(extended, masks, table, at)
        sig = 1.0 / (1.0 + jnp.exp(-total))
        grad_total = grad_mixed[:, at] * sig * (1.0 + total * (1.0 - sig))
        taps = []
        for tap in range(CONV):
            first = TAP_ROWS + tap
            kept = grad_total * masks[:, tap : tap + 1] if tap < CONV - 1 else grad_total
            taps.append(jnp.sum(kept * extended[first : first + rows, at], axis=0, keepdims=True))
            grad_ext[first : first + rows, at] += table[tap : tap + 1, at] * kept
        taps.append(jnp.sum(grad_total, axis=0, keepdims=True))
        taps.append(jnp.zeros((8 - CONV - 1, 256), jnp.float32))
        grad_conv[:, at] = jnp.concatenate(taps, axis=0)
    grad_rim[...] = grad_ext[0:8]
    grad_inner[...] = grad_ext[8:]


def dot_rows(left, right):
    return down(left, right).astype(jnp.bfloat16)


class Sums:
    def __init__(self, net, kinds, here, near, core, came, summed, own=None):
        self.net, self.kinds, self.here, self.near, self.core = net, kinds, here, near, core
        self.came, self.summed, self.own = came, summed, own
        self.pending = [None, None, None]

    def refs(self, part, stage, fixed, at):
        index = index_of(ORDERS[part][stage:], fixed, at)
        if stage:
            return [ref.at[index] for ref in self.summed[part, stage - 1]]
        return [
            ref.at[(*index, *(span(pair) for pair in CUTS[kind][part]))]
            for kind, ref in zip(self.kinds, self.own)
        ]

    def early(self, e, send_sem, recv_sem):
        at = {**self.here, "x": (self.here["x"] + e + 1) % 4}
        return [
            pltpu.make_async_remote_copy(
                src_ref=src,
                dst_ref=dst.at[e],
                send_sem=send_sem.at[len(self.kinds) * e + k],
                recv_sem=recv_sem.at[len(self.kinds) * e + k],
                device_id=device_of(at, self.core),
                device_id_type=MESH,
            )
            for k, (src, dst) in enumerate(
                zip(self.refs(0, 0, ("x",), at), self.came[0, 0])
            )
        ]

    def send(self, part, stage):
        dim = ORDERS[part][stage]
        self.pending[part] = [
            self.net.push(src, dst.at[e], device_of(at, self.core))
            for e, at in enumerate(self.near[dim])
            for src, dst in zip(self.refs(part, stage, (dim,), at), self.came[part, stage])
        ]

    def wait(self, part):
        for copy in self.pending[part] or ():
            copy.wait_recv()

    def add_up(self, part, stage):
        kept, rest = ORDERS[part][stage:], ORDERS[part][stage + 1 :]

        def unit(number, nothing):
            at, left = dict(self.here), number
            for axis, axis_dim in reversed(AXES):
                if axis_dim in rest:
                    at[axis] = left % EXTENT[axis]
                    left = left // EXTENT[axis]
            inner = index_of(rest, rest, at)
            own_refs = self.refs(part, stage, kept, at)
            for own, came, out in zip(
                own_refs, self.came[part, stage], self.summed[part, stage]
            ):
                total = own[...].astype(jnp.float32)
                for e in range(3):
                    total = total + came[(e, *inner)].astype(jnp.float32)
                out[inner if inner else Ellipsis] = total.astype(jnp.bfloat16)
            return nothing

        count = 1
        for size in extents(rest):
            count *= size
        if count == 1:
            unit(0, 0)
        else:
            lax.fori_loop(0, count, unit, 0)


def piece_shapes(kinds, part):
    return [
        tuple(pair[1] - pair[0] for pair in CUTS[kind][part]) for kind in kinds
    ]


def came_shapes(kinds, part, stage):
    rest = extents(ORDERS[part][stage + 1 :])
    return [(3, *rest, *shape) for shape in piece_shapes(kinds, part)]


def summed_shapes(kinds, part, stage):
    rest = extents(ORDERS[part][stage + 1 :])
    return [(*rest, *shape) for shape in piece_shapes(kinds, part)]


def stage_keys(stages):
    return [(part, stage) for part in range(3) for stage in stages]


def take(refs, keys, kinds):
    found = {}
    for key in keys:
        found[key], refs = refs[: len(kinds)], refs[len(kinds) :]
    return found, refs


def low_scratch(shapes):
    return [pltpu.VMEM(dims, jnp.bfloat16) for dims in shapes]


def half_of(core, kind):
    return pl.ds(pl.multiple_of(core * HALVES[kind], 128), HALVES[kind])


LATE = ("two", "three")


def backward_body(
    grad,
    mixed,
    entering,
    decays,
    query,
    grad_out,
    kv_all,
    hidden_mask,
    log_total,
    norm,
    grads_two,
    acts_attn,
    acts_mixer,
    acts_hidden,
    grads_three,
    carried,
    cumulative,
    sizes,
    inner,
    rim,
    steps,
    masks,
    intra,
    table,
    cosine,
    sine,
    grad_z,
    grads_one,
    grad_conv,
    grad_heads,
    out_two,
    out_three,
    *rest,
):
    came, rest = take(rest, stage_keys(range(3)), LATE)
    summed, rest = take(rest, stage_keys(range(3)), LATE)
    states, parts, carries, came_back, terms, term_parts = rest[:6]
    both_norm, both_two, both_act, both_three, own_two, own_three = rest[6:12]
    key_sum, value_sum, wide_states, leaving, grad_query, grad_inner, grad_rim, rim_back = rest[12:20]
    extended, grad_ext, grad_mixed, grad_steps, send_sem, recv_sem = rest[20:]
    here, core = coordinates()
    near = neighbours(here, core)
    c = at_ctx(here["y"], here["zl"], core)
    peers = ctx_peers(c)
    meet(peers + all_near(near, core))
    net = Sender(send_sem.at[pl.ds(6, 100)], recv_sem.at[pl.ds(6, 100)])
    sibling = device_of(here, 1 - core)
    toks = norm.shape[0]
    mine, theirs = pl.ds(0, toks), pl.ds(toks, toks)
    other = 1 - core
    output_map = mixed[:, WIDTH + STATE :].astype(jnp.bfloat16)
    wide_states[...] = down(
        output_map, (expand(entering[...]) * grad[...]).astype(jnp.bfloat16)
    )
    pack(wide_states, states)
    copies = [
        net.push(states.at[(c + e + 1) % CTX], parts.at[c], peer) for e, peer in enumerate(peers)
    ]
    first = [
        net.push(norm, both_norm.at[theirs], sibling),
        net.push(grads_two.at[:, half_of(other, "two")], both_two.at[theirs], sibling),
        net.push(acts_attn, both_act.at[theirs, pl.ds(0, 512)], sibling),
        net.push(acts_mixer, both_act.at[theirs, pl.ds(512, 1536)], sibling),
        net.push(acts_hidden, both_act.at[theirs, pl.ds(2048, 2048)], sibling),
        net.push(grads_three.at[:, :, half_of(other, "three")], both_three.at[:, theirs], sibling),
    ]
    both_norm[mine] = norm[...]
    both_two[mine] = grads_two[:, half_of(core, "two")]
    both_act[mine, 0:512] = acts_attn[...]
    both_act[mine, 512:2048] = acts_mixer[...]
    both_act[mine, 2048:4096] = acts_hidden[...]
    both_three[:, mine] = grads_three[:, :, half_of(core, "three")]
    parts[c] = states[c]
    for copy in copies:
        copy.wait_recv()
    scan_rows(range(CTX - 1, -1, -1), decays, parts, carries)
    back = send_back(net, c, peers, carries, came_back)
    for copy in first:
        copy.wait_recv()

    def block(owner_x):
        features = both_norm[:, pl.ds(pl.multiple_of(owner_x * 256, 256), 256)]
        wide = HALVES["two"] // 2
        for piece in range(2):
            at = pl.ds(piece * wide, wide)
            found = dot_rows(features, both_two[:, at])
            for unit in range(16):
                own_two[owner_x, unit // 8, unit // 2 % 4, unit % 2, :, at] = found[
                    unit * 16 : unit * 16 + 16
                ]
        found = []
        for source, (start, size) in enumerate(((0, 128), (512, 384), (2048, 512))):
            at = pl.ds(pl.multiple_of(start + owner_x * size, 128), size)
            found.append(dot_rows(both_act[:, at], both_three[source]))
        for owner_z in range(2):
            for unit in range(8):
                source = 0 if unit < 1 else 1 if unit < 4 else 2
                at = (unit - (0, 1, 4)[source]) * 64 + owner_z * (64, 192, 256)[source]
                own_three[owner_x, owner_z, unit // 2, unit % 2] = found[source][at : at + 64]

    sums = Sums(net, LATE, here, near, core, came, summed, (own_two, own_three))

    def turn(e, nothing):
        block((here["x"] + e + 1) % 4)
        for copy in sums.early(e, send_sem, recv_sem):
            copy.start()
        return nothing

    lax.fori_loop(0, 3, turn, 0)
    block(here["x"])
    sums.send(1, 0)
    sums.send(2, 0)
    key_sum[...] = jnp.zeros_like(key_sum)
    value_sum[...] = jnp.zeros_like(value_sum)

    def head(h, nothing):
        keys = kv_all[:, :, 0:128].reshape(CTX * toks, 128)
        values = kv_all[:, :, 128:256].reshape(CTX * toks, 128)
        scores = across(query[h], keys) + hidden_mask[...]
        probs = jnp.exp(scores - log_total[h][:, 0:1])
        grad_probs = across(grad_out[h], values)
        inner_sum = jnp.sum(probs * grad_probs, axis=-1, keepdims=True)
        grad_scores = (probs * (grad_probs - inner_sum)).astype(jnp.bfloat16)
        grad_query[h] = jnp.dot(grad_scores, keys, preferred_element_type=jnp.float32)
        key_sum[...] += down(query[h], grad_scores)
        value_sum[...] += down(grad_out[h], probs.astype(jnp.bfloat16))
        return nothing

    lax.fori_loop(0, HEADS, head, 0)
    for k in range(CTX):
        at = pl.ds(k * toks, toks)
        terms[k, 0:128] = key_sum[:, at].astype(jnp.bfloat16)
        terms[k, 128:256] = value_sum[:, at].astype(jnp.bfloat16)
    key_copies = [
        net.push(terms.at[(c + e + 1) % CTX], term_parts.at[e], peer)
        for e, peer in enumerate(peers)
    ]
    for copy in back:
        copy.wait_recv()
    unpack(came_back, leaving)
    mixer_grads_body(
        grad,
        leaving,
        carried,
        mixed,
        cumulative,
        sizes,
        entering,
        inner,
        rim,
        steps,
        masks,
        intra,
        table,
        grad_inner,
        grad_rim,
        grad_steps,
        grad_conv,
        grad_heads,
        extended,
        grad_ext,
        grad_mixed,
    )
    rim_copy = net.push(grad_rim, rim_back, peers[-1])
    for e in range(3):
        for copy in sums.early(e, send_sem, recv_sem):
            copy.wait_recv()
    for part in range(3):
        sums.wait(part)
        sums.add_up(part, 0)
        sums.send(part, 1)

    def turn_back(both):
        return both * cosine[...] - swap_quarters(both) * sine[...]

    low = jnp.bfloat16
    for j in range(HEADS // 2):
        grads_one[:, 128 * j : 128 * j + 128] = (
            turn_back(join_pair(grad_query, j)) * HEAD_DIM ** (-0.5)
        ).astype(low)
    for copy in key_copies:
        copy.wait_recv()
    collected = terms[c].astype(jnp.float32)
    for e in range(CTX - 1):
        collected = collected + term_parts[e].astype(jnp.float32)
    key_at = HEADS * HEAD_DIM
    grads_one[:, key_at : key_at + 128] = (turn_back(collected[0:128].T) * key_scale).astype(low)
    grads_one[:, key_at + 128 : Z_AT] = collected[128:256].T.astype(low)
    grads_one[:, Z_AT:INNER_AT] = grad_z[...]
    rim_copy.wait_recv()
    grad_inner[toks - 8 :] = grad_inner[toks - 8 :] + rim_back[...]
    grads_one[:, INNER_AT:STEP_AT] = grad_inner[...].astype(low)
    grads_one[:, STEP_AT : STEP_AT + 128] = grad_steps[...].astype(low)
    grads_one[:, PAD_AT:COLS] = jnp.zeros((toks, COLS - PAD_AT), low)
    for part in range(3):
        sums.wait(part)
        sums.add_up(part, 1)
        sums.send(part, 2)
    for part in range(3):
        sums.wait(part)
        sums.add_up(part, 2)
        for kind, out, ref in zip(LATE, (out_two, out_three), summed[part, 2]):
            out[tuple(span(pair) for pair in CUTS[kind][part])] = ref[...]
    for e in range(3):
        for copy in sums.early(e, send_sem, recv_sem):
            copy.wait_send()
    net.drain()


def backward(*ins):
    low, f32 = jnp.bfloat16, jnp.float32
    rows = ins[0].shape[0]
    scratch = [shape for key in stage_keys(range(3)) for shape in came_shapes(LATE, *key)]
    scratch += [shape for key in stage_keys(range(3)) for shape in summed_shapes(LATE, *key)]
    scratch += [
        *[(CTX, 16, HALF_WIDTH)] * 4,
        (CTX, 256, rows),
        (CTX - 1, 256, rows),
        (2 * rows, 1024),
        (2 * rows, HALVES["two"]),
        (2 * rows, 4096),
        (3, 2 * rows, HALVES["three"]),
        (4, 2, 4, 2, 16, HALVES["two"]),
        (4, 2, 4, 2, 64, HALVES["three"]),
    ]
    wide = [
        (128, CTX * rows),
        (128, CTX * rows),
        (STATE, WIDTH),
        (STATE, WIDTH),
        (HEADS, rows, 128),
        (rows, CONV_WIDTH),
        (8, CONV_WIDTH),
        (8, CONV_WIDTH),
        (rows + 8, CONV_WIDTH),
        (rows + 8, CONV_WIDTH),
        (rows, CONV_WIDTH),
        (rows, 128),
    ]
    return call_kernel(
        backward_body,
        "backward",
        3,
        (
            shape_of((rows, COLS), low),
            shape_of((8, CONV_WIDTH), f32),
            shape_of((8, 128), f32),
            shape_of((16, HALVES["two"]), low),
            shape_of((64, HALVES["three"]), low),
        ),
        ins,
        106,
        [*low_scratch(scratch), *[pltpu.VMEM(dims, f32) for dims in wide]],
    )


FIRST = ("one",)


def weight_grads_body(
    norm, grads_one, small, unit_two, unit_three, out_one, out_two, out_three, *rest
):
    came, rest = take(rest, stage_keys(range(3)), FIRST)
    summed, rest = take(rest, stage_keys(range(3)), FIRST)
    both_norm, both_one, own_one, small_in, send_sem, recv_sem = rest
    here, core = coordinates()
    near = neighbours(here, core)
    toks = norm.shape[0]
    sibling = device_of(here, 1 - core)
    meet(all_near(near, core) + [sibling])
    net = Sender(send_sem.at[pl.ds(3, 42)], recv_sem.at[pl.ds(3, 42)])
    mine, theirs = pl.ds(0, toks), pl.ds(toks, toks)
    first = [
        net.push(norm, both_norm.at[theirs], sibling),
        net.push(grads_one.at[:, half_of(1 - core, "one")], both_one.at[theirs], sibling),
        net.push(small, small_in, sibling),
    ]
    both_norm[mine] = norm[...]
    both_one[mine] = grads_one[:, half_of(core, "one")]
    over_z = device_of({**here, "zl": 1 - here["zl"]}, core)
    y, low_z = here["y"], here["zl"]
    late = {"two": out_two, "three": out_three}
    out_two[y, low_z, :, half_of(core, "two")] = unit_two[...]
    out_three[y, low_z, :, half_of(core, "three")] = unit_three[...]

    def pass_on(kind, ref, at_y, at_z, targets):
        piece = ref.at[at_y, at_z, :, half_of(core, kind)]
        return [net.push(piece, piece, target) for target in targets]

    def late_step(at_y, at_z, targets):
        return [
            copy
            for kind, ref in late.items()
            for copy in pass_on(kind, ref, at_y, at_z, targets)
        ]

    to_y = [device_of(at, core) for at in near["y"]]
    late_copies = late_step(y, low_z, [over_z])
    for copy in first:
        copy.wait_recv()

    def block(owner_x, owner_z):
        owner = owner_x * 2 + owner_z
        features = both_norm[:, pl.ds(pl.multiple_of(owner * 128, 128), 128)]
        for low_at, high_at in ((0, 1024), (1024, 2176)):
            found = dot_rows(features, both_one[:, low_at:high_at])
            for unit in range(8):
                rows = found[unit * 16 : unit * 16 + 16]
                if unit == 0 and low_at:
                    extra = (small[owner] + small_in[owner]) * core.astype(jnp.float32)
                    tail = rows[:, 1024:].astype(jnp.float32) + extra
                    rows = jnp.concatenate([rows[:, :1024], tail.astype(jnp.bfloat16)], axis=1)
                own_one[owner_x, owner_z, unit // 2, unit % 2, :, low_at:high_at] = rows

    sums = Sums(net, FIRST, here, near, core, came, summed, (own_one,))

    def turn(e, nothing):
        owner_x = (here["x"] + e + 1) % 4
        block(owner_x, 0)
        block(owner_x, 1)
        for copy in sums.early(e, send_sem, recv_sem):
            copy.start()
        return nothing

    lax.fori_loop(0, 3, turn, 0)

    def own_turn(owner_z, nothing):
        block(here["x"], owner_z)
        return nothing

    lax.fori_loop(0, 2, own_turn, 0)
    sums.send(1, 0)
    sums.send(2, 0)
    for copy in late_copies:
        copy.wait_recv()
    late_copies = late_step(y, slice(None), to_y)
    for e in range(3):
        for copy in sums.early(e, send_sem, recv_sem):
            copy.wait_recv()
    for stage in range(3):
        for part in range(3):
            sums.wait(part)
            sums.add_up(part, stage)
            if stage < 2:
                sums.send(part, stage + 1)
        if stage == 1:
            for copy in late_copies:
                copy.wait_recv()
            late_copies = late_step(slice(None), slice(None), [sibling])
    for part in range(3):
        rows, cols = cut_of("one", part, core)
        out_one[y, low_z, rows, cols] = summed[part, 2][0][...]
    for step in (
        (y, low_z, [over_z]),
        (y, slice(None), to_y),
        (slice(None), slice(None), [sibling]),
    ):
        for copy in pass_on("one", out_one, *step):
            copy.wait_recv()
    for copy in late_copies:
        copy.wait_recv()
    for e in range(3):
        for copy in sums.early(e, send_sem, recv_sem):
            copy.wait_send()
    net.drain()


def sum_weight_grads(norm, grads_one, small, unit_two, unit_three):
    toks = norm.shape[0]
    low = jnp.bfloat16
    scratch = [shape for key in stage_keys(range(3)) for shape in came_shapes(FIRST, *key)]
    scratch += [shape for key in stage_keys(range(3)) for shape in summed_shapes(FIRST, *key)]
    scratch += [
        (2 * toks, 1024),
        (2 * toks, HALVES["one"]),
        (4, 2, 4, 2, 16, HALVES["one"]),
    ]
    return call_kernel(
        weight_grads_body,
        "sum_weight_grads",
        5,
        tuple(
            shape_of((4, 2, UNIT_ROWS[kind], 2 * HALVES[kind]), low)
            for kind in ("one", "two", "three")
        ),
        (norm, grads_one, small, unit_two, unit_three),
        45,
        [*low_scratch(scratch), pltpu.VMEM(small.shape, jnp.float32)],
    )


def local(
    layer_input,
    segment_ids,
    norm_gain,
    w_query,
    w_key,
    w_value,
    w_attn_out,
    w_gate_z,
    w_inner,
    w_step,
    conv_weight,
    conv_bias,
    step_bias,
    decay_log,
    skip_gain,
    mixer_gain,
    w_mixer_out,
    ffn_gain,
    w_gate,
    w_up,
    w_down,
    out_grad,
):
    low = jnp.bfloat16
    tok_rows = layer_input.shape[1]
    ctx_here = lax.axis_index("ctx")
    first_pos = ctx_here * tok_rows
    seg_here = segment_ids[0]
    pos_here = first_pos + jnp.arange(tok_rows, dtype=jnp.int32)
    residual_in = layer_input[0].astype(jnp.float32)
    grad_final = out_grad[0].astype(jnp.float32)
    kv_width = KV_HEADS * HEAD_DIM
    q_width = HEADS * HEAD_DIM
    width_inner = SSM_HEADS * SSM_DIM
    conv_width = width_inner + 2 * STATE
    z_at = q_width + 2 * kv_width
    inner_at = z_at + width_inner
    step_at = inner_at + conv_width

    small = jnp.stack(
        [
            jnp.pad(row, (0, 256 - row.shape[0]))
            for row in (
                *conv_weight,
                conv_bias,
                mixer_gain,
                ffn_gain,
                norm_gain,
                step_bias,
                decay_log,
                skip_gain,
                *[jnp.zeros((256,), low)] * 5,
            )
        ]
    )
    in_one = jnp.concatenate(
        [w_query, w_key, w_value, w_gate_z, w_inner, jnp.pad(w_step, ((0, 0), (0, 232)))], axis=1
    )
    half_dim = HEAD_DIM // 2
    inverse = rope_base ** (-jnp.arange(half_dim, dtype=jnp.float32) / half_dim)
    angles = pos_here.astype(jnp.float32)[:, None] * inverse[None, :]
    cosine = jnp.tile(jnp.cos(angles), (1, 4))
    sine = jnp.sin(angles)
    sine = jnp.concatenate([-sine, sine, -sine, sine], axis=1)
    seg_early = jnp.concatenate([jnp.full((CONV - 1,), -2, jnp.int32), seg_here])
    seg_cols = jnp.stack([seg_early[k : k + tok_rows] for k in range(CONV)], axis=1)
    (
        normed_low,
        query,
        gate_z,
        inner_pre,
        steps,
        table,
        hidden_mask,
        masks,
        intra,
        kv_all,
        rim_got,
        mixed,
        cumulative,
        sizes,
        entering,
        carried,
        mixer_result,
        decays,
        attended,
        log_total,
        all_one,
        all_two,
        all_three,
    ) = forward(
        residual_in,
        cosine,
        sine,
        small,
        jnp.broadcast_to(segment_ids, (8, tok_rows)),
        jnp.pad(seg_cols, ((0, 0), (0, 128 - CONV))),
        in_one,
        jnp.concatenate([w_gate, w_up], axis=1),
        jnp.concatenate([w_attn_out, w_mixer_out, w_down], axis=0),
    )
    kv_all = kv_all.reshape(CTX, tok_rows, 256)
    full_one = all_one.reshape(FSDP * 128, COLS)
    (
        layer_out,
        grad_middle,
        attn_low,
        mixer_low,
        hidden_low,
        normed_two_low,
        grads_two,
        grads_three,
        grad_out_wide,
        grad_result,
        grad_z,
        grad_gain_two,
        grad_mixer_gain,
    ) = middle_part(
        residual_in,
        grad_final,
        attended,
        mixer_result,
        gate_z,
        table,
        all_two.reshape(FSDP * 128, 2 * HALVES["two"]),
        all_three.reshape(FSDP, OUT_ROWS, 2 * HALVES["three"]),
    )
    grad_gain_two, grad_mixer_gain = grad_gain_two[0], grad_mixer_gain[0]
    grads_one, grad_conv_all, grad_heads, unit_two, unit_three = backward(
        grad_result,
        mixed,
        entering,
        decays,
        query,
        grad_out_wide,
        kv_all,
        hidden_mask,
        log_total,
        normed_two_low,
        grads_two,
        attn_low,
        mixer_low,
        hidden_low,
        grads_three,
        carried,
        cumulative,
        sizes,
        inner_pre,
        rim_got,
        steps,
        masks,
        intra,
        table,
        cosine,
        sine,
        grad_z,
    )
    grad_conv, grad_conv_bias = grad_conv_all[:CONV], grad_conv_all[CONV]
    grad_step_bias = grad_heads[0, :SSM_HEADS]
    grad_decay = grad_heads[1, :SSM_HEADS]
    grad_skip = grad_heads[2, :SSM_HEADS]
    grad_normed_one = right_trans(grads_one, full_one)
    _, pull_one = jax.vjp(rms_scale, residual_in, table[7, : residual_in.shape[1]])
    grad_in_norm, grad_gain_one = pull_one(grad_normed_one)
    input_grad = grad_middle + grad_in_norm

    small_grads = jnp.concatenate(
        [
            grad_gain_one.reshape(FSDP, 128),
            grad_conv.reshape(CONV, FSDP, 224).transpose(1, 0, 2).reshape(FSDP, CONV * 224),
            grad_conv_bias.reshape(FSDP, 224),
            grad_step_bias.reshape(FSDP, 3),
            grad_decay.reshape(FSDP, 3),
            grad_skip.reshape(FSDP, 3),
            grad_mixer_gain.reshape(FSDP, 192),
            grad_gain_two.reshape(FSDP, 128),
            jnp.zeros((FSDP, 2048 - SMALL), jnp.float32),
        ],
        axis=1,
    ).reshape(FSDP, 16, 128)
    sum_one, sum_two, sum_three = sum_weight_grads(
        normed_low, grads_one, small_grads, unit_two, unit_three
    )
    one = sum_one.reshape(128, COLS).astype(jnp.float32)
    two = sum_two.reshape(128, 2 * HALVES["two"]).astype(jnp.float32)
    three = sum_three.reshape(OUT_ROWS, 2 * HALVES["three"]).astype(jnp.float32)
    tiny = one[0:16, PAD_AT:COLS].reshape(-1)
    return (
        layer_out[None],
        input_grad[None],
        tiny[0:128],
        one[:, :q_width],
        one[:, q_width : q_width + kv_width],
        one[:, q_width + kv_width : z_at],
        three[0:64],
        one[:, z_at:inner_at],
        one[:, inner_at:step_at],
        one[:, step_at : step_at + SSM_HEADS],
        tiny[128:1024].reshape(CONV, 224),
        tiny[1024:1248],
        tiny[1248:1251],
        tiny[1251:1254],
        tiny[1254:1257],
        tiny[1257:1449],
        three[64:256],
        tiny[1449:1577],
        two[:, : HALVES["two"]],
        two[:, HALVES["two"] :],
        three[256:512],
    )


def solution(mesh):
    in_specs = (
        P("fsdp", "ctx", None),
        P("fsdp", "ctx"),
        P("fsdp"),
        P("fsdp", None),
        P("fsdp", None),
        P("fsdp", None),
        P("fsdp", None),
        P("fsdp", None),
        P("fsdp", None),
        P("fsdp", None),
        P(None, "fsdp"),
        P("fsdp"),
        P("fsdp"),
        P("fsdp"),
        P("fsdp"),
        P("fsdp"),
        P("fsdp", None),
        P("fsdp"),
        P("fsdp", None),
        P("fsdp", None),
        P("fsdp", None),
        P("fsdp", "ctx", None),
    )
    out_specs = (
        P("fsdp", "ctx", None),
        P("fsdp", "ctx", None),
        P("fsdp"),
        P("fsdp", None),
        P("fsdp", None),
        P("fsdp", None),
        P("fsdp", None),
        P("fsdp", None),
        P("fsdp", None),
        P("fsdp", None),
        P(None, "fsdp"),
        P("fsdp"),
        P("fsdp"),
        P("fsdp"),
        P("fsdp"),
        P("fsdp"),
        P("fsdp", None),
        P("fsdp"),
        P("fsdp", None),
        P("fsdp", None),
        P("fsdp", None),
    )
    return jax.shard_map(local, mesh=mesh, in_specs=in_specs, out_specs=out_specs, check_vma=False)
```

```python
import jax
import jax.numpy as jnp
from jax import lax
from jax.experimental import pallas as pl
from jax.experimental.pallas import tpu as pltpu
from jax.sharding import PartitionSpec as P

HEADS = 8
KV_HEADS = 2
HEAD_DIM = 64
SSM_HEADS = 24
SSM_DIM = 64
STATE = 128
CONV = 4


epsilon = 1e-05
rope_base = 10000.0
key_scale = 0.5
attn_out_scale = 0.8
mixer_out_scale = 0.5
gate_scale = 0.75
down_scale = 0.8
masked_score = -1e30
highest = lax.Precision.HIGHEST


def matmul_f32(left_side, right_side):
    return jnp.dot(left_side, right_side, preferred_element_type=jnp.float32)


def right_trans(left_side, right_side):
    return lax.dot_general(
        left_side, right_side, (((1,), (1,)), ((), ())), preferred_element_type=jnp.float32
    )


def rms_scale(values, gain_vec):
    return (
        values * lax.rsqrt(jnp.mean(values * values, axis=-1, keepdims=True) + epsilon) * gain_vec
    )


MESH = pl.DeviceIdType.MESH
CTX = 16
FSDP = 8
COLS = 4352
PAD_AT = 4224
HALVES = {"one": 2176, "two": 2048, "three": 512}
UNIT_ROWS = {"one": 16, "two": 16, "three": 64}
ORDERS = (("x", "y", "z"), ("y", "z", "x"), ("z", "x", "y"))
CUTS = {
    "one": (((0, 16), (0, 768)), ((0, 16), (768, 1536)), ((0, 16), (1536, 2176))),
    "two": (((0, 16), (0, 256)), ((0, 16), (256, 1152)), ((0, 16), (1152, 2048))),
    "three": (((0, 32), (0, 512)), ((32, 48), (0, 512)), ((48, 64), (0, 512))),
}
OUT_ROWS = 512
EVERYTHING = ("x", "y", "z")
SMALL = 1577
WIDTH = SSM_DIM * SSM_HEADS
HALF_WIDTH = WIDTH // 2
CONV_WIDTH = WIDTH + 2 * STATE
VMEM_LIMIT = 60 * 2**20


def place():
    f, c = lax.axis_index("fsdp"), lax.axis_index("ctx")
    return f, c, c // 4, (c // 2) % 2, c % 2


def at_ctx(y, low_z, core):
    return (y * 2 + low_z) * 2 + core


def meet(partners):
    barrier = pltpu.get_barrier_semaphore()
    for partner in partners:
        pl.semaphore_signal(barrier, inc=1, device_id=partner, device_id_type=MESH)
    pl.semaphore_wait(barrier, len(partners))


class Sender:
    def __init__(self, send_sem, recv_sem):
        self.send_sem, self.recv_sem, self.used, self.all = send_sem, recv_sem, 0, []

    def push(self, src, dst, partner):
        index = self.used
        self.used += 1
        copy = pltpu.make_async_remote_copy(
            src_ref=src,
            dst_ref=dst,
            send_sem=self.send_sem.at[index],
            recv_sem=self.recv_sem.at[index],
            device_id=partner,
            device_id_type=MESH,
        )
        copy.start()
        self.all.append(copy)
        return copy

    def drain(self):
        for copy in self.all:
            copy.wait_send()


def call_kernel(body, name, cid, outs, ins, sems, scratch=(), far_in=(), far_out=(), aliases=None):
    def spec(far):
        return pl.BlockSpec(memory_space=pl.ANY if far else pltpu.VMEM)

    return pl.pallas_call(
        body,
        name=name,
        out_shape=outs,
        in_specs=[spec(k in far_in) for k in range(len(ins))],
        out_specs=tuple(spec(k in far_out) for k in range(len(outs))),
        scratch_shapes=[
            *scratch,
            pltpu.SemaphoreType.DMA((sems,)),
            pltpu.SemaphoreType.DMA((sems,)),
        ],
        input_output_aliases=aliases or {},
        compiler_params=pltpu.CompilerParams(
            collective_id=cid, has_side_effects=True, vmem_limit_bytes=VMEM_LIMIT
        ),
    )(*ins)


def shape_of(dims, kind):
    return jax.ShapeDtypeStruct(dims, kind)


AXES = (("x", "x"), ("zh", "z"), ("y", "y"), ("zl", "z"))
EXTENT = {"x": 4, "zh": 2, "y": 4, "zl": 2}


def coordinates():
    f, c, y, low_z, core = place()
    return {"x": f // 2, "zh": f % 2, "y": y, "zl": low_z}, core


def neighbours(here, core):
    z = here["zh"] * 2 + here["zl"]
    found = {"x": [], "y": [], "z": []}
    for e in range(1, 4):
        found["x"].append({**here, "x": (here["x"] + e) % 4})
        found["y"].append({**here, "y": (here["y"] + e) % 4})
        other = (z + e) % 4
        found["z"].append({**here, "zh": other // 2, "zl": other % 2})
    return found


def device_of(at, core):
    return {"fsdp": at["x"] * 2 + at["zh"], "ctx": at_ctx(at["y"], at["zl"], core)}


def index_of(kept, fixed, at):
    return tuple(
        at[axis] if axis_dim in fixed else slice(None)
        for axis, axis_dim in AXES
        if axis_dim in kept
    )


def extents(kept):
    return tuple(EXTENT[axis] for axis, axis_dim in AXES if axis_dim in kept)


def span(pair):
    return pl.ds(pair[0], pair[1] - pair[0])


def cut_of(kind, part, core):
    rows, cols = CUTS[kind][part]
    at = pl.multiple_of(core * HALVES[kind] + cols[0], 128)
    return span(rows), pl.ds(at, cols[1] - cols[0])


def all_near(near, core):
    return [device_of(at, core) for dim in EVERYTHING for at in near[dim]]


class Gather:
    def __init__(self, net, outs, here, near, core):
        self.net, self.outs, self.here, self.near, self.core = net, outs, here, near, core
        self.pending, self.crossing = [[], [], []], []
        self.sibling = device_of(here, 1 - core)

    def pieces(self, part, fixed, at):
        index = index_of(EVERYTHING, fixed, at)
        return [
            ref.at[(*index, *cut_of(kind, part, self.core))] for kind, ref in self.outs.items()
        ]

    def own(self, ins, sem):
        point = index_of(EVERYTHING, EVERYTHING, self.here)
        copies = []
        for k, (kind, ref) in enumerate(self.outs.items()):
            half = HALVES[kind]
            cols = pl.ds(pl.multiple_of(self.core * half, 128), half)
            copies.append(
                pltpu.make_async_copy(
                    ins[kind].at[self.here["y"], self.here["zl"], :, cols],
                    ref.at[(*point, slice(None), cols)],
                    sem.at[k],
                )
            )
        return copies

    def stage(self, number, ins=None):
        jobs = []
        for part, order in enumerate(ORDERS):
            steps = order[::-1]
            dim, fixed = steps[number], steps[number:]
            for copy in self.pending[part]:
                copy.wait_recv()
            refs = self.pieces(part, fixed, self.here)
            sources = refs
            if ins is not None:
                sources = [
                    ins[kind].at[
                        (self.here["y"], self.here["zl"], *cut_of(kind, part, self.core))
                    ]
                    for kind in self.outs
                ]
            jobs.append((self.near[dim], sources, refs))
            self.pending[part] = []
        for e in range(3):
            for part, (near, sources, refs) in enumerate(jobs):
                self.pending[part] += [
                    self.net.push(src, ref, device_of(near[e], self.core))
                    for src, ref in zip(sources, refs)
                ]
        if number == 2:
            for _, _, refs in jobs:
                self.crossing += [self.net.push(ref, ref, self.sibling) for ref in refs]

    def finish(self):
        kinds = len(self.outs)
        for e in range(3):
            for part, order in enumerate(ORDERS):
                for copy in self.pending[part][kinds * e : kinds * e + kinds]:
                    copy.wait_recv()
                source = self.near[order[0]][2 - e]
                self.crossing += [
                    self.net.push(ref, ref, self.sibling)
                    for ref in self.pieces(part, (order[0],), source)
                ]
        for copy in self.crossing:
            copy.wait_recv()


def gather_shapes(kinds):
    return [
        shape_of((4, 2, 4, 2, UNIT_ROWS[kind], 2 * HALVES[kind]), jnp.bfloat16) for kind in kinds
    ]


TABLE = ((0, 5, 224), (5, 6, 192), (6, 8, 128), (8, 11, 3))


def ctx_peers(c):
    return [{"ctx": (c + e) % CTX} for e in range(1, CTX)]


def expand(per_head):
    rows = per_head.shape[0]
    lane = lax.broadcasted_iota(jnp.int32, (rows, 128), 1)
    return jnp.concatenate(
        [
            jnp.where(
                lane < SSM_DIM,
                jnp.broadcast_to(per_head[:, 2 * j : 2 * j + 1], (rows, 128)),
                jnp.broadcast_to(per_head[:, 2 * j + 1 : 2 * j + 2], (rows, 128)),
            )
            for j in range(SSM_HEADS // 2)
        ],
        axis=1,
    )


def pack(states, chunks):
    for k in range(CTX):
        rows = states[8 * k : 8 * k + 8]
        chunks[k] = jnp.concatenate([rows[:, :HALF_WIDTH], rows[:, HALF_WIDTH:]], axis=0).astype(
            jnp.bfloat16
        )


def unpack(chunks, states):
    for k in range(CTX):
        rows = chunks[k].astype(jnp.float32)
        states[8 * k : 8 * k + 8] = jnp.concatenate([rows[:8], rows[8:]], axis=1)


def scan_rows(order, decay_of, parts, carries):
    wide = expand(jnp.concatenate([decay_of[k, 0:1] for k in range(CTX)], axis=0))
    state = jnp.zeros((16, HALF_WIDTH), jnp.float32)
    for at in order:
        carries[at] = state.astype(jnp.bfloat16)
        decay = jnp.concatenate(
            [
                jnp.broadcast_to(wide[at : at + 1, :HALF_WIDTH], (8, HALF_WIDTH)),
                jnp.broadcast_to(wide[at : at + 1, HALF_WIDTH:], (8, HALF_WIDTH)),
            ],
            axis=0,
        )
        state = decay * state + parts[at].astype(jnp.float32)


def send_back(net, c, peers, carries, carried):
    copies = [
        net.push(carries.at[(c + e + 1) % CTX], carried.at[c], peer) for e, peer in enumerate(peers)
    ]
    carried[c] = carries[c]
    return copies


def across(left, right):
    return lax.dot_general(
        left, right, (((1,), (1,)), ((), ())), preferred_element_type=jnp.float32
    )


def down(left, right):
    return lax.dot_general(
        left, right, (((0,), (0,)), ((), ())), preferred_element_type=jnp.float32
    )


def masks_from(seg, seg_cols, seg_all, c, hidden_mask, masks, intra):
    rows = seg_cols.shape[0]
    row = lax.broadcasted_iota(jnp.int32, (rows, 128), 0)
    lane = lax.broadcasted_iota(jnp.int32, (rows, 128), 1)
    here = seg_cols[:, 3:4]
    before = jnp.where(c > 0, seg_all[(c + CTX - 1) % CTX][0:1], -1)
    found = jnp.zeros((rows, 128), jnp.float32)
    for tap in range(CONV - 1):
        earlier = jnp.broadcast_to(seg_cols[:, tap : tap + 1], (rows, 128))
        for t in range(CONV - 1 - tap):
            at = 125 + t + tap
            earlier = jnp.where(row == t, before[:, at : at + 1], earlier)
        found = jnp.where((lane == tap) & (earlier == here), 1.0, found)
    last, prior = seg[0:1, 127:128], before[:, 127:128]
    found = jnp.where((lane == 3) & (here == prior), 1.0, found)
    found = jnp.where((lane == 4) & (here == last), 1.0, found)
    masks[...] = jnp.where((lane == 5) & (last == prior), 1.0, found)
    intra[...] = jnp.where((row >= lane) & (here == seg[0:1]), 1.0, 0.0)
    for k in range(CTX):
        seen = (here == seg_all[k][0:1]) & (lane + k * rows <= row + c * rows)
        hidden_mask[:, k * rows : (k + 1) * rows] = jnp.where(seen, 0.0, masked_score)


def forward_body(
    row_in,
    cosine,
    sine,
    small,
    seg,
    seg_cols,
    in_one,
    in_two,
    in_three,
    norm_low,
    query,
    gate_z,
    inner,
    steps,
    table,
    hidden_mask,
    masks,
    intra,
    kv_all,
    rim_all,
    mixed,
    cumulative,
    sizes,
    entering,
    carried,
    result,
    decays,
    attended,
    log_total,
    out_one,
    out_two,
    out_three,
    kv,
    got_small,
    seg_all,
    states,
    inside,
    extended,
    wide_states,
    parts,
    carries,
    came_back,
    decay,
    own_sem,
    send_sem,
    recv_sem,
):
    here, core = coordinates()
    near = neighbours(here, core)
    y, low_z = here["y"], here["zl"]
    c = at_ctx(y, low_z, core)
    f = here["x"] * 2 + here["zh"]
    peers = ctx_peers(c)
    rows = row_in.shape[0]
    small_peers = [{"fsdp": (f + d) % FSDP} for d in range(1, FSDP)]
    meet(
        peers
        + all_near(near, core)
        + [{"fsdp": (here["x"] + e) % 4 * 2 + 1 - here["zh"]} for e in range(1, 4)]
    )
    net = Sender(send_sem, recv_sem)
    early = Gather(net, {"one": out_one}, here, near, core)
    early.stage(0, {"one": in_one})
    tiny = [net.push(small, got_small.at[f], peer) for peer in small_peers]
    tiny += [net.push(seg, seg_all.at[c], peer) for peer in peers]
    ins = {"two": in_two, "three": in_three}
    late = Gather(net, {"two": out_two, "three": out_three}, here, near, core)
    own = early.own({"one": in_one}, own_sem.at[pl.ds(0, 1)])
    own_late = late.own(ins, own_sem.at[pl.ds(1, 2)])
    for copy in own + own_late:
        copy.start()
    got_small[f] = small[...]
    seg_all[c] = seg[...]
    for copy in own:
        copy.wait()
    early.stage(1)
    early.stage(2)
    late.stage(0, ins)
    for copy in tiny:
        copy.wait_recv()
    table[...] = jnp.zeros_like(table)
    for k in range(FSDP):
        piece = got_small[k].astype(jnp.float32)
        for first, last, width in TABLE:
            table[first:last, k * width : k * width + width] = piece[first:last, :width]
    table[9:10] = jnp.exp(table[9:10])
    table[11:12, :WIDTH] = expand(table[10:11, 0:128])
    masks_from(seg, seg_cols, seg_all, c, hidden_mask, masks, intra)
    early.finish()
    for copy in own_late:
        copy.wait()
    late.stage(1)
    project_body(
        row_in, table, cosine, sine, out_one, norm_low, query, kv, gate_z, inner, steps
    )
    rim_copy = net.push(inner.at[pl.ds(rows - 8, 8)], rim_all, peers[0])
    over_z = device_of({**here, "zl": 1 - low_z}, core)
    sibling = device_of(here, 1 - core)
    kv_all[y, low_z, core] = kv[...]
    to_z = net.push(kv, kv_all.at[y, low_z, core], over_z)
    rim_copy.wait_recv()
    mixer_parts_body(
        inner,
        rim_all,
        steps,
        masks,
        intra,
        table,
        mixed,
        cumulative,
        sizes,
        states,
        decay,
        entering,
        inside,
        extended,
        wide_states,
    )
    copies = []
    for e, peer in enumerate(peers):
        copies.append(net.push(states.at[(c + e + 1) % CTX], parts.at[c], peer))
        copies.append(net.push(decay, decays.at[c], peer))
    parts[c] = states[c]
    decays[c] = decay[...]
    to_z.wait_recv()
    pair = kv_all.at[y, :, core]
    to_y = [net.push(pair, pair, device_of(at, core)) for at in near["y"]]
    for copy in to_y:
        copy.wait_recv()
    whole = kv_all.at[:, :, core]
    net.push(whole, whole, sibling).wait_recv()

    def head(h, nothing):
        keys = kv_all[:, :, :, :, 0:128].reshape(CTX * rows, 128)
        values = kv_all[:, :, :, :, 128:256].reshape(CTX * rows, 128)
        scores = across(query[h], keys) + hidden_mask[...]
        row_max = jnp.max(scores, axis=-1, keepdims=True)
        weights = jnp.exp(scores - row_max)
        row_sum = jnp.sum(weights, axis=-1, keepdims=True)
        probs = (weights * (1.0 / row_sum)).astype(jnp.bfloat16)
        attended[h] = jnp.dot(probs, values, preferred_element_type=jnp.float32).astype(
            jnp.bfloat16
        )
        log_total[h] = jnp.broadcast_to(row_max + jnp.log(row_sum), (rows, 128))
        return nothing

    for copy in copies:
        copy.wait_recv()
    scan_rows(range(CTX), decays, parts, carries)
    back = send_back(net, c, peers, carries, came_back)
    late.stage(2)
    lax.fori_loop(0, HEADS, head, 0)
    for copy in back:
        copy.wait_recv()
    unpack(came_back, carried)
    output_map = mixed[:, WIDTH + STATE :].astype(jnp.bfloat16)
    result[...] = inside[...] + expand(entering[...]) * jnp.dot(
        output_map, carried[...].astype(jnp.bfloat16), preferred_element_type=jnp.float32
    )
    late.finish()
    net.drain()


def forward(row_in, cosine, sine, small, seg, seg_cols, one, two, three):
    rows, dim = row_in.shape
    f32, low = jnp.float32, jnp.bfloat16
    return call_kernel(
        forward_body,
        "forward",
        1,
        (
            shape_of((rows, dim), low),
            shape_of((HEADS, rows, 128), low),
            shape_of((rows, WIDTH), f32),
            shape_of((rows, CONV_WIDTH), f32),
            shape_of((rows, 128), f32),
            shape_of((16, CONV_WIDTH), f32),
            shape_of((rows, CTX * rows), f32),
            shape_of((rows, 128), f32),
            shape_of((rows, rows), f32),
            shape_of((4, 2, 2, rows, 256), low),
            shape_of((8, CONV_WIDTH), f32),
            shape_of((rows, CONV_WIDTH), f32),
            shape_of((rows, 128), f32),
            shape_of((rows, 128), f32),
            shape_of((rows, 128), f32),
            shape_of((STATE, WIDTH), f32),
            shape_of((rows, WIDTH), f32),
            shape_of((CTX, 8, 128), f32),
            shape_of((HEADS, rows, 128), low),
            shape_of((HEADS, rows, 128), f32),
            *gather_shapes(["one", "two", "three"]),
        ),
        (
            row_in,
            cosine,
            sine,
            small,
            seg,
            seg_cols,
            one.reshape(4, 2, 16, 2 * HALVES["one"]),
            two.reshape(4, 2, 16, 2 * HALVES["two"]),
            three.reshape(4, 2, 64, 2 * HALVES["three"]),
        ),
        190,
        (
            pltpu.VMEM((rows, 256), low),
            pltpu.VMEM((FSDP, 16, 256), low),
            pltpu.VMEM((CTX, 8, 128), jnp.int32),
            pltpu.VMEM((CTX, 16, HALF_WIDTH), low),
            pltpu.VMEM((rows, WIDTH), f32),
            pltpu.VMEM((rows + 8, CONV_WIDTH), f32),
            pltpu.VMEM((STATE, WIDTH), f32),
            *[pltpu.VMEM((CTX, 16, HALF_WIDTH), low)] * 3,
            pltpu.VMEM((8, 128), f32),
            pltpu.SemaphoreType.DMA((3,)),
        ),
        (6, 7, 8),
        (21, 22),
    )


def plain_kernel(body, name, outs, ins, scratch=()):
    return pl.pallas_call(
        body,
        name=name,
        out_shape=outs,
        in_specs=[pl.BlockSpec(memory_space=pltpu.VMEM)] * len(ins),
        out_specs=tuple(pl.BlockSpec(memory_space=pltpu.VMEM) for _ in outs),
        scratch_shapes=list(scratch),
        compiler_params=pltpu.CompilerParams(vmem_limit_bytes=VMEM_LIMIT),
    )(*ins)


TAP_ROWS = 8 - CONV + 1


def conv_sum(extended, masks, conv_par, at):
    rows = masks.shape[0]
    total = jnp.broadcast_to(conv_par[CONV : CONV + 1, at], (rows, conv_par[0:1, at].shape[1]))
    for tap in range(CONV):
        first = TAP_ROWS + tap
        term = conv_par[tap : tap + 1, at] * extended[first : first + rows, at]
        total = total + (term * masks[:, tap : tap + 1] if tap < CONV - 1 else term)
    return total


def lower_ones(rows):
    at = lax.broadcasted_iota(jnp.int32, (rows, rows), 0)
    return (at >= lax.broadcasted_iota(jnp.int32, (rows, rows), 1)).astype(jnp.float32)


def exact(left, right, contract):
    return lax.dot_general(
        left,
        right,
        ((contract[0], contract[1]), ((), ())),
        precision=highest,
        preferred_element_type=jnp.float32,
    )


def swap_quarters(values):
    lane = lax.broadcasted_iota(jnp.int32, values.shape, 1)
    quarter = HEAD_DIM // 2
    ahead = jnp.concatenate([values[:, quarter:], values[:, :quarter]], axis=1)
    behind = jnp.concatenate([values[:, 128 - quarter :], values[:, : 128 - quarter]], axis=1)
    return jnp.where(lane % HEAD_DIM < quarter, ahead, behind)


def split_pair(both, j, out):
    lane = lax.broadcasted_iota(jnp.int32, both.shape, 1)
    turned = shift_half(both)
    low = jnp.bfloat16
    if j < HEADS // 4:
        out[2 * j] = jnp.where(lane < HEAD_DIM, both, 0.0).astype(low)
        out[2 * j + 1] = jnp.where(lane < HEAD_DIM, turned, 0.0).astype(low)
    else:
        out[2 * j] = jnp.where(lane < HEAD_DIM, 0.0, turned).astype(low)
        out[2 * j + 1] = jnp.where(lane < HEAD_DIM, 0.0, both).astype(low)


def join_pair(values, j):
    first, second = values[2 * j].astype(jnp.float32), values[2 * j + 1].astype(jnp.float32)
    if j < HEADS // 4:
        second = shift_half(second)
    else:
        first = shift_half(first)
    lane = lax.broadcasted_iota(jnp.int32, first.shape, 1)
    return jnp.where(lane < HEAD_DIM, first, second)


Z_AT = HEADS * HEAD_DIM + 2 * KV_HEADS * HEAD_DIM
INNER_AT = Z_AT + WIDTH
STEP_AT = INNER_AT + CONV_WIDTH


def project_body(row_in, table, cosine, sine, weights, norm_low, query, kv, gate_z, inner, steps):
    values = row_in[...]
    scale = lax.rsqrt(mean_last(values * values) + epsilon)
    normed = (values * scale * table[7:8, 0 : values.shape[1]]).astype(jnp.bfloat16)
    norm_low[...] = normed

    def part(first, last):
        piece = weights[:, :, :, :, :, first:last].reshape(values.shape[1], last - first)
        return jnp.dot(normed, piece, preferred_element_type=jnp.float32)

    def turn(both):
        return both * cosine[...] + swap_quarters(both) * sine[...]

    for j in range(HEADS // 2):
        split_pair(turn(part(128 * j, 128 * j + 128)) * HEAD_DIM ** (-0.5), j, query)
    key_at = HEADS * HEAD_DIM
    kv[:, 0:128] = (turn(part(key_at, key_at + 128)) * key_scale).astype(jnp.bfloat16)
    kv[:, 128:256] = part(key_at + 128, key_at + 256).astype(jnp.bfloat16)
    for at in range(0, WIDTH, 512):
        gate_z[:, at : at + 512] = part(Z_AT + at, Z_AT + at + 512)
    for at in range(0, CONV_WIDTH, 256):
        inner[:, at : at + 256] = part(INNER_AT + at, INNER_AT + at + 256)
    steps[...] = part(STEP_AT, STEP_AT + 128)


def mixer_parts_body(
    inner,
    rim,
    steps,
    masks,
    intra,
    table,
    mixed,
    cumulative,
    sizes,
    chunks,
    decay,
    entering,
    inside,
    extended,
    states,
):
    rows = inner.shape[0]
    low = jnp.bfloat16
    extended[0:8] = rim[...]
    extended[8:] = inner[...]
    for piece in range(CONV_WIDTH // 256):
        at = slice(piece * 256, piece * 256 + 256)
        total = conv_sum(extended, masks, table, at)
        mixed[:, at] = total / (1.0 + jnp.exp(-total))
    raw = steps[...] + table[8:9, 0:128]
    size = jnp.maximum(raw, 0.0) + jnp.log1p(jnp.exp(-jnp.abs(raw)))
    sums = exact(lower_ones(rows), -size * table[9:10, 0:128], ((1,), (0,)))
    cumulative[...] = sums
    sizes[...] = size
    last = sums[rows - 1 : rows]
    entering[...] = jnp.exp(sums) * masks[:, 3:4]
    decay[...] = jnp.broadcast_to(jnp.exp(last) * masks[0:1, 5:6], (8, 128))
    tail = masks[:, 4:5] * jnp.exp(last - sums) * size
    weighted = (expand(tail) * mixed[:, :WIDTH]).astype(low)
    input_map = mixed[:, WIDTH : WIDTH + STATE]
    output_map = mixed[:, WIDTH + STATE :]
    states[...] = down(input_map.astype(low), weighted)
    pack(states, chunks)
    pairing = exact(output_map, input_map, ((1,), (1,))) * intra[...]
    sums_t, size_t = sums.T, size.T
    lane = lax.broadcasted_iota(jnp.int32, (rows, 128), 1)
    for j in range(SSM_HEADS // 2):
        at = slice(128 * j, 128 * j + 128)
        values = mixed[:, at]
        found = []
        for h in (2 * j, 2 * j + 1):
            spread = jnp.minimum(sums[:, h : h + 1] - sums_t[h : h + 1], 0.0)
            mixing = (jnp.exp(spread) * pairing * size_t[h : h + 1]).astype(low)
            found.append(jnp.dot(mixing, values.astype(low), preferred_element_type=jnp.float32))
        inside[:, at] = jnp.where(lane < SSM_DIM, found[0], found[1]) + table[11:12, at] * values


def mean_last(values):
    return jnp.mean(values, axis=-1, keepdims=True)


def pair_of(weights, j, first, last):
    return jnp.concatenate([weights[2 * j, first:last], weights[2 * j + 1, first:last]], axis=0)


def shift_half(values):
    return jnp.concatenate([values[:, HEAD_DIM:], values[:, :HEAD_DIM]], axis=1)


def middle_body(
    row_in,
    row_grad,
    attended,
    result,
    gate_z,
    table,
    w_two,
    w_three,
    row_out,
    grad_middle,
    attn_low,
    mixer_low,
    hidden_low,
    norm_low,
    grads_two,
    grads_three,
    grad_out,
    grad_result,
    grad_z,
    grad_ffn_gain,
    grad_mixer_gain,
    down_sum,
    norm_sum,
    grad_flat,
):
    low, f32 = jnp.bfloat16, jnp.float32
    attn_sum = jnp.zeros(row_in.shape, f32)
    for j in range(HEADS // 2):
        both = join_pair(attended, j).astype(low)
        attn_low[:, 128 * j : 128 * j + 128] = both
        attn_sum = attn_sum + jnp.dot(
            both, pair_of(w_three, j, 0, 64), preferred_element_type=f32
        )
    z, mixed_out = gate_z[...], result[...]
    sig_z = 1.0 / (1.0 + jnp.exp(-z))
    flat = mixed_out * (z * sig_z)
    scale = lax.rsqrt(mean_last(flat * flat) + epsilon)
    normed = (flat * scale * table[5:6, 0:WIDTH]).astype(low)
    mixer_low[...] = normed
    mixer_sum = jnp.zeros(row_in.shape, f32)
    for j in range(4):
        mixer_sum = mixer_sum + jnp.dot(
            normed[:, 384 * j : 384 * j + 384],
            pair_of(w_three, j, 64, 256),
            preferred_element_type=f32,
        )
    middle = row_in[...] + attn_sum * attn_out_scale + mixer_sum * mixer_out_scale
    scale_two = lax.rsqrt(mean_last(middle * middle) + epsilon)
    norm_low[...] = (middle * scale_two * table[6:7, 0 : row_in.shape[1]]).astype(low)
    grad_down = (row_grad[...] * down_scale).astype(low)
    grads_three[2] = grad_down
    down_sum[...] = jnp.zeros_like(down_sum)
    norm_sum[...] = jnp.zeros_like(norm_sum)
    ff_width = FSDP * 256

    def chunk(f, nothing):
        at = pl.ds(pl.multiple_of(f * 256, 256), 256)
        at_up = pl.ds(pl.multiple_of(ff_width + f * 256, 256), 256)
        w_gate, w_up, w_down = w_two[:, at], w_two[:, at_up], w_three[f, 256:512]
        gate = jnp.dot(norm_low[...], w_gate, preferred_element_type=f32) * gate_scale
        up = jnp.dot(norm_low[...], w_up, preferred_element_type=f32)
        sig = 1.0 / (1.0 + jnp.exp(-gate))
        hidden = (gate * sig * up).astype(low)
        hidden_low[:, at] = hidden
        down_sum[...] += jnp.dot(hidden, w_down, preferred_element_type=f32)
        grad_hidden = across(grad_down, w_down)
        grad_gate = (
            grad_hidden * up * sig * (1.0 + gate * (1.0 - sig)) * gate_scale
        ).astype(low)
        grad_up = (grad_hidden * gate * sig).astype(low)
        grads_two[:, at] = grad_gate
        grads_two[:, at_up] = grad_up
        norm_sum[...] += across(grad_gate, w_gate) + across(grad_up, w_up)
        return nothing

    lax.fori_loop(0, FSDP, chunk, 0)
    row_out[...] = (middle + down_sum[...] * down_scale).astype(low)
    grad_norm = norm_sum[...]
    weighted = grad_norm * table[6:7, 0 : row_in.shape[1]]
    grad_mid = (
        row_grad[...]
        + scale_two * weighted
        - middle * (scale_two * scale_two * scale_two) * mean_last(middle * weighted)
    )
    grad_middle[...] = grad_mid
    grad_ffn_gain[...] = jnp.broadcast_to(
        jnp.sum(grad_norm * middle * scale_two, axis=0, keepdims=True), grad_ffn_gain.shape
    )
    grad_attn = (grad_mid * attn_out_scale).astype(low)
    grad_mix = (grad_mid * mixer_out_scale).astype(low)
    grads_three[0] = grad_attn
    grads_three[1] = grad_mix
    for j in range(HEADS // 2):
        split_pair(across(grad_attn, pair_of(w_three, j, 0, 64)), j, grad_out)
    for j in range(4):
        grad_flat[:, 384 * j : 384 * j + 384] = across(grad_mix, pair_of(w_three, j, 64, 256))
    grad_normed = grad_flat[...]
    weighted = grad_normed * table[5:6, 0:WIDTH]
    grad_mixer_gain[...] = jnp.broadcast_to(
        jnp.sum(grad_normed * flat * scale, axis=0, keepdims=True), grad_mixer_gain.shape
    )
    grad_gated = scale * weighted - flat * (scale * scale * scale) * mean_last(flat * weighted)
    grad_result[...] = grad_gated * (z * sig_z)
    grad_z[...] = (grad_gated * mixed_out * sig_z * (1.0 + z * (1.0 - sig_z))).astype(low)


def middle_part(row_in, row_grad, attended, result, gate_z, table, w_two, w_three):
    rows, dim = row_in.shape
    f32, low = jnp.float32, jnp.bfloat16
    return plain_kernel(
        middle_body,
        "middle_part",
        (
            shape_of((rows, dim), low),
            shape_of((rows, dim), f32),
            shape_of((rows, HEADS * HEAD_DIM), low),
            shape_of((rows, WIDTH), low),
            shape_of((rows, FSDP * 256), low),
            shape_of((rows, dim), low),
            shape_of((rows, 2 * FSDP * 256), low),
            shape_of((3, rows, dim), low),
            shape_of((HEADS, rows, 128), low),
            shape_of((rows, WIDTH), f32),
            shape_of((rows, WIDTH), low),
            shape_of((8, dim), f32),
            shape_of((8, WIDTH), f32),
        ),
        (row_in, row_grad, attended, result, gate_z, table, w_two, w_three),
        (
            pltpu.VMEM((rows, dim), f32),
            pltpu.VMEM((rows, dim), f32),
            pltpu.VMEM((rows, WIDTH), f32),
        ),
    )


def mixer_grads_body(
    grad,
    leaving,
    carried,
    mixed,
    cumulative,
    sizes,
    entering,
    inner,
    rim,
    steps,
    masks,
    intra,
    table,
    grad_inner,
    grad_rim,
    grad_steps,
    grad_conv,
    grad_heads,
    extended,
    grad_ext,
    grad_mixed,
):
    rows = inner.shape[0]
    low = jnp.bfloat16
    sums, size = cumulative[...], sizes[...]
    last = sums[rows - 1 : rows]
    input_map = mixed[:, WIDTH : WIDTH + STATE]
    output_map = mixed[:, WIDTH + STATE :]
    gather_head = (
        lax.broadcasted_iota(jnp.int32, (WIDTH, 128), 0) // SSM_DIM
        == lax.broadcasted_iota(jnp.int32, (WIDTH, 128), 1)
    ).astype(jnp.float32)

    def per_head(wide):
        return exact(wide, gather_head, ((1,), (0,)))

    tail_decay = masks[:, 4:5] * jnp.exp(last - sums)
    tail = tail_decay * size
    leaving_low, carried_low = leaving[...].astype(low), carried[...].astype(low)
    from_state = jnp.dot(input_map.astype(low), leaving_low, preferred_element_type=jnp.float32)
    to_output = jnp.dot(output_map.astype(low), carried_low, preferred_element_type=jnp.float32)
    wide_tail = expand(tail)
    values_all, grad_all = mixed[:, :WIDTH], grad[...]
    grad_tail = per_head(values_all * from_state)
    grad_entering = per_head(grad_all * to_output)
    grad_skip = per_head(jnp.sum(grad_all * values_all, axis=0, keepdims=True))
    grad_block = per_head(jnp.sum(leaving[...] * carried[...], axis=0, keepdims=True))
    grad_input = across((wide_tail * values_all).astype(low), leaving_low)
    grad_output = across((expand(entering[...]) * grad_all).astype(low), carried_low)
    grad_mixed[:, :WIDTH] = wide_tail * from_state + table[11:12, 0:WIDTH] * grad_all

    pairing = exact(output_map, input_map, ((1,), (1,)))
    sums_t, size_t = sums.T, size.T
    lane = lax.broadcasted_iota(jnp.int32, (rows, 128), 1)
    grad_pairing = jnp.zeros((rows, rows), jnp.float32)
    row_sums = jnp.zeros((rows, 128), jnp.float32)
    size_rows = []
    for j in range(SSM_HEADS // 2):
        at = slice(128 * j, 128 * j + 128)
        values, grads = mixed[:, at].astype(low), grad[:, at]
        found = []
        for h in (2 * j, 2 * j + 1):
            own_lanes = lane < SSM_DIM if h == 2 * j else lane >= SSM_DIM
            spread = jnp.minimum(sums[:, h : h + 1] - sums_t[h : h + 1], 0.0)
            decays = jnp.exp(spread) * intra[...]
            inner_part = decays * pairing
            mixing = inner_part * size_t[h : h + 1]
            found.append(down(mixing.astype(low), grads.astype(low)))
            grad_mixing = across(jnp.where(own_lanes, grads, 0.0).astype(low), values)
            grad_pairing = grad_pairing + grad_mixing * decays * size_t[h : h + 1]
            by_size = grad_mixing * inner_part
            size_rows.append(jnp.sum(by_size, axis=0, keepdims=True))
            row_sum = jnp.sum(by_size * size_t[h : h + 1], axis=1, keepdims=True)
            row_sums = jnp.where(lane == h, row_sum, row_sums)
        grad_mixed[:, at] += jnp.where(lane < SSM_DIM, found[0], found[1])
    size_rows.append(jnp.zeros((128 - SSM_HEADS, rows), jnp.float32))
    grad_size = jnp.concatenate(size_rows, axis=0).T
    grad_sums = row_sums - size * grad_size
    grad_size = grad_size + grad_tail * tail_decay
    by_tail = grad_tail * tail
    grad_sums = grad_sums - by_tail + grad_entering * entering[...]
    grad_last = jnp.sum(by_tail, axis=0, keepdims=True) + grad_block * (
        jnp.exp(last) * masks[0:1, 5:6]
    )
    row = lax.broadcasted_iota(jnp.int32, (rows, 128), 0)
    grad_sums = grad_sums + jnp.where(row == rows - 1, grad_last, 0.0)
    grad_log = exact(lower_ones(rows), grad_sums, ((0,), (0,)))
    rate = table[9:10, 0:128]
    grad_size = grad_size - rate * grad_log
    raw = steps[...] + table[8:9, 0:128]
    grad_raw = grad_size / (1.0 + jnp.exp(-raw))
    grad_steps[...] = grad_raw
    grad_heads[...] = jnp.concatenate(
        [
            jnp.sum(grad_raw, axis=0, keepdims=True),
            jnp.sum(-grad_log * size * rate, axis=0, keepdims=True),
            grad_skip,
            jnp.zeros((5, 128), jnp.float32),
        ],
        axis=0,
    )
    grad_pairing = grad_pairing.astype(low)
    grad_mixed[:, WIDTH : WIDTH + STATE] = grad_input + down(grad_pairing, output_map.astype(low))
    grad_mixed[:, WIDTH + STATE :] = grad_output + jnp.dot(
        grad_pairing, input_map.astype(low), preferred_element_type=jnp.float32
    )

    extended[0:8] = rim[...]
    extended[8:] = inner[...]
    grad_ext[...] = jnp.zeros_like(grad_ext)
    for piece in range(CONV_WIDTH // 256):
        at = slice(piece * 256, piece * 256 + 256)
        total = conv_sum(extended, masks, table, at)
        sig = 1.0 / (1.0 + jnp.exp(-total))
        grad_total = grad_mixed[:, at] * sig * (1.0 + total * (1.0 - sig))
        taps = []
        for tap in range(CONV):
            first = TAP_ROWS + tap
            kept = grad_total * masks[:, tap : tap + 1] if tap < CONV - 1 else grad_total
            taps.append(jnp.sum(kept * extended[first : first + rows, at], axis=0, keepdims=True))
            grad_ext[first : first + rows, at] += table[tap : tap + 1, at] * kept
        taps.append(jnp.sum(grad_total, axis=0, keepdims=True))
        taps.append(jnp.zeros((8 - CONV - 1, 256), jnp.float32))
        grad_conv[:, at] = jnp.concatenate(taps, axis=0)
    grad_rim[...] = grad_ext[0:8]
    grad_inner[...] = grad_ext[8:]


def dot_rows(left, right):
    return down(left, right).astype(jnp.bfloat16)


class Sums:
    def __init__(self, net, kinds, here, near, core, came, summed, own=None):
        self.net, self.kinds, self.here, self.near, self.core = net, kinds, here, near, core
        self.came, self.summed, self.own = came, summed, own
        self.pending = [None, None, None]

    def refs(self, part, stage, fixed, at):
        index = index_of(ORDERS[part][stage:], fixed, at)
        if stage:
            return [ref.at[index] for ref in self.summed[part, stage - 1]]
        return [
            ref.at[(*index, *(span(pair) for pair in CUTS[kind][part]))]
            for kind, ref in zip(self.kinds, self.own)
        ]

    def early(self, e, send_sem, recv_sem):
        at = {**self.here, "x": (self.here["x"] + e + 1) % 4}
        return [
            pltpu.make_async_remote_copy(
                src_ref=src,
                dst_ref=dst.at[e],
                send_sem=send_sem.at[len(self.kinds) * e + k],
                recv_sem=recv_sem.at[len(self.kinds) * e + k],
                device_id=device_of(at, self.core),
                device_id_type=MESH,
            )
            for k, (src, dst) in enumerate(
                zip(self.refs(0, 0, ("x",), at), self.came[0, 0])
            )
        ]

    def send(self, part, stage):
        dim = ORDERS[part][stage]
        self.pending[part] = [
            self.net.push(src, dst.at[e], device_of(at, self.core))
            for e, at in enumerate(self.near[dim])
            for src, dst in zip(self.refs(part, stage, (dim,), at), self.came[part, stage])
        ]

    def wait(self, part):
        for copy in self.pending[part] or ():
            copy.wait_recv()

    def add_up(self, part, stage):
        kept, rest = ORDERS[part][stage:], ORDERS[part][stage + 1 :]

        def unit(number, nothing):
            at, left = dict(self.here), number
            for axis, axis_dim in reversed(AXES):
                if axis_dim in rest:
                    at[axis] = left % EXTENT[axis]
                    left = left // EXTENT[axis]
            inner = index_of(rest, rest, at)
            own_refs = self.refs(part, stage, kept, at)
            for own, came, out in zip(
                own_refs, self.came[part, stage], self.summed[part, stage]
            ):
                total = own[...].astype(jnp.float32)
                for e in range(3):
                    total = total + came[(e, *inner)].astype(jnp.float32)
                out[inner if inner else Ellipsis] = total.astype(jnp.bfloat16)
            return nothing

        count = 1
        for size in extents(rest):
            count *= size
        if count == 1:
            unit(0, 0)
        else:
            lax.fori_loop(0, count, unit, 0)


def piece_shapes(kinds, part):
    return [
        tuple(pair[1] - pair[0] for pair in CUTS[kind][part]) for kind in kinds
    ]


def came_shapes(kinds, part, stage):
    rest = extents(ORDERS[part][stage + 1 :])
    return [(3, *rest, *shape) for shape in piece_shapes(kinds, part)]


def summed_shapes(kinds, part, stage):
    rest = extents(ORDERS[part][stage + 1 :])
    return [(*rest, *shape) for shape in piece_shapes(kinds, part)]


def stage_keys(stages):
    return [(part, stage) for part in range(3) for stage in stages]


def take(refs, keys, kinds):
    found = {}
    for key in keys:
        found[key], refs = refs[: len(kinds)], refs[len(kinds) :]
    return found, refs


def low_scratch(shapes):
    return [pltpu.VMEM(dims, jnp.bfloat16) for dims in shapes]


def half_of(core, kind):
    return pl.ds(pl.multiple_of(core * HALVES[kind], 128), HALVES[kind])


LATE = ("two", "three")


def backward_body(
    grad,
    mixed,
    entering,
    decays,
    query,
    grad_out,
    kv_all,
    hidden_mask,
    log_total,
    norm,
    grads_two,
    acts_attn,
    acts_mixer,
    acts_hidden,
    grads_three,
    carried,
    cumulative,
    sizes,
    inner,
    rim,
    steps,
    masks,
    intra,
    table,
    cosine,
    sine,
    grad_z,
    grads_one,
    grad_conv,
    grad_heads,
    out_two,
    out_three,
    *rest,
):
    came, rest = take(rest, stage_keys(range(3)), LATE)
    summed, rest = take(rest, stage_keys(range(3)), LATE)
    states, parts, carries, came_back, terms, term_parts = rest[:6]
    both_norm, both_two, both_act, both_three, own_two, own_three = rest[6:12]
    key_sum, value_sum, wide_states, leaving, grad_query, grad_inner, grad_rim, rim_back = rest[12:20]
    extended, grad_ext, grad_mixed, grad_steps, send_sem, recv_sem = rest[20:]
    here, core = coordinates()
    near = neighbours(here, core)
    c = at_ctx(here["y"], here["zl"], core)
    peers = ctx_peers(c)
    meet(peers + all_near(near, core))
    net = Sender(send_sem.at[pl.ds(6, 100)], recv_sem.at[pl.ds(6, 100)])
    sibling = device_of(here, 1 - core)
    toks = norm.shape[0]
    mine, theirs = pl.ds(0, toks), pl.ds(toks, toks)
    other = 1 - core
    output_map = mixed[:, WIDTH + STATE :].astype(jnp.bfloat16)
    wide_states[...] = down(
        output_map, (expand(entering[...]) * grad[...]).astype(jnp.bfloat16)
    )
    pack(wide_states, states)
    copies = [
        net.push(states.at[(c + e + 1) % CTX], parts.at[c], peer) for e, peer in enumerate(peers)
    ]
    first = [
        net.push(norm, both_norm.at[theirs], sibling),
        net.push(grads_two.at[:, half_of(other, "two")], both_two.at[theirs], sibling),
        net.push(acts_attn, both_act.at[theirs, pl.ds(0, 512)], sibling),
        net.push(acts_mixer, both_act.at[theirs, pl.ds(512, 1536)], sibling),
        net.push(acts_hidden, both_act.at[theirs, pl.ds(2048, 2048)], sibling),
        net.push(grads_three.at[:, :, half_of(other, "three")], both_three.at[:, theirs], sibling),
    ]
    both_norm[mine] = norm[...]
    both_two[mine] = grads_two[:, half_of(core, "two")]
    both_act[mine, 0:512] = acts_attn[...]
    both_act[mine, 512:2048] = acts_mixer[...]
    both_act[mine, 2048:4096] = acts_hidden[...]
    both_three[:, mine] = grads_three[:, :, half_of(core, "three")]
    parts[c] = states[c]
    for copy in copies:
        copy.wait_recv()
    scan_rows(range(CTX - 1, -1, -1), decays, parts, carries)
    back = send_back(net, c, peers, carries, came_back)
    for copy in first:
        copy.wait_recv()

    def block(owner_x):
        features = both_norm[:, pl.ds(pl.multiple_of(owner_x * 256, 256), 256)]
        wide = HALVES["two"] // 2
        for piece in range(2):
            at = pl.ds(piece * wide, wide)
            found = dot_rows(features, both_two[:, at])
            for unit in range(16):
                own_two[owner_x, unit // 8, unit // 2 % 4, unit % 2, :, at] = found[
                    unit * 16 : unit * 16 + 16
                ]
        found = []
        for source, (start, size) in enumerate(((0, 128), (512, 384), (2048, 512))):
            at = pl.ds(pl.multiple_of(start + owner_x * size, 128), size)
            found.append(dot_rows(both_act[:, at], both_three[source]))
        for owner_z in range(2):
            for unit in range(8):
                source = 0 if unit < 1 else 1 if unit < 4 else 2
                at = (unit - (0, 1, 4)[source]) * 64 + owner_z * (64, 192, 256)[source]
                own_three[owner_x, owner_z, unit // 2, unit % 2] = found[source][at : at + 64]

    sums = Sums(net, LATE, here, near, core, came, summed, (own_two, own_three))

    def turn(e, nothing):
        block((here["x"] + e + 1) % 4)
        for copy in sums.early(e, send_sem, recv_sem):
            copy.start()
        return nothing

    lax.fori_loop(0, 3, turn, 0)
    block(here["x"])
    sums.send(1, 0)
    sums.send(2, 0)
    key_sum[...] = jnp.zeros_like(key_sum)
    value_sum[...] = jnp.zeros_like(value_sum)

    def head(h, nothing):
        keys = kv_all[:, :, 0:128].reshape(CTX * toks, 128)
        values = kv_all[:, :, 128:256].reshape(CTX * toks, 128)
        scores = across(query[h], keys) + hidden_mask[...]
        probs = jnp.exp(scores - log_total[h][:, 0:1])
        grad_probs = across(grad_out[h], values)
        inner_sum = jnp.sum(probs * grad_probs, axis=-1, keepdims=True)
        grad_scores = (probs * (grad_probs - inner_sum)).astype(jnp.bfloat16)
        grad_query[h] = jnp.dot(grad_scores, keys, preferred_element_type=jnp.float32)
        key_sum[...] += down(query[h], grad_scores)
        value_sum[...] += down(grad_out[h], probs.astype(jnp.bfloat16))
        return nothing

    lax.fori_loop(0, HEADS, head, 0)
    for k in range(CTX):
        at = pl.ds(k * toks, toks)
        terms[k, 0:128] = key_sum[:, at].astype(jnp.bfloat16)
        terms[k, 128:256] = value_sum[:, at].astype(jnp.bfloat16)
    key_copies = [
        net.push(terms.at[(c + e + 1) % CTX], term_parts.at[e], peer)
        for e, peer in enumerate(peers)
    ]
    for copy in back:
        copy.wait_recv()
    unpack(came_back, leaving)
    mixer_grads_body(
        grad,
        leaving,
        carried,
        mixed,
        cumulative,
        sizes,
        entering,
        inner,
        rim,
        steps,
        masks,
        intra,
        table,
        grad_inner,
        grad_rim,
        grad_steps,
        grad_conv,
        grad_heads,
        extended,
        grad_ext,
        grad_mixed,
    )
    rim_copy = net.push(grad_rim, rim_back, peers[-1])
    for e in range(3):
        for copy in sums.early(e, send_sem, recv_sem):
            copy.wait_recv()
    for part in range(3):
        sums.wait(part)
        sums.add_up(part, 0)
        sums.send(part, 1)

    def turn_back(both):
        return both * cosine[...] - swap_quarters(both) * sine[...]

    low = jnp.bfloat16
    for j in range(HEADS // 2):
        grads_one[:, 128 * j : 128 * j + 128] = (
            turn_back(join_pair(grad_query, j)) * HEAD_DIM ** (-0.5)
        ).astype(low)
    for copy in key_copies:
        copy.wait_recv()
    collected = terms[c].astype(jnp.float32)
    for e in range(CTX - 1):
        collected = collected + term_parts[e].astype(jnp.float32)
    key_at = HEADS * HEAD_DIM
    grads_one[:, key_at : key_at + 128] = (turn_back(collected[0:128].T) * key_scale).astype(low)
    grads_one[:, key_at + 128 : Z_AT] = collected[128:256].T.astype(low)
    grads_one[:, Z_AT:INNER_AT] = grad_z[...]
    rim_copy.wait_recv()
    grad_inner[toks - 8 :] = grad_inner[toks - 8 :] + rim_back[...]
    grads_one[:, INNER_AT:STEP_AT] = grad_inner[...].astype(low)
    grads_one[:, STEP_AT : STEP_AT + 128] = grad_steps[...].astype(low)
    grads_one[:, PAD_AT:COLS] = jnp.zeros((toks, COLS - PAD_AT), low)
    for part in range(3):
        sums.wait(part)
        sums.add_up(part, 1)
        sums.send(part, 2)
    for part in range(3):
        sums.wait(part)
        sums.add_up(part, 2)
        for kind, out, ref in zip(LATE, (out_two, out_three), summed[part, 2]):
            out[tuple(span(pair) for pair in CUTS[kind][part])] = ref[...]
    for e in range(3):
        for copy in sums.early(e, send_sem, recv_sem):
            copy.wait_send()
    net.drain()


def backward(*ins):
    low, f32 = jnp.bfloat16, jnp.float32
    rows = ins[0].shape[0]
    scratch = [shape for key in stage_keys(range(3)) for shape in came_shapes(LATE, *key)]
    scratch += [shape for key in stage_keys(range(3)) for shape in summed_shapes(LATE, *key)]
    scratch += [
        *[(CTX, 16, HALF_WIDTH)] * 4,
        (CTX, 256, rows),
        (CTX - 1, 256, rows),
        (2 * rows, 1024),
        (2 * rows, HALVES["two"]),
        (2 * rows, 4096),
        (3, 2 * rows, HALVES["three"]),
        (4, 2, 4, 2, 16, HALVES["two"]),
        (4, 2, 4, 2, 64, HALVES["three"]),
    ]
    wide = [
        (128, CTX * rows),
        (128, CTX * rows),
        (STATE, WIDTH),
        (STATE, WIDTH),
        (HEADS, rows, 128),
        (rows, CONV_WIDTH),
        (8, CONV_WIDTH),
        (8, CONV_WIDTH),
        (rows + 8, CONV_WIDTH),
        (rows + 8, CONV_WIDTH),
        (rows, CONV_WIDTH),
        (rows, 128),
    ]
    return call_kernel(
        backward_body,
        "backward",
        3,
        (
            shape_of((rows, COLS), low),
            shape_of((8, CONV_WIDTH), f32),
            shape_of((8, 128), f32),
            shape_of((16, HALVES["two"]), low),
            shape_of((64, HALVES["three"]), low),
        ),
        ins,
        106,
        [*low_scratch(scratch), *[pltpu.VMEM(dims, f32) for dims in wide]],
    )


FIRST = ("one",)


def weight_grads_body(
    norm, grads_one, small, unit_two, unit_three, out_one, out_two, out_three, *rest
):
    came, rest = take(rest, stage_keys(range(3)), FIRST)
    summed, rest = take(rest, stage_keys(range(3)), FIRST)
    both_norm, both_one, own_one, small_in, send_sem, recv_sem = rest
    here, core = coordinates()
    near = neighbours(here, core)
    toks = norm.shape[0]
    sibling = device_of(here, 1 - core)
    meet(all_near(near, core) + [sibling])
    net = Sender(send_sem.at[pl.ds(3, 42)], recv_sem.at[pl.ds(3, 42)])
    mine, theirs = pl.ds(0, toks), pl.ds(toks, toks)
    first = [
        net.push(norm, both_norm.at[theirs], sibling),
        net.push(grads_one.at[:, half_of(1 - core, "one")], both_one.at[theirs], sibling),
        net.push(small, small_in, sibling),
    ]
    both_norm[mine] = norm[...]
    both_one[mine] = grads_one[:, half_of(core, "one")]
    over_z = device_of({**here, "zl": 1 - here["zl"]}, core)
    y, low_z = here["y"], here["zl"]
    late = {"two": out_two, "three": out_three}
    out_two[y, low_z, :, half_of(core, "two")] = unit_two[...]
    out_three[y, low_z, :, half_of(core, "three")] = unit_three[...]

    def pass_on(kind, ref, at_y, at_z, targets):
        piece = ref.at[at_y, at_z, :, half_of(core, kind)]
        return [net.push(piece, piece, target) for target in targets]

    def late_step(at_y, at_z, targets):
        return [
            copy
            for kind, ref in late.items()
            for copy in pass_on(kind, ref, at_y, at_z, targets)
        ]

    to_y = [device_of(at, core) for at in near["y"]]
    late_copies = late_step(y, low_z, [over_z])
    for copy in first:
        copy.wait_recv()

    def block(owner_x, owner_z):
        owner = owner_x * 2 + owner_z
        features = both_norm[:, pl.ds(pl.multiple_of(owner * 128, 128), 128)]
        for low_at, high_at in ((0, 1024), (1024, 2176)):
            found = dot_rows(features, both_one[:, low_at:high_at])
            for unit in range(8):
                rows = found[unit * 16 : unit * 16 + 16]
                if unit == 0 and low_at:
                    extra = (small[owner] + small_in[owner]) * core.astype(jnp.float32)
                    tail = rows[:, 1024:].astype(jnp.float32) + extra
                    rows = jnp.concatenate([rows[:, :1024], tail.astype(jnp.bfloat16)], axis=1)
                own_one[owner_x, owner_z, unit // 2, unit % 2, :, low_at:high_at] = rows

    sums = Sums(net, FIRST, here, near, core, came, summed, (own_one,))

    def turn(e, nothing):
        owner_x = (here["x"] + e + 1) % 4
        block(owner_x, 0)
        block(owner_x, 1)
        for copy in sums.early(e, send_sem, recv_sem):
            copy.start()
        return nothing

    lax.fori_loop(0, 3, turn, 0)

    def own_turn(owner_z, nothing):
        block(here["x"], owner_z)
        return nothing

    lax.fori_loop(0, 2, own_turn, 0)
    sums.send(1, 0)
    sums.send(2, 0)
    for copy in late_copies:
        copy.wait_recv()
    late_copies = late_step(y, slice(None), to_y)
    for e in range(3):
        for copy in sums.early(e, send_sem, recv_sem):
            copy.wait_recv()
    for stage in range(3):
        for part in range(3):
            sums.wait(part)
            sums.add_up(part, stage)
            if stage < 2:
                sums.send(part, stage + 1)
        if stage == 1:
            for copy in late_copies:
                copy.wait_recv()
            late_copies = late_step(slice(None), slice(None), [sibling])
    for part in range(3):
        rows, cols = cut_of("one", part, core)
        out_one[y, low_z, rows, cols] = summed[part, 2][0][...]
    for step in (
        (y, low_z, [over_z]),
        (y, slice(None), to_y),
        (slice(None), slice(None), [sibling]),
    ):
        for copy in pass_on("one", out_one, *step):
            copy.wait_recv()
    for copy in late_copies:
        copy.wait_recv()
    for e in range(3):
        for copy in sums.early(e, send_sem, recv_sem):
            copy.wait_send()
    net.drain()


def sum_weight_grads(norm, grads_one, small, unit_two, unit_three):
    toks = norm.shape[0]
    low = jnp.bfloat16
    scratch = [shape for key in stage_keys(range(3)) for shape in came_shapes(FIRST, *key)]
    scratch += [shape for key in stage_keys(range(3)) for shape in summed_shapes(FIRST, *key)]
    scratch += [
        (2 * toks, 1024),
        (2 * toks, HALVES["one"]),
        (4, 2, 4, 2, 16, HALVES["one"]),
    ]
    return call_kernel(
        weight_grads_body,
        "sum_weight_grads",
        5,
        tuple(
            shape_of((4, 2, UNIT_ROWS[kind], 2 * HALVES[kind]), low)
            for kind in ("one", "two", "three")
        ),
        (norm, grads_one, small, unit_two, unit_three),
        45,
        [*low_scratch(scratch), pltpu.VMEM(small.shape, jnp.float32)],
    )


def first_norm_grads_body(grads_one, weights, row_in, grad_middle, table, input_grad, gain_grad):
    dim = row_in.shape[1]
    grad_norm = across(grads_one[...], weights[...])
    values = row_in[...]
    scale = lax.rsqrt(mean_last(values * values) + epsilon)
    weighted = grad_norm * table[7:8, 0:dim]
    input_grad[...] = (
        grad_middle[...]
        + scale * weighted
        - values * (scale * scale * scale) * mean_last(values * weighted)
    )
    gain_grad[...] = jnp.broadcast_to(
        jnp.sum(grad_norm * values * scale, axis=0, keepdims=True), gain_grad.shape
    )


def first_norm_grads(grads_one, weights, row_in, grad_middle, table):
    return plain_kernel(
        first_norm_grads_body,
        "first_norm_grads",
        (shape_of(row_in.shape, jnp.float32), shape_of((8, row_in.shape[1]), jnp.float32)),
        (grads_one, weights, row_in, grad_middle, table),
    )


def local(
    layer_input,
    segment_ids,
    norm_gain,
    w_query,
    w_key,
    w_value,
    w_attn_out,
    w_gate_z,
    w_inner,
    w_step,
    conv_weight,
    conv_bias,
    step_bias,
    decay_log,
    skip_gain,
    mixer_gain,
    w_mixer_out,
    ffn_gain,
    w_gate,
    w_up,
    w_down,
    out_grad,
):
    low = jnp.bfloat16
    tok_rows = layer_input.shape[1]
    ctx_here = lax.axis_index("ctx")
    first_pos = ctx_here * tok_rows
    seg_here = segment_ids[0]
    pos_here = first_pos + jnp.arange(tok_rows, dtype=jnp.int32)
    residual_in = layer_input[0].astype(jnp.float32)
    grad_final = out_grad[0].astype(jnp.float32)
    kv_width = KV_HEADS * HEAD_DIM
    q_width = HEADS * HEAD_DIM
    width_inner = SSM_HEADS * SSM_DIM
    conv_width = width_inner + 2 * STATE
    z_at = q_width + 2 * kv_width
    inner_at = z_at + width_inner
    step_at = inner_at + conv_width

    small_rows = (
        *conv_weight,
        conv_bias,
        mixer_gain,
        ffn_gain,
        norm_gain,
        step_bias,
        decay_log,
        skip_gain,
    )
    small = jnp.concatenate(
        [piece for row in small_rows for piece in (row, jnp.zeros((256 - row.shape[0],), low))]
        + [jnp.zeros((5 * 256,), low)]
    ).reshape(16, 256)
    in_one = jnp.concatenate(
        [w_query, w_key, w_value, w_gate_z, w_inner, jnp.pad(w_step, ((0, 0), (0, 232)))], axis=1
    )
    half_dim = HEAD_DIM // 2
    inverse = rope_base ** (-jnp.arange(half_dim, dtype=jnp.float32) / half_dim)
    angles = pos_here.astype(jnp.float32)[:, None] * inverse[None, :]
    cosine = jnp.tile(jnp.cos(angles), (1, 4))
    sine = jnp.sin(angles)
    sine = jnp.concatenate([-sine, sine, -sine, sine], axis=1)
    seg_early = jnp.concatenate([jnp.full((CONV - 1,), -2, jnp.int32), seg_here])
    seg_cols = jnp.stack([seg_early[k : k + tok_rows] for k in range(CONV)], axis=1)
    (
        normed_low,
        query,
        gate_z,
        inner_pre,
        steps,
        table,
        hidden_mask,
        masks,
        intra,
        kv_all,
        rim_got,
        mixed,
        cumulative,
        sizes,
        entering,
        carried,
        mixer_result,
        decays,
        attended,
        log_total,
        all_one,
        all_two,
        all_three,
    ) = forward(
        residual_in,
        cosine,
        sine,
        small,
        jnp.broadcast_to(segment_ids, (8, tok_rows)),
        jnp.pad(seg_cols, ((0, 0), (0, 128 - CONV))),
        in_one,
        jnp.concatenate([w_gate, w_up], axis=1),
        jnp.concatenate([w_attn_out, w_mixer_out, w_down], axis=0),
    )
    kv_all = kv_all.reshape(CTX, tok_rows, 256)
    full_one = all_one.reshape(FSDP * 128, COLS)
    (
        layer_out,
        grad_middle,
        attn_low,
        mixer_low,
        hidden_low,
        normed_two_low,
        grads_two,
        grads_three,
        grad_out_wide,
        grad_result,
        grad_z,
        grad_gain_two,
        grad_mixer_gain,
    ) = middle_part(
        residual_in,
        grad_final,
        attended,
        mixer_result,
        gate_z,
        table,
        all_two.reshape(FSDP * 128, 2 * HALVES["two"]),
        all_three.reshape(FSDP, OUT_ROWS, 2 * HALVES["three"]),
    )
    grad_gain_two, grad_mixer_gain = grad_gain_two[0], grad_mixer_gain[0]
    grads_one, grad_conv_all, grad_heads, unit_two, unit_three = backward(
        grad_result,
        mixed,
        entering,
        decays,
        query,
        grad_out_wide,
        kv_all,
        hidden_mask,
        log_total,
        normed_two_low,
        grads_two,
        attn_low,
        mixer_low,
        hidden_low,
        grads_three,
        carried,
        cumulative,
        sizes,
        inner_pre,
        rim_got,
        steps,
        masks,
        intra,
        table,
        cosine,
        sine,
        grad_z,
    )
    grad_conv, grad_conv_bias = grad_conv_all[:CONV], grad_conv_all[CONV]
    grad_step_bias = grad_heads[0, :SSM_HEADS]
    grad_decay = grad_heads[1, :SSM_HEADS]
    grad_skip = grad_heads[2, :SSM_HEADS]
    input_grad, grad_gain_one = first_norm_grads(
        grads_one, full_one, residual_in, grad_middle, table
    )
    grad_gain_one = grad_gain_one[0]

    small_grads = jnp.concatenate(
        [
            grad_gain_one.reshape(FSDP, 128),
            grad_conv.reshape(CONV, FSDP, 224).transpose(1, 0, 2).reshape(FSDP, CONV * 224),
            grad_conv_bias.reshape(FSDP, 224),
            grad_step_bias.reshape(FSDP, 3),
            grad_decay.reshape(FSDP, 3),
            grad_skip.reshape(FSDP, 3),
            grad_mixer_gain.reshape(FSDP, 192),
            grad_gain_two.reshape(FSDP, 128),
            jnp.zeros((FSDP, 2048 - SMALL), jnp.float32),
        ],
        axis=1,
    ).reshape(FSDP, 16, 128)
    sum_one, sum_two, sum_three = sum_weight_grads(
        normed_low, grads_one, small_grads, unit_two, unit_three
    )
    one = sum_one.reshape(128, COLS).astype(jnp.float32)
    two = sum_two.reshape(128, 2 * HALVES["two"]).astype(jnp.float32)
    three = sum_three.reshape(OUT_ROWS, 2 * HALVES["three"]).astype(jnp.float32)
    tiny = one[0:16, PAD_AT:COLS].reshape(-1)
    return (
        layer_out[None],
        input_grad[None],
        tiny[0:128],
        one[:, :q_width],
        one[:, q_width : q_width + kv_width],
        one[:, q_width + kv_width : z_at],
        three[0:64],
        one[:, z_at:inner_at],
        one[:, inner_at:step_at],
        one[:, step_at : step_at + SSM_HEADS],
        tiny[128:1024].reshape(CONV, 224),
        tiny[1024:1248],
        tiny[1248:1251],
        tiny[1251:1254],
        tiny[1254:1257],
        tiny[1257:1449],
        three[64:256],
        tiny[1449:1577],
        two[:, : HALVES["two"]],
        two[:, HALVES["two"] :],
        three[256:512],
    )


def solution(mesh):
    in_specs = (
        P("fsdp", "ctx", None),
        P("fsdp", "ctx"),
        P("fsdp"),
        P("fsdp", None),
        P("fsdp", None),
        P("fsdp", None),
        P("fsdp", None),
        P("fsdp", None),
        P("fsdp", None),
        P("fsdp", None),
        P(None, "fsdp"),
        P("fsdp"),
        P("fsdp"),
        P("fsdp"),
        P("fsdp"),
        P("fsdp"),
        P("fsdp", None),
        P("fsdp"),
        P("fsdp", None),
        P("fsdp", None),
        P("fsdp", None),
        P("fsdp", "ctx", None),
    )
    out_specs = (
        P("fsdp", "ctx", None),
        P("fsdp", "ctx", None),
        P("fsdp"),
        P("fsdp", None),
        P("fsdp", None),
        P("fsdp", None),
        P("fsdp", None),
        P("fsdp", None),
        P("fsdp", None),
        P("fsdp", None),
        P(None, "fsdp"),
        P("fsdp"),
        P("fsdp"),
        P("fsdp"),
        P("fsdp"),
        P("fsdp"),
        P("fsdp", None),
        P("fsdp"),
        P("fsdp", None),
        P("fsdp", None),
        P("fsdp", None),
    )
    return jax.shard_map(local, mesh=mesh, in_specs=in_specs, out_specs=out_specs, check_vma=False)
```
